32 devices in a mesh: occ: 2 (over core), row: 4 (over y, x), col: 4 (over z).
Axes of the slice: x: 2, y: 2, z: 4, core: 2. Of those that a mesh axis runs over, the one named last changes fastest.
Arguments:
- bra_factor: bfloat16 [3072, 2, 4096], P(('occ', 'col'), None, 'row'), may hold values from -0.5 to 0.5
- ket_factor: bfloat16 [3072, 2, 4096], P(('occ', 'row'), None, 'col'), may hold values from -0.5 to 0.5
- occ_energy: float32 [2], replicated, may hold values from -2 to -0.5
- virt_energy: float32 [4096], replicated, may hold values from 0.2 to 3
Outputs:
- amplitudes: bfloat16 [2, 2, 4096, 4096], P(None, None, 'row', 'col')
- gamma: float32 [3072, 2, 4096], P(('occ', 'col'), None, 'row')
The draws below stay inside these ranges and needn't reach their ends.
All inputs are finite; a program needn't handle non-finite values.
Results may differ from the reference program's by a relative error of at most 0.002.
Values may be sent and summed in bfloat16 or wider, within the bound.
No kernel may reach another device: no remote copies, remote signals or barrier semaphores. Data moves between devices by JAX's collectives and lax.ppermute only.
A program may use at most 128 MiB of HBM per device.

```python
import jax
import jax.numpy as jnp

NAUX = 3072
NVIRT = 4096
OCC_WIN = 2


def strengthened(result, key, source, target, parts, factor):
    def block_of(dim):
        return (jnp.arange(result.shape[dim]) // (result.shape[dim] // parts)).reshape((-1,) + (1,) * (result.ndim - 1 - dim))

    one_side = jax.random.permutation(key, parts)[block_of(target)]
    far = (block_of(target) + parts // 2) % parts
    return jnp.where((block_of(source) == one_side) | (block_of(source) == far), factor * result, result)


def block_scale(rng, extent, pieces, least, high):
    level = 1.0
    for position, parts in pieces:
        steps = jax.random.uniform(jax.random.fold_in(jax.random.fold_in(rng, 6), position), (parts,), jnp.float32, least / len(pieces), high / len(pieces))
        level = level * jnp.repeat(jnp.exp(steps), extent[position] // parts).reshape((-1,) + (1,) * (len(extent) - 1 - position))
    return level


def gaussian(rng, extent, width, bound, split=(), held_as=jnp.bfloat16):
    factor_of = block_scale(rng, extent, split, -0.22, 0.18) if split else 1.0
    drawn = jax.random.normal(rng, extent, jnp.float32) * width * factor_of
    return jnp.minimum(jnp.maximum(drawn, -bound), bound).astype(held_as)


def bell_draw_with(stream_key, extent, spread, reach, shards, heavy, dtype=jnp.bfloat16):
    result = spread * jax.random.normal(stream_key, extent, jnp.float32)
    if shards:
        result = result * block_scale(stream_key, extent, shards, -0.22, 0.18)
    return jnp.clip(strengthened(result, jax.random.fold_in(stream_key, 3), *heavy), -reach, reach).astype(dtype)


def setup_inputs(seed: int = 0) -> dict:
    key_list = jax.random.split(jax.random.key(seed), 5)
    return {
        "bra_factor": gaussian(key_list[0], (NAUX, OCC_WIN, NVIRT), 0.08, 0.5, ((0, 8), (2, 4))),
        "ket_factor": bell_draw_with(key_list[1], (NAUX, OCC_WIN, NVIRT), 0.08, 0.5, ((0, 8), (2, 4)), (2, 0, 8, 2.0)),
        "occ_energy": jnp.clip(jax.random.uniform(key_list[2], (OCC_WIN,), jnp.float32, -2.0, -0.5), -2.0, -0.5),
        "virt_energy": jnp.clip(jax.random.uniform(key_list[3], (NVIRT,), jnp.float32, 0.2, 3.0), 0.2, 3.0),
    }


def reference(bra_factor, ket_factor, occ_energy, virt_energy):
    bra_wide = bra_factor.astype(jnp.float32)
    ket_wide = ket_factor.astype(jnp.float32)
    coulomb = jnp.einsum("qia,qjb->ijab", bra_wide, ket_wide)
    denominator = (occ_energy[:, None, None, None] + occ_energy[None, :, None, None]
                   - virt_energy[None, None, :, None] - virt_energy[None, None, None, :])
    amplitudes = ((2.0 * coulomb - jnp.transpose(coulomb, (1, 0, 2, 3))) / denominator).astype(jnp.bfloat16)
    gamma = jnp.einsum("ijab,qjb->qia", amplitudes.astype(jnp.float32), ket_wide)
    return amplitudes, gamma
```

```python
import functools

import jax
import jax.numpy as jnp
from jax import lax
from jax.experimental import pallas as pl
from jax.experimental.pallas import tpu as pltpu
from jax.sharding import PartitionSpec as P


def make_amplitudes(coulomb, occ_energy, virt_first, virt_second):
    denominator = (
        occ_energy[:, None, None, None]
        + occ_energy[None, :, None, None]
        - virt_first[None, None, :, None]
        - virt_second[None, None, None, :]
    )
    return ((2.0 * coulomb - jnp.transpose(coulomb, (1, 0, 2, 3))) / denominator).astype(
        jnp.bfloat16
    )


def general(bra_factor, ket_factor, occ_energy, virt_energy):
    a_width = bra_factor.shape[2]
    b_width = ket_factor.shape[2]
    ket_whole = lax.all_gather(ket_factor, "row", axis=0, tiled=True)
    row_index = lax.axis_index("row")
    col_index = lax.axis_index("col")
    virt_first = lax.dynamic_slice_in_dim(virt_energy, row_index * a_width, a_width, 0)
    virt_second = lax.dynamic_slice_in_dim(virt_energy, col_index * b_width, b_width, 0)
    partial_sum = jnp.einsum(
        "qia,qjb->ijab",
        lax.all_gather(bra_factor, "col", axis=0, tiled=True),
        ket_whole,
        preferred_element_type=jnp.float32,
    )
    batch_count = lax.axis_size("occ")
    pad_rows = (batch_count - a_width % batch_count) % batch_count
    padded = jnp.pad(partial_sum, ((0, 0), (0, 0), (0, pad_rows), (0, 0)))
    share_sum = lax.psum_scatter(padded, "occ", scatter_dimension=2, tiled=True)
    share_len = share_sum.shape[2]
    energy_padded = jnp.pad(virt_first, (0, pad_rows), constant_values=1.0)
    energy_share = lax.dynamic_slice_in_dim(
        energy_padded, lax.axis_index("occ") * share_len, share_len, 0
    )
    share_amps = make_amplitudes(share_sum, occ_energy, energy_share, virt_second)
    collected = lax.all_gather(share_amps, "occ", axis=2, tiled=True)
    amplitudes = collected[:, :, :a_width, :]
    gamma = lax.psum_scatter(
        jnp.einsum("ijab,qjb->qia", amplitudes, ket_whole, preferred_element_type=jnp.float32),
        "col",
        scatter_dimension=0,
        tiled=True,
    )
    return (amplitudes, gamma)


CHUNKS = 4


def chunk_kernel(pieces, cols, groups, *refs):
    count = 2 * len(pieces)
    ket = refs[:count]
    bra, occ_ref, first_ref, second_ref = refs[count : count + 4]
    amps_ref, gamma_ref = refs[count + 4 : count + 6]
    kv, bv, bt, t2, ket_sem, bra_sem = refs[count + 6 :]
    width = first_ref.shape[0]
    span = second_ref.shape[1]
    part = span // groups
    batch = bra.shape[2]
    here_row, here_col = lax.axis_index("row"), lax.axis_index("col")

    bra_copy = pltpu.make_async_copy(bra, bv, bra_sem)
    bra_copy.start()
    copies = []
    for group in range(groups):
        of_group = []
        for q in range(2):
            for index, (offset, begin, rows) in enumerate(pieces):
                home = lax.bitwise_xor(here_row, offset)
                to_row = pl.multiple_of(home * (2 * batch) + q * batch + begin, 16)
                for j in range(2):
                    columns = pl.ds(j * span + group * part, part)
                    copy = pltpu.make_async_copy(
                        ket[q * len(pieces) + index].at[:, columns],
                        kv.at[pl.ds(to_row, rows), columns],
                        ket_sem.at[group, q, index, j],
                    )
                    copy.start()
                    of_group.append(copy)
        copies.append(of_group)
    bra_copy.wait()
    for d in range(cols):
        for q in range(2):
            at = (2 * d + q) * batch
            bt[:, at : at + batch] = bv[d, q].T
    for group in range(groups):
        for copy in copies[group]:
            copy.wait()
        tile = [
            jnp.dot(
                bt[...],
                kv[:, j * span + group * part : j * span + (group + 1) * part],
                preferred_element_type=jnp.float32,
            )
            for j in range(2)
        ]
        second = second_ref[:, group * part : (group + 1) * part]
        for i in range(2):
            for j in range(2):
                direct = tile[j][i * width : (i + 1) * width, :]
                exchange = tile[i][j * width : (j + 1) * width, :]
                denominator = ((occ_ref[i] + occ_ref[j]) - first_ref[...]) - second
                amps = ((2.0 * direct - exchange) / denominator).astype(jnp.bfloat16)
                amps_ref[i, j, :, group * part : (group + 1) * part] = amps
                t2[
                    i * width : (i + 1) * width,
                    j * span + group * part : j * span + (group + 1) * part,
                ] = amps
    for t in range(cols):
        home = lax.rem(here_col + t, cols)
        rows = pl.ds(pl.multiple_of(home * (2 * batch), 16), 2 * batch)
        gamma_ref[t] = lax.dot_general(
            kv[rows, :],
            t2[...],
            (((1,), (1,)), ((), ())),
            preferred_element_type=jnp.float32,
        )


def run_chunk(ket, pieces, bra, occ_energy, first, second):
    cols, _, batch, double = bra.shape
    width = double // 2
    span = second.shape[1]
    groups = 4
    total = cols * 2 * batch
    flops = 2 * 2 * total * double * 2 * span
    return pl.pallas_call(
        functools.partial(chunk_kernel, pieces, cols, groups),
        out_shape=(
            jax.ShapeDtypeStruct((2, 2, width, span), jnp.bfloat16),
            jax.ShapeDtypeStruct((cols, 2 * batch, double), jnp.float32),
        ),
        in_specs=[pl.BlockSpec(memory_space=pl.ANY)] * (len(ket) + 1)
        + [
            pl.BlockSpec(memory_space=pltpu.SMEM),
            pl.BlockSpec(memory_space=pltpu.VMEM),
            pl.BlockSpec(memory_space=pltpu.VMEM),
        ],
        out_specs=(
            pl.BlockSpec(memory_space=pltpu.VMEM),
            pl.BlockSpec(memory_space=pltpu.VMEM),
        ),
        scratch_shapes=[
            pltpu.VMEM((total, 2 * span), jnp.bfloat16),
            pltpu.VMEM(bra.shape, jnp.bfloat16),
            pltpu.VMEM((double, total), jnp.bfloat16),
            pltpu.VMEM((double, 2 * span), jnp.bfloat16),
            pltpu.SemaphoreType.DMA((groups, 2, len(pieces), 2)),
            pltpu.SemaphoreType.DMA,
        ],
        compiler_params=pltpu.CompilerParams(vmem_limit_bytes=48 * 2**20),
        cost_estimate=pl.CostEstimate(
            flops=flops, bytes_accessed=total * 2 * span * 2, transcendentals=0
        ),
    )(*ket, bra, occ_energy, first, second)


def place_kernel(width, half, count, *refs):
    own, other, out, sem = refs[:count], refs[count : 2 * count], refs[2 * count], refs[-1]
    me = lax.axis_index("occ")
    copies = []
    for k in range(count):
        for side, source in ((me, own[k]), (1 - me, other[k])):
            at = pl.multiple_of(side * half + k * width, 16)
            copy = pltpu.make_async_copy(
                source, out.at[:, :, pl.ds(at, width), :], sem.at[len(copies)]
            )
            copy.start()
            copies.append(copy)
    for copy in copies:
        copy.wait()


def place(own, other):
    count = len(own)
    _, _, width, span = own[0].shape
    return pl.pallas_call(
        functools.partial(place_kernel, width, width * count, count),
        out_shape=jax.ShapeDtypeStruct((2, 2, 2 * count * width, span), own[0].dtype),
        in_specs=[pl.BlockSpec(memory_space=pl.ANY)] * (2 * count),
        out_specs=pl.BlockSpec(memory_space=pl.ANY),
        scratch_shapes=[pltpu.SemaphoreType.DMA((2 * count,))],
        cost_estimate=pl.CostEstimate(
            flops=0, bytes_accessed=16 * 2 * count * width * span, transcendentals=0
        ),
    )(*own, *other)


def swap(x):
    return lax.ppermute(x, "occ", [(0, 1), (1, 0)])


def planar(x, offset):
    return lax.ppermute(x, "row", [(r, r ^ offset) for r in range(4)])


def sum_along(share, cols):
    up = down = None
    for step in range(cols - 1):
        send_up = share[cols - 1 - step]
        send_down = share[step + 1]
        if step:
            send_up, send_down = send_up + up, send_down + down
        up = lax.ppermute(
            send_up.astype(jnp.bfloat16), "col", [(c, c + 1) for c in range(step + 1)]
        ).astype(jnp.float32)
        down = lax.ppermute(
            send_down.astype(jnp.bfloat16),
            "col",
            [(cols - 1 - c, cols - 2 - c) for c in range(step + 1)],
        ).astype(jnp.float32)
    return share[0] + up + down


def planned(bra_factor, ket_factor, occ_energy, virt_energy):
    batch, _, a_width = bra_factor.shape
    b_width = ket_factor.shape[2]
    half = a_width // 2
    width = half // CHUNKS
    cols = lax.axis_size("col")
    me, row_index, col_index = (lax.axis_index(name) for name in ("occ", "row", "col"))

    def rows_of(side):
        part = lax.dynamic_slice_in_dim(bra_factor, side * half, half, 2)
        part = part.reshape(batch, 2, CHUNKS, width).transpose(2, 0, 1, 3)
        return part.reshape(CHUNKS, batch, 2 * width)

    ket_own = ket_factor.reshape(batch, 2 * b_width)
    ket_x = planar(ket_own, 1)
    ket_y = planar(ket_own, 2)
    cut = batch // 2
    ket_far_y = planar(ket_x[:cut], 2)
    ket_far_x = planar(ket_y[cut:], 1)
    mine = [ket_own, ket_x, ket_y, ket_far_y, ket_far_x]
    pieces = ((0, 0, batch), (1, 0, batch), (2, 0, batch), (3, 0, cut), (3, cut, batch - cut))
    ket = mine + [swap(piece) for piece in mine]

    bra_own = rows_of(me)
    bra_other = swap(rows_of(1 - me))
    second = lax.dynamic_slice_in_dim(virt_energy, col_index * b_width, b_width, 0)[None, :]
    first_start = row_index * a_width + me * half

    amps, sums = [], []
    for k in range(CHUNKS):
        bra = lax.all_gather(jnp.stack([bra_own[k], bra_other[k]]), "col", axis=0)
        first = lax.dynamic_slice_in_dim(virt_energy, first_start + k * width, width, 0)
        part, share = run_chunk(ket, pieces, bra, occ_energy, first[:, None], second)
        amps.append(part)
        sums.append(sum_along(share, cols))
    amplitudes = place(amps, [swap(part) for part in amps])

    def gathered(parts):
        whole = jnp.stack(parts).reshape(CHUNKS, batch, 2, width)
        return whole.transpose(1, 2, 0, 3).reshape(batch, 2, half)

    kept = gathered([total[:batch] for total in sums])
    received = gathered([swap(total[batch:]) for total in sums])
    gamma = jnp.where(
        me == 0,
        jnp.concatenate([kept, received], axis=2),
        jnp.concatenate([received, kept], axis=2),
    )
    return (amplitudes, gamma)


def solution(mesh):
    sizes = mesh.shape

    def on_device(bra_factor, ket_factor, occ_energy, virt_energy):
        fits = (
            sizes["occ"] == 2
            and sizes["row"] == 4
            and sizes["col"] > 1
            and bra_factor.shape[2] % (256 * CHUNKS) == 0
            and ket_factor.shape[2] % 512 == 0
            and bra_factor.shape[0] % 128 == 0
        )
        body = planned if fits else general
        return body(bra_factor, ket_factor, occ_energy, virt_energy)

    placed = (P(("occ", "col"), None, "row"), P(("occ", "row"), None, "col"), P(), P())
    return jax.shard_map(
        on_device,
        mesh=mesh,
        in_specs=placed,
        out_specs=(P(None, None, "row", "col"), P(("occ", "col"), None, "row")),
        check_vma=False,
    )
```

```python
import functools

import jax
import jax.numpy as jnp
from jax import lax
from jax.experimental import pallas as pl
from jax.experimental.pallas import tpu as pltpu
from jax.sharding import PartitionSpec as P


def make_amplitudes(coulomb, occ_energy, virt_first, virt_second):
    denominator = (
        occ_energy[:, None, None, None]
        + occ_energy[None, :, None, None]
        - virt_first[None, None, :, None]
        - virt_second[None, None, None, :]
    )
    return ((2.0 * coulomb - jnp.transpose(coulomb, (1, 0, 2, 3))) / denominator).astype(
        jnp.bfloat16
    )


def general(bra_factor, ket_factor, occ_energy, virt_energy):
    a_width = bra_factor.shape[2]
    b_width = ket_factor.shape[2]
    ket_whole = lax.all_gather(ket_factor, "row", axis=0, tiled=True)
    row_index = lax.axis_index("row")
    col_index = lax.axis_index("col")
    virt_first = lax.dynamic_slice_in_dim(virt_energy, row_index * a_width, a_width, 0)
    virt_second = lax.dynamic_slice_in_dim(virt_energy, col_index * b_width, b_width, 0)
    partial_sum = jnp.einsum(
        "qia,qjb->ijab",
        lax.all_gather(bra_factor, "col", axis=0, tiled=True),
        ket_whole,
        preferred_element_type=jnp.float32,
    )
    batch_count = lax.axis_size("occ")
    pad_rows = (batch_count - a_width % batch_count) % batch_count
    padded = jnp.pad(partial_sum, ((0, 0), (0, 0), (0, pad_rows), (0, 0)))
    share_sum = lax.psum_scatter(padded, "occ", scatter_dimension=2, tiled=True)
    share_len = share_sum.shape[2]
    energy_padded = jnp.pad(virt_first, (0, pad_rows), constant_values=1.0)
    energy_share = lax.dynamic_slice_in_dim(
        energy_padded, lax.axis_index("occ") * share_len, share_len, 0
    )
    share_amps = make_amplitudes(share_sum, occ_energy, energy_share, virt_second)
    collected = lax.all_gather(share_amps, "occ", axis=2, tiled=True)
    amplitudes = collected[:, :, :a_width, :]
    gamma = lax.psum_scatter(
        jnp.einsum("ijab,qjb->qia", amplitudes, ket_whole, preferred_element_type=jnp.float32),
        "col",
        scatter_dimension=0,
        tiled=True,
    )
    return (amplitudes, gamma)


CHUNKS = 4
GROUPS = 4


def chunk_kernel(pieces, cols, steps, chunk, *refs):
    refs = list(refs)
    take = lambda count: [refs.pop(0) for _ in range(count)]
    ket = take(2 * len(pieces))
    (bra,) = take(1)
    ups, downs = take(cols - 1), take(cols - 1)
    occ_ref, first_ref, second_ref = take(3)
    if chunk:
        take(2)
    whole_ref, half_ref, share_ref, up_ref, down_ref = take(5)
    kv, bv, bt, t2, amps, ket_sem, bra_sem, out_sem = refs
    width = first_ref.shape[0]
    span = second_ref.shape[1]
    part = span // GROUPS
    batch = bra.shape[3]
    here_row, here_col = lax.axis_index("row"), lax.axis_index("col")
    me = lax.axis_index("occ")

    def bra_copies(source, place, home, slot):
        return [
            pltpu.make_async_copy(
                source.at[place, q, i],
                bv.at[home, pl.ds(q * batch, batch), pl.ds(i * width, width)],
                bra_sem.at[slot, q, i],
            )
            for q in range(2)
            for i in range(2)
        ]

    for copy in bra_copies(bra, chunk, here_col, 0):
        copy.start()
    for d in range(1, cols):
        home = lax.rem(here_col + cols - d, cols)

        @pl.when(here_col >= d)
        def _():
            for copy in bra_copies(ups[d - 1], steps[d - 1], home, d):
                copy.start()

        @pl.when(here_col < d)
        def _():
            for copy in bra_copies(downs[cols - 1 - d], steps[cols - 1 - d], home, d):
                copy.start()

    copies = []
    for group in range(GROUPS):
        of_group = []
        for q in range(2):
            for index, (offset, begin, rows) in enumerate(pieces):
                home = lax.bitwise_xor(here_row, offset)
                to_row = pl.multiple_of(home * (2 * batch) + q * batch + begin, 16)
                for j in range(2):
                    columns = pl.ds(j * span + group * part, part)
                    copy = pltpu.make_async_copy(
                        ket[q * len(pieces) + index].at[:, columns],
                        kv.at[pl.ds(to_row, rows), columns],
                        ket_sem.at[group, q, index, j],
                    )
                    copy.start()
                    of_group.append(copy)
        copies.append(of_group)
    for d in range(cols):
        home = lax.rem(here_col + cols - d, cols)
        for copy in bra_copies(bra, chunk, home, d):
            copy.wait()
    for d in range(cols):
        bt[:, d * 2 * batch : (d + 1) * 2 * batch] = bv[d].T
    for group in range(GROUPS):
        for copy in copies[group]:
            copy.wait()
        tile = [
            jnp.dot(
                bt[...],
                kv[:, j * span + group * part : j * span + (group + 1) * part],
                preferred_element_type=jnp.float32,
            )
            for j in range(2)
        ]
        second = second_ref[:, group * part : (group + 1) * part]
        for i in range(2):
            for j in range(2):
                direct = tile[j][i * width : (i + 1) * width, :]
                exchange = tile[i][j * width : (j + 1) * width, :]
                denominator = ((occ_ref[i] + occ_ref[j]) - first_ref[...]) - second
                block = ((2.0 * direct - exchange) / denominator).astype(jnp.bfloat16)
                amps[i, j, :, group * part : (group + 1) * part] = block
                t2[
                    i * width : (i + 1) * width,
                    j * span + group * part : j * span + (group + 1) * part,
                ] = block
    half = half_ref.shape[2]
    at = pl.multiple_of(me * half + chunk * width, 16)
    outs = [
        pltpu.make_async_copy(amps, whole_ref.at[:, :, pl.ds(at, width), :], out_sem.at[0]),
        pltpu.make_async_copy(
            amps, half_ref.at[:, :, pl.ds(chunk * width, width), :], out_sem.at[1]
        ),
    ]
    for copy in outs:
        copy.start()
    for t in range(cols):
        home = lax.rem(here_col + t, cols)
        rows = pl.ds(pl.multiple_of(home * (2 * batch), 16), 2 * batch)
        share = lax.dot_general(
            kv[rows, :],
            t2[...],
            (((1,), (1,)), ((), ())),
            preferred_element_type=jnp.float32,
        )
        share_ref[t] = share
        if t == 1:
            down_ref[...] = share.astype(jnp.bfloat16)
        if t == cols - 1:
            up_ref[...] = share.astype(jnp.bfloat16)
    for copy in outs:
        copy.wait()


def run_chunk(chunk, ket, pieces, bra, ups, downs, steps, energies, held):
    _, _, _, batch, width = bra.shape
    cols = len(ups) + 1
    occ_energy, first, second = energies
    span = second.shape[1]
    half = width * CHUNKS
    total = cols * 2 * batch
    flops = 2 * 2 * total * 2 * width * 2 * span
    ins = [*ket, bra, *ups, *downs]
    any_space = pl.BlockSpec(memory_space=pl.ANY)
    in_vmem = pl.BlockSpec(memory_space=pltpu.VMEM)
    return pl.pallas_call(
        functools.partial(chunk_kernel, pieces, cols, steps, chunk),
        out_shape=(
            jax.ShapeDtypeStruct((2, 2, 2 * half, span), jnp.bfloat16),
            jax.ShapeDtypeStruct((2, 2, half, span), jnp.bfloat16),
            jax.ShapeDtypeStruct((cols, 2 * batch, 2 * width), jnp.float32),
            jax.ShapeDtypeStruct((2 * batch, 2 * width), jnp.bfloat16),
            jax.ShapeDtypeStruct((2 * batch, 2 * width), jnp.bfloat16),
        ),
        in_specs=[any_space] * len(ins)
        + [pl.BlockSpec(memory_space=pltpu.SMEM), in_vmem, in_vmem]
        + [any_space] * len(held),
        out_specs=(any_space, any_space, in_vmem, in_vmem, in_vmem),
        scratch_shapes=[
            pltpu.VMEM((total, 2 * span), jnp.bfloat16),
            pltpu.VMEM((cols, 2 * batch, 2 * width), jnp.bfloat16),
            pltpu.VMEM((2 * width, total), jnp.bfloat16),
            pltpu.VMEM((2 * width, 2 * span), jnp.bfloat16),
            pltpu.VMEM((2, 2, width, span), jnp.bfloat16),
            pltpu.SemaphoreType.DMA((GROUPS, 2, len(pieces), 2)),
            pltpu.SemaphoreType.DMA((cols, 2, 2)),
            pltpu.SemaphoreType.DMA((2,)),
        ],
        input_output_aliases={len(ins) + 3 + n: n for n in range(len(held))},
        compiler_params=pltpu.CompilerParams(vmem_limit_bytes=48 * 2**20),
        cost_estimate=pl.CostEstimate(
            flops=flops, bytes_accessed=total * 2 * span * 2, transcendentals=0
        ),
    )(*ins, occ_energy, first, second, *held)


def place_kernel(other, _, out, buffer, sems):
    half = other.shape[2]
    at = pl.multiple_of((1 - lax.axis_index("occ")) * half, 16)
    blocks = [(i, j) for i in range(2) for j in range(2)]
    reads = [
        pltpu.make_async_copy(other.at[i, j], buffer.at[i, j], sems.at[0, i, j]) for i, j in blocks
    ]
    writes = [
        pltpu.make_async_copy(
            buffer.at[i, j], out.at[i, j, pl.ds(at, half), :], sems.at[1, i, j]
        )
        for i, j in blocks
    ]
    for copy in reads:
        copy.start()
    for read, write in zip(reads, writes):
        read.wait()
        write.start()
    for copy in writes:
        copy.wait()


def place(other, whole):
    any_space = pl.BlockSpec(memory_space=pl.ANY)
    return pl.pallas_call(
        place_kernel,
        out_shape=jax.ShapeDtypeStruct(whole.shape, whole.dtype),
        in_specs=[any_space, any_space],
        out_specs=any_space,
        scratch_shapes=[
            pltpu.VMEM(other.shape, other.dtype),
            pltpu.SemaphoreType.DMA((2, 2, 2)),
        ],
        input_output_aliases={1: 0},
        compiler_params=pltpu.CompilerParams(vmem_limit_bytes=16 * 2**20),
        cost_estimate=pl.CostEstimate(
            flops=0, bytes_accessed=4 * other.size, transcendentals=0
        ),
    )(other, whole)


def swap(x):
    return lax.ppermute(x, "occ", [(0, 1), (1, 0)])


def planar(x, offset):
    return lax.ppermute(x, "row", [(r, r ^ offset) for r in range(4)])


def hop_up(x, cols, first=0, last=None):
    last = cols - 1 if last is None else last
    return lax.ppermute(x, "col", [(c, c + 1) for c in range(first, last)])


def hop_down(x, cols, first=0, last=None):
    last = cols - 1 if last is None else last
    return lax.ppermute(x, "col", [(cols - 1 - c, cols - 2 - c) for c in range(first, last)])


def both(*arrays):
    return lax.optimization_barrier(arrays)


def planned(bra_factor, ket_factor, occ_energy, virt_energy):
    batch, _, a_width = bra_factor.shape
    b_width = ket_factor.shape[2]
    half = a_width // 2
    width = half // CHUNKS
    cols = lax.axis_size("col")
    me, row_index, col_index = (lax.axis_index(name) for name in ("occ", "row", "col"))

    ket_own = ket_factor.reshape(batch, 2 * b_width)
    ket_x = planar(ket_own, 1)
    ket_y = planar(ket_own, 2)
    cut = batch // 2
    ket_far_y = planar(ket_x[:cut], 2)
    ket_far_x = planar(ket_y[cut:], 1)
    mine = [ket_own, ket_x, ket_y, ket_far_y, ket_far_x]
    pieces = ((0, 0, batch), (1, 0, batch), (2, 0, batch), (3, 0, cut), (3, cut, batch - cut))
    ket = mine + [swap(piece) for piece in mine]

    bra_plain = both(bra_factor.transpose(1, 0, 2))[0]

    def rows_of(side):
        part = lax.dynamic_slice_in_dim(bra_plain, side * half, half, 2)
        return part.reshape(2, batch, CHUNKS, width).transpose(2, 0, 1, 3)

    bra = jnp.stack([rows_of(me), swap(rows_of(1 - me))], axis=1)

    first_up, first_down = hop_up(bra[:1], cols), hop_down(bra[:1], cols)
    rest_up, rest_down = hop_up(bra[1:], cols), hop_down(bra[1:], cols)
    arrived = {0: ([first_up], [first_down])}
    for k in range(1, CHUNKS):
        arrived[k] = ([rest_up[k - 1 : k]], [rest_down[k - 1 : k]])

    def pass_on(k):
        ups, downs = arrived[k]
        for step in range(1, cols - 1):
            ups.append(hop_up(ups[-1], cols, first=step))
            downs.append(hop_down(downs[-1], cols, first=step))

    for k in range(CHUNKS):
        pass_on(k)

    second = lax.dynamic_slice_in_dim(virt_energy, col_index * b_width, b_width, 0)[None, :]
    first_all = lax.dynamic_slice_in_dim(virt_energy, row_index * a_width + me * half, half, 0)
    first_all = first_all[:, None]

    held = ()
    sums = {}
    shares = {}

    def step_sum(k, step):
        if step == 0:
            send_up, send_down = shares[k][1:]
        else:
            share = shares[k][0]
            up, down = sums[k]
            send_up = (share[cols - 1 - step] + up.astype(jnp.float32)).astype(jnp.bfloat16)
            send_down = (share[step + 1] + down.astype(jnp.float32)).astype(jnp.bfloat16)
        sums[k] = (hop_up(send_up, cols, last=step + 1), hop_down(send_down, cols, last=step + 1))

    ticks = CHUNKS + cols - 2
    for tick in range(ticks):
        if tick < CHUNKS:
            k = tick
            ups, downs = arrived[k]
            if k >= 2:
                older = [n for n in range(k - 1) if n in sums and n >= k - cols]
                flat = [x for n in older for x in sums[n]]
                tied = both(ups[0], *flat)
                ups = [tied[0], *ups[1:]]
                flat = tied[1:]
                for index, n in enumerate(older):
                    sums[n] = (flat[2 * index], flat[2 * index + 1])
            first = first_all[k * width : (k + 1) * width]
            steps = [0] * (cols - 1)
            *held, share, send_up, send_down = run_chunk(
                k, ket, pieces, bra, ups, downs, steps, (occ_energy, first, second), held
            )
            shares[k] = (share, send_up, send_down)
        for step in range(cols - 2, -1, -1):
            if 0 <= tick - step < CHUNKS:
                step_sum(tick - step, step)

    whole, mine_half = held
    amplitudes = place(swap(mine_half), whole)

    totals = []
    for k in range(CHUNKS):
        up, down = sums[k]
        totals.append(shares[k][0][0] + up.astype(jnp.float32) + down.astype(jnp.float32))

    def gathered(parts):
        whole = jnp.stack(parts).reshape(CHUNKS, batch, 2, width)
        return whole.transpose(1, 2, 0, 3).reshape(batch, 2, half)

    kept = gathered([total[:batch] for total in totals])
    received = gathered([swap(total[batch:]) for total in totals])
    gamma = jnp.where(
        me == 0,
        jnp.concatenate([kept, received], axis=2),
        jnp.concatenate([received, kept], axis=2),
    )
    return (amplitudes, gamma)


def solution(mesh):
    sizes = mesh.shape

    def on_device(bra_factor, ket_factor, occ_energy, virt_energy):
        fits = (
            sizes["occ"] == 2
            and sizes["row"] == 4
            and sizes["col"] > 1
            and bra_factor.shape[2] % (256 * CHUNKS) == 0
            and ket_factor.shape[2] % 512 == 0
            and bra_factor.shape[0] % 128 == 0
        )
        body = planned if fits else general
        return body(bra_factor, ket_factor, occ_energy, virt_energy)

    placed = (P(("occ", "col"), None, "row"), P(("occ", "row"), None, "col"), P(), P())
    return jax.shard_map(
        on_device,
        mesh=mesh,
        in_specs=placed,
        out_specs=(P(None, None, "row", "col"), P(("occ", "col"), None, "row")),
        check_vma=False,
    )
```

```python
import functools

import jax
import jax.numpy as jnp
from jax import lax
from jax.experimental import pallas as pl
from jax.experimental.pallas import tpu as pltpu
from jax.sharding import PartitionSpec as P


def make_amplitudes(coulomb, occ_energy, virt_first, virt_second):
    denominator = (
        occ_energy[:, None, None, None]
        + occ_energy[None, :, None, None]
        - virt_first[None, None, :, None]
        - virt_second[None, None, None, :]
    )
    return ((2.0 * coulomb - jnp.transpose(coulomb, (1, 0, 2, 3))) / denominator).astype(
        jnp.bfloat16
    )


def general(bra_factor, ket_factor, occ_energy, virt_energy):
    a_width = bra_factor.shape[2]
    b_width = ket_factor.shape[2]
    ket_whole = lax.all_gather(ket_factor, "row", axis=0, tiled=True)
    row_index = lax.axis_index("row")
    col_index = lax.axis_index("col")
    virt_first = lax.dynamic_slice_in_dim(virt_energy, row_index * a_width, a_width, 0)
    virt_second = lax.dynamic_slice_in_dim(virt_energy, col_index * b_width, b_width, 0)
    partial_sum = jnp.einsum(
        "qia,qjb->ijab",
        lax.all_gather(bra_factor, "col", axis=0, tiled=True),
        ket_whole,
        preferred_element_type=jnp.float32,
    )
    batch_count = lax.axis_size("occ")
    pad_rows = (batch_count - a_width % batch_count) % batch_count
    padded = jnp.pad(partial_sum, ((0, 0), (0, 0), (0, pad_rows), (0, 0)))
    share_sum = lax.psum_scatter(padded, "occ", scatter_dimension=2, tiled=True)
    share_len = share_sum.shape[2]
    energy_padded = jnp.pad(virt_first, (0, pad_rows), constant_values=1.0)
    energy_share = lax.dynamic_slice_in_dim(
        energy_padded, lax.axis_index("occ") * share_len, share_len, 0
    )
    share_amps = make_amplitudes(share_sum, occ_energy, energy_share, virt_second)
    collected = lax.all_gather(share_amps, "occ", axis=2, tiled=True)
    amplitudes = collected[:, :, :a_width, :]
    gamma = lax.psum_scatter(
        jnp.einsum("ijab,qjb->qia", amplitudes, ket_whole, preferred_element_type=jnp.float32),
        "col",
        scatter_dimension=0,
        tiled=True,
    )
    return (amplitudes, gamma)


CHUNKS = 4
GROUPS = 4


def chunk_kernel(pieces, chunk, *refs):
    refs = list(refs)
    take = lambda count: [refs.pop(0) for _ in range(count)]
    ket = take(2 * len(pieces))
    bra, paired, crossed, handed, occ_ref, first_ref, second_ref = take(7)
    if chunk:
        take(2)
    whole_ref, half_ref, own_ref, pair_ref, far_ref, send_ref = take(6)
    kv, bv, bt, t2, amps, ket_sem, bra_sem, out_sem = refs
    width = first_ref.shape[0]
    span = second_ref.shape[1]
    part = span // GROUPS
    batch = bra.shape[2]
    here_row, here_col = lax.axis_index("row"), lax.axis_index("col")
    me = lax.axis_index("occ")
    pair = lax.bitwise_xor(here_col, 1)
    low = here_col < 2
    middle = jnp.logical_or(here_col == 1, here_col == 2)

    def bra_copies(source, home, slot):
        return [
            pltpu.make_async_copy(
                source.at[q, i],
                bv.at[home, pl.ds(q * batch, batch), pl.ds(i * width, width)],
                bra_sem.at[slot, q, i],
            )
            for q in range(2)
            for i in range(2)
        ]

    for copy in bra_copies(bra, here_col, 0) + bra_copies(paired, pair, 1):
        copy.start()
    for n in range(2):
        home = jnp.where(low, 2 + n, 1 - n)

        @pl.when(middle)
        def _():
            for copy in bra_copies(crossed.at[n], home, 2 + n):
                copy.start()

        @pl.when(jnp.logical_not(middle))
        def _():
            for copy in bra_copies(handed.at[n], home, 2 + n):
                copy.start()

    copies = []
    for group in range(GROUPS):
        of_group = []
        for q in range(2):
            for index, (offset, begin, rows) in enumerate(pieces):
                home = lax.bitwise_xor(here_row, offset)
                to_row = pl.multiple_of(home * (2 * batch) + q * batch + begin, 16)
                for j in range(2):
                    columns = pl.ds(j * span + group * part, part)
                    copy = pltpu.make_async_copy(
                        ket[q * len(pieces) + index].at[:, columns],
                        kv.at[pl.ds(to_row, rows), columns],
                        ket_sem.at[group, q, index, j],
                    )
                    copy.start()
                    of_group.append(copy)
        copies.append(of_group)
    for slot in range(4):
        for copy in bra_copies(bra, slot, slot):
            copy.wait()
    for d in range(4):
        bt[:, d * 2 * batch : (d + 1) * 2 * batch] = bv[d].T
    for group in range(GROUPS):
        for copy in copies[group]:
            copy.wait()
        tile = [
            jnp.dot(
                bt[...],
                kv[:, j * span + group * part : j * span + (group + 1) * part],
                preferred_element_type=jnp.float32,
            )
            for j in range(2)
        ]
        second = second_ref[:, group * part : (group + 1) * part]
        for i in range(2):
            for j in range(2):
                direct = tile[j][i * width : (i + 1) * width, :]
                exchange = tile[i][j * width : (j + 1) * width, :]
                denominator = ((occ_ref[i] + occ_ref[j]) - first_ref[...]) - second
                block = ((2.0 * direct - exchange) / denominator).astype(jnp.bfloat16)
                amps[i, j, :, group * part : (group + 1) * part] = block
                t2[
                    i * width : (i + 1) * width,
                    j * span + group * part : j * span + (group + 1) * part,
                ] = block
    half = half_ref.shape[2]
    at = pl.multiple_of(me * half + chunk * width, 16)
    outs = [
        pltpu.make_async_copy(amps, whole_ref.at[:, :, pl.ds(at, width), :], out_sem.at[0]),
        pltpu.make_async_copy(
            amps, half_ref.at[:, :, pl.ds(chunk * width, width), :], out_sem.at[1]
        ),
    ]
    for copy in outs:
        copy.start()

    def share_of(home):
        rows = pl.ds(pl.multiple_of(home * (2 * batch), 16), 2 * batch)
        return lax.dot_general(
            kv[rows, :],
            t2[...],
            (((1,), (1,)), ((), ())),
            preferred_element_type=jnp.float32,
        )

    for n in range(2):
        share = share_of(jnp.where(low, 2 + n, n))
        far_ref[n] = share
        send_ref[n] = share.astype(jnp.bfloat16)
    pair_ref[...] = share_of(pair)
    own_ref[...] = share_of(here_col)
    for copy in outs:
        copy.wait()


def run_chunk(chunk, ket, pieces, bras, energies, held):
    _, _, batch, width = bras[0].shape
    occ_energy, first, second = energies
    span = second.shape[1]
    half = width * CHUNKS
    total = 8 * batch
    flops = 2 * 2 * total * 2 * width * 2 * span
    ins = [*ket, *bras]
    any_space = pl.BlockSpec(memory_space=pl.ANY)
    in_vmem = pl.BlockSpec(memory_space=pltpu.VMEM)
    return pl.pallas_call(
        functools.partial(chunk_kernel, pieces, chunk),
        out_shape=(
            jax.ShapeDtypeStruct((2, 2, 2 * half, span), jnp.bfloat16),
            jax.ShapeDtypeStruct((2, 2, half, span), jnp.bfloat16),
            jax.ShapeDtypeStruct((2 * batch, 2 * width), jnp.float32),
            jax.ShapeDtypeStruct((2 * batch, 2 * width), jnp.float32),
            jax.ShapeDtypeStruct((2, 2 * batch, 2 * width), jnp.float32),
            jax.ShapeDtypeStruct((2, 2 * batch, 2 * width), jnp.bfloat16),
        ),
        in_specs=[any_space] * len(ins)
        + [pl.BlockSpec(memory_space=pltpu.SMEM), in_vmem, in_vmem]
        + [any_space] * len(held),
        out_specs=(any_space, any_space, in_vmem, in_vmem, in_vmem, in_vmem),
        scratch_shapes=[
            pltpu.VMEM((total, 2 * span), jnp.bfloat16),
            pltpu.VMEM((4, 2 * batch, 2 * width), jnp.bfloat16),
            pltpu.VMEM((2 * width, total), jnp.bfloat16),
            pltpu.VMEM((2 * width, 2 * span), jnp.bfloat16),
            pltpu.VMEM((2, 2, width, span), jnp.bfloat16),
            pltpu.SemaphoreType.DMA((GROUPS, 2, len(pieces), 2)),
            pltpu.SemaphoreType.DMA((4, 2, 2)),
            pltpu.SemaphoreType.DMA((2,)),
        ],
        input_output_aliases={len(ins) + 3 + n: n for n in range(len(held))},
        compiler_params=pltpu.CompilerParams(vmem_limit_bytes=48 * 2**20),
        cost_estimate=pl.CostEstimate(
            flops=flops, bytes_accessed=total * 2 * span * 2, transcendentals=0
        ),
    )(*ins, occ_energy, first, second, *held)


def place_kernel(other, _, out, buffer, sems):
    half = other.shape[2]
    at = pl.multiple_of((1 - lax.axis_index("occ")) * half, 16)
    blocks = [(i, j) for i in range(2) for j in range(2)]
    reads = [
        pltpu.make_async_copy(other.at[i, j], buffer.at[i, j], sems.at[0, i, j]) for i, j in blocks
    ]
    writes = [
        pltpu.make_async_copy(
            buffer.at[i, j], out.at[i, j, pl.ds(at, half), :], sems.at[1, i, j]
        )
        for i, j in blocks
    ]
    for copy in reads:
        copy.start()
    for read, write in zip(reads, writes):
        read.wait()
        write.start()
    for copy in writes:
        copy.wait()


def place(other, whole):
    any_space = pl.BlockSpec(memory_space=pl.ANY)
    return pl.pallas_call(
        place_kernel,
        out_shape=jax.ShapeDtypeStruct(whole.shape, whole.dtype),
        in_specs=[any_space, any_space],
        out_specs=any_space,
        scratch_shapes=[
            pltpu.VMEM(other.shape, other.dtype),
            pltpu.SemaphoreType.DMA((2, 2, 2)),
        ],
        input_output_aliases={1: 0},
        compiler_params=pltpu.CompilerParams(vmem_limit_bytes=16 * 2**20),
        cost_estimate=pl.CostEstimate(
            flops=0, bytes_accessed=4 * other.size, transcendentals=0
        ),
    )(other, whole)


def join_kernel(*refs):
    out = refs[-1]
    me = lax.axis_index("occ")
    width = refs[0].shape[1] // 2
    for n, ref in enumerate(refs[:-1]):
        side, k = divmod(n, CHUNKS)
        home = jnp.where(me == side, 0, CHUNKS * width) + k * width
        for i in range(2):
            out[:, i, pl.ds(pl.multiple_of(home, 128), width)] = ref[
                : out.shape[0], i * width : (i + 1) * width
            ]


def join(kept, received):
    batch, double = received[0].shape
    return pl.pallas_call(
        join_kernel,
        out_shape=jax.ShapeDtypeStruct((batch, 2, CHUNKS * double), jnp.float32),
        compiler_params=pltpu.CompilerParams(vmem_limit_bytes=40 * 2**20),
        cost_estimate=pl.CostEstimate(
            flops=0, bytes_accessed=16 * batch * double * CHUNKS, transcendentals=0
        ),
    )(*kept, *received)


def swap(x):
    return lax.ppermute(x, "occ", [(0, 1), (1, 0)])


def planar(x, offset):
    return lax.ppermute(x, "row", [(r, r ^ offset) for r in range(4)])


def pairs(x):
    return lax.ppermute(x, "col", [(0, 1), (1, 0), (2, 3), (3, 2)])


def across(x):
    return lax.ppermute(x, "col", [(1, 2), (2, 1)])


def outward(x):
    return lax.ppermute(x, "col", [(1, 0), (2, 3)])


def inward(x):
    return lax.ppermute(x, "col", [(0, 1), (3, 2)])


def tie(*arrays):
    return lax.optimization_barrier(arrays)


def planned(bra_factor, ket_factor, occ_energy, virt_energy):
    batch, _, a_width = bra_factor.shape
    b_width = ket_factor.shape[2]
    half = a_width // 2
    width = half // CHUNKS
    me, row_index, col_index = (lax.axis_index(name) for name in ("occ", "row", "col"))

    ket_own = ket_factor.reshape(batch, 2 * b_width)
    ket_own, bra_factor = tie(ket_own, bra_factor)
    ket_x = planar(ket_own, 1)
    ket_y = planar(ket_own, 2)
    cut = batch // 2
    ket_far_y = planar(ket_x[:cut], 2)
    ket_far_x = planar(ket_y[cut:], 1)
    mine = [ket_own, ket_x, ket_y, ket_far_y, ket_far_x]
    pieces = ((0, 0, batch), (1, 0, batch), (2, 0, batch), (3, 0, cut), (3, cut, batch - cut))
    ket = mine + [swap(piece) for piece in mine]

    bra_plain = tie(bra_factor.transpose(1, 0, 2))[0]

    def rows_of(side):
        part = lax.dynamic_slice_in_dim(bra_plain, side * half, half, 2)
        return part.reshape(2, batch, CHUNKS, width).transpose(2, 0, 1, 3)

    bra = jnp.stack([rows_of(me), swap(rows_of(1 - me))], axis=1)
    paired_first, paired_rest = pairs(bra[0]), pairs(bra[1:])
    bras = []
    for k in range(CHUNKS):
        paired = paired_rest[k - 1] if k else paired_first
        crossed = across(jnp.stack([bra[k], paired]))
        bras.append((bra[k], paired, crossed, outward(crossed)))

    second = lax.dynamic_slice_in_dim(virt_energy, col_index * b_width, b_width, 0)[None, :]
    first_all = lax.dynamic_slice_in_dim(virt_energy, row_index * a_width + me * half, half, 0)
    first_all = first_all[:, None]

    def up_cast(x):
        return x.astype(jnp.float32)

    near = lax.bitwise_and(col_index, 1)
    held = ()
    own, pair, far, one, two, three, kept, received = ({} for _ in range(8))

    def cross(k):
        two[k] = across((far[k] + up_cast(one[k])).astype(jnp.bfloat16))

    def exchange(k):
        theirs = lax.dynamic_index_in_dim(two[k], 1 - near, 0, keepdims=False)
        three[k] = pairs((pair[k] + up_cast(theirs)).astype(jnp.bfloat16))

    def finish(k):
        ours = lax.dynamic_index_in_dim(two[k], near, 0, keepdims=False)
        total = own[k] + up_cast(ours) + up_cast(three[k])
        kept[k] = total[:batch]
        received[k] = swap(total[batch:])

    for tick in range(CHUNKS + 3):
        if tick < CHUNKS:
            k = tick
            blocks = list(bras[k])
            if k >= 2:
                one[k - 2], blocks[0] = tie(one[k - 2], blocks[0])
            if k >= 3:
                two[k - 3], blocks[0] = tie(two[k - 3], blocks[0])
            first = first_all[k * width : (k + 1) * width]
            *held, own[k], pair[k], far[k], send = run_chunk(
                k, ket, pieces, blocks, (occ_energy, first, second), held
            )
            one[k] = inward(send)
        for step, move in ((3, finish), (2, exchange), (1, cross)):
            if 0 <= tick - step < CHUNKS:
                move(tick - step)

    whole, mine_half = held
    amplitudes = place(swap(mine_half), whole)
    last = CHUNKS - 1
    amplitudes, kept[last] = tie(amplitudes, kept[last])
    gamma = join([kept[k] for k in range(CHUNKS)], [received[k] for k in range(CHUNKS)])
    return (amplitudes, gamma)


def solution(mesh):
    sizes = mesh.shape

    def on_device(bra_factor, ket_factor, occ_energy, virt_energy):
        fits = (
            sizes["occ"] == 2
            and sizes["row"] == 4
            and sizes["col"] == 4
            and bra_factor.shape[2] % (256 * CHUNKS) == 0
            and ket_factor.shape[2] % 512 == 0
            and bra_factor.shape[0] % 128 == 0
        )
        body = planned if fits else general
        return body(bra_factor, ket_factor, occ_energy, virt_energy)

    placed = (P(("occ", "col"), None, "row"), P(("occ", "row"), None, "col"), P(), P())
    return jax.shard_map(
        on_device,
        mesh=mesh,
        in_specs=placed,
        out_specs=(P(None, None, "row", "col"), P(("occ", "col"), None, "row")),
        check_vma=False,
    )
```

```python
import functools

import jax
import jax.numpy as jnp
from jax import lax
from jax.experimental import pallas as pl
from jax.experimental.pallas import tpu as pltpu
from jax.sharding import PartitionSpec as P


def make_amplitudes(coulomb, occ_energy, virt_first, virt_second):
    denominator = (
        occ_energy[:, None, None, None]
        + occ_energy[None, :, None, None]
        - virt_first[None, None, :, None]
        - virt_second[None, None, None, :]
    )
    return ((2.0 * coulomb - jnp.transpose(coulomb, (1, 0, 2, 3))) / denominator).astype(
        jnp.bfloat16
    )


def general(bra_factor, ket_factor, occ_energy, virt_energy):
    a_width = bra_factor.shape[2]
    b_width = ket_factor.shape[2]
    ket_whole = lax.all_gather(ket_factor, "row", axis=0, tiled=True)
    row_index = lax.axis_index("row")
    col_index = lax.axis_index("col")
    virt_first = lax.dynamic_slice_in_dim(virt_energy, row_index * a_width, a_width, 0)
    virt_second = lax.dynamic_slice_in_dim(virt_energy, col_index * b_width, b_width, 0)
    partial_sum = jnp.einsum(
        "qia,qjb->ijab",
        lax.all_gather(bra_factor, "col", axis=0, tiled=True),
        ket_whole,
        preferred_element_type=jnp.float32,
    )
    batch_count = lax.axis_size("occ")
    pad_rows = (batch_count - a_width % batch_count) % batch_count
    padded = jnp.pad(partial_sum, ((0, 0), (0, 0), (0, pad_rows), (0, 0)))
    share_sum = lax.psum_scatter(padded, "occ", scatter_dimension=2, tiled=True)
    share_len = share_sum.shape[2]
    energy_padded = jnp.pad(virt_first, (0, pad_rows), constant_values=1.0)
    energy_share = lax.dynamic_slice_in_dim(
        energy_padded, lax.axis_index("occ") * share_len, share_len, 0
    )
    share_amps = make_amplitudes(share_sum, occ_energy, energy_share, virt_second)
    collected = lax.all_gather(share_amps, "occ", axis=2, tiled=True)
    amplitudes = collected[:, :, :a_width, :]
    gamma = lax.psum_scatter(
        jnp.einsum("ijab,qjb->qia", amplitudes, ket_whole, preferred_element_type=jnp.float32),
        "col",
        scatter_dimension=0,
        tiled=True,
    )
    return (amplitudes, gamma)


CHUNKS = 4
GROUPS = 4


def chunk_kernel(pieces, chunk, *refs):
    refs = list(refs)
    take = lambda count: [refs.pop(0) for _ in range(count)]
    ket = take(2 * len(pieces))
    bra, paired, crossed, handed, occ_ref, virt_ref = take(6)
    if chunk:
        take(2)
    whole_ref, half_ref, own_ref, pair_ref, far_ref, send_ref = take(6)
    kv, bv, bt, t2, amps, ket_sem, bra_sem, out_sem = refs
    width = bra.shape[3]
    span = ket[0].shape[1] // 2
    half = half_ref.shape[2]
    part = span // GROUPS
    batch = bra.shape[2]
    here_row, here_col = lax.axis_index("row"), lax.axis_index("col")
    me = lax.axis_index("occ")
    pair = lax.bitwise_xor(here_col, 1)
    low = here_col < 2
    middle = jnp.logical_or(here_col == 1, here_col == 2)

    def bra_copies(source, home, slot):
        return [
            pltpu.make_async_copy(
                source.at[q, i],
                bv.at[home, pl.ds(q * batch, batch), pl.ds(i * width, width)],
                bra_sem.at[slot, q, i],
            )
            for q in range(2)
            for i in range(2)
        ]

    for copy in bra_copies(bra, here_col, 0) + bra_copies(paired, pair, 1):
        copy.start()
    for n in range(2):
        home = jnp.where(low, 2 + n, 1 - n)

        @pl.when(middle)
        def _():
            for copy in bra_copies(crossed.at[n], home, 2 + n):
                copy.start()

        @pl.when(jnp.logical_not(middle))
        def _():
            for copy in bra_copies(handed.at[n], home, 2 + n):
                copy.start()

    copies = []
    for group in range(GROUPS):
        of_group = []
        for q in range(2):
            for index, (offset, begin, rows) in enumerate(pieces):
                home = lax.bitwise_xor(here_row, offset)
                to_row = pl.multiple_of(home * (2 * batch) + q * batch + begin, 16)
                for j in range(2):
                    columns = pl.ds(j * span + group * part, part)
                    copy = pltpu.make_async_copy(
                        ket[q * len(pieces) + index].at[:, columns],
                        kv.at[pl.ds(to_row, rows), columns],
                        ket_sem.at[group, q, index, j],
                    )
                    copy.start()
                    of_group.append(copy)
        copies.append(of_group)
    for slot in range(4):
        for copy in bra_copies(bra, slot, slot):
            copy.wait()
    first_at = here_row * (2 * half) + me * half + chunk * width
    first = virt_ref[:, pl.ds(pl.multiple_of(first_at, 128), width)]
    first = jnp.broadcast_to(first, (width, width)).T[:, :1]
    for d in range(4):
        bt[:, d * 2 * batch : (d + 1) * 2 * batch] = bv[d].T
    for group in range(GROUPS):
        for copy in copies[group]:
            copy.wait()
        tile = [
            jnp.dot(
                bt[...],
                kv[:, j * span + group * part : j * span + (group + 1) * part],
                preferred_element_type=jnp.float32,
            )
            for j in range(2)
        ]
        second_at = pl.multiple_of(here_col * span + group * part, 128)
        second = virt_ref[:, pl.ds(second_at, part)]
        for i in range(2):
            for j in range(2):
                direct = tile[j][i * width : (i + 1) * width, :]
                exchange = tile[i][j * width : (j + 1) * width, :]
                denominator = ((occ_ref[i] + occ_ref[j]) - first) - second
                block = ((2.0 * direct - exchange) / denominator).astype(jnp.bfloat16)
                amps[i, j, :, group * part : (group + 1) * part] = block
                t2[
                    i * width : (i + 1) * width,
                    j * span + group * part : j * span + (group + 1) * part,
                ] = block
    at = pl.multiple_of(me * half + chunk * width, 16)
    outs = [
        pltpu.make_async_copy(amps, whole_ref.at[:, :, pl.ds(at, width), :], out_sem.at[0]),
        pltpu.make_async_copy(
            amps, half_ref.at[:, :, pl.ds(chunk * width, width), :], out_sem.at[1]
        ),
    ]
    for copy in outs:
        copy.start()

    def share_of(home):
        rows = pl.ds(pl.multiple_of(home * (2 * batch), 16), 2 * batch)
        return lax.dot_general(
            kv[rows, :],
            t2[...],
            (((1,), (1,)), ((), ())),
            preferred_element_type=jnp.float32,
        )

    for n in range(2):
        share = share_of(jnp.where(low, 2 + n, n))
        far_ref[n] = share
        send_ref[n] = share.astype(jnp.bfloat16)
    pair_ref[...] = share_of(pair)
    own_ref[...] = share_of(here_col)
    for copy in outs:
        copy.wait()


def run_chunk(chunk, ket, pieces, bras, energies, held):
    _, _, batch, width = bras[0].shape
    span = ket[0].shape[1] // 2
    half = width * CHUNKS
    total = 8 * batch
    flops = 2 * 2 * total * 2 * width * 2 * span
    ins = [*ket, *bras]
    any_space = pl.BlockSpec(memory_space=pl.ANY)
    in_vmem = pl.BlockSpec(memory_space=pltpu.VMEM)
    return pl.pallas_call(
        functools.partial(chunk_kernel, pieces, chunk),
        out_shape=(
            jax.ShapeDtypeStruct((2, 2, 2 * half, span), jnp.bfloat16),
            jax.ShapeDtypeStruct((2, 2, half, span), jnp.bfloat16),
            jax.ShapeDtypeStruct((2 * batch, 2 * width), jnp.float32),
            jax.ShapeDtypeStruct((2 * batch, 2 * width), jnp.float32),
            jax.ShapeDtypeStruct((2, 2 * batch, 2 * width), jnp.float32),
            jax.ShapeDtypeStruct((2, 2 * batch, 2 * width), jnp.bfloat16),
        ),
        in_specs=[any_space] * len(ins)
        + [pl.BlockSpec(memory_space=pltpu.SMEM), in_vmem]
        + [any_space] * len(held),
        out_specs=(any_space, any_space, in_vmem, in_vmem, in_vmem, in_vmem),
        scratch_shapes=[
            pltpu.VMEM((total, 2 * span), jnp.bfloat16),
            pltpu.VMEM((4, 2 * batch, 2 * width), jnp.bfloat16),
            pltpu.VMEM((2 * width, total), jnp.bfloat16),
            pltpu.VMEM((2 * width, 2 * span), jnp.bfloat16),
            pltpu.VMEM((2, 2, width, span), jnp.bfloat16),
            pltpu.SemaphoreType.DMA((GROUPS, 2, len(pieces), 2)),
            pltpu.SemaphoreType.DMA((4, 2, 2)),
            pltpu.SemaphoreType.DMA((2,)),
        ],
        input_output_aliases={len(ins) + 2 + n: n for n in range(len(held))},
        compiler_params=pltpu.CompilerParams(vmem_limit_bytes=30 * 2**20),
        cost_estimate=pl.CostEstimate(
            flops=flops, bytes_accessed=total * 2 * span * 2, transcendentals=0
        ),
    )(*ins, *energies, *held)


def place_kernel(other, _, out, buffer, sems):
    half = other.shape[2]
    at = pl.multiple_of((1 - lax.axis_index("occ")) * half, 16)
    blocks = [(i, j) for i in range(2) for j in range(2)]
    reads = [
        pltpu.make_async_copy(other.at[i, j], buffer.at[i, j], sems.at[0, i, j]) for i, j in blocks
    ]
    writes = [
        pltpu.make_async_copy(
            buffer.at[i, j], out.at[i, j, pl.ds(at, half), :], sems.at[1, i, j]
        )
        for i, j in blocks
    ]
    for copy in reads:
        copy.start()
    for read, write in zip(reads, writes):
        read.wait()
        write.start()
    for copy in writes:
        copy.wait()


def place(other, whole):
    any_space = pl.BlockSpec(memory_space=pl.ANY)
    return pl.pallas_call(
        place_kernel,
        out_shape=jax.ShapeDtypeStruct(whole.shape, whole.dtype),
        in_specs=[any_space, any_space],
        out_specs=any_space,
        scratch_shapes=[
            pltpu.VMEM(other.shape, other.dtype),
            pltpu.SemaphoreType.DMA((2, 2, 2)),
        ],
        input_output_aliases={1: 0},
        compiler_params=pltpu.CompilerParams(vmem_limit_bytes=16 * 2**20),
        cost_estimate=pl.CostEstimate(
            flops=0, bytes_accessed=4 * other.size, transcendentals=0
        ),
    )(other, whole)


def join_kernel(chunks, held, *refs):
    out, buffers, sems = refs[-3:]
    me = lax.axis_index("occ")
    count = len(chunks)
    batch, _, columns = out.shape
    width = refs[0].shape[1] // 2
    copies = []
    for n in range(2 * count):
        side, place = divmod(n, count)
        home = jnp.where(me == side, 0, columns // 2) + chunks[place] * width
        for i in range(2):
            buffers[n, :, i, :] = refs[n][:, i * width : (i + 1) * width]
        copies.append(
            pltpu.make_async_copy(
                buffers.at[n], out.at[:, :, pl.ds(pl.multiple_of(home, 128), width)], sems.at[n]
            )
        )
        copies[-1].start()
    for copy in copies:
        copy.wait()


def join(chunks, kept, received, held=()):
    batch, double = received[0].shape
    count = len(chunks)
    any_space = pl.BlockSpec(memory_space=pl.ANY)
    return pl.pallas_call(
        functools.partial(join_kernel, chunks, len(held)),
        out_shape=jax.ShapeDtypeStruct((batch, 2, CHUNKS * double), jnp.float32),
        in_specs=[pl.BlockSpec(memory_space=pltpu.VMEM)] * (2 * count) + [any_space] * len(held),
        out_specs=any_space,
        scratch_shapes=[
            pltpu.VMEM((2 * count, batch, 2, double // 2), jnp.float32),
            pltpu.SemaphoreType.DMA((2 * count,)),
        ],
        input_output_aliases={2 * count: 0} if held else {},
        compiler_params=pltpu.CompilerParams(vmem_limit_bytes=40 * 2**20),
        cost_estimate=pl.CostEstimate(
            flops=0, bytes_accessed=16 * batch * double * count, transcendentals=0
        ),
    )(*kept, *received, *held)


def swap(x):
    return lax.ppermute(x, "occ", [(0, 1), (1, 0)])


def planar(x, offset):
    return lax.ppermute(x, "row", [(r, r ^ offset) for r in range(4)])


def pairs(x):
    return lax.ppermute(x, "col", [(0, 1), (1, 0), (2, 3), (3, 2)])


def across(x):
    return lax.ppermute(x, "col", [(1, 2), (2, 1)])


def outward(x):
    return lax.ppermute(x, "col", [(1, 0), (2, 3)])


def inward(x):
    return lax.ppermute(x, "col", [(0, 1), (3, 2)])


def tie(*arrays):
    return lax.optimization_barrier(arrays)


def planned(bra_factor, ket_factor, occ_energy, virt_energy):
    batch, _, a_width = bra_factor.shape
    b_width = ket_factor.shape[2]
    half = a_width // 2
    width = half // CHUNKS
    me, row_index, col_index = (lax.axis_index(name) for name in ("occ", "row", "col"))

    ket_own = ket_factor.reshape(batch, 2 * b_width)
    ket_own, bra_factor = tie(ket_own, bra_factor)
    ket_x = planar(ket_own, 1)
    ket_y = planar(ket_own, 2)
    cut = batch // 2
    ket_far_y = planar(ket_x[:cut], 2)
    ket_far_x = planar(ket_y[cut:], 1)
    pieces = ((0, 0, batch), (1, 0, batch), (2, 0, batch), (3, 0, cut), (3, cut, batch - cut))

    bra_plain = tie(bra_factor.transpose(1, 0, 2))[0]

    def rows_of(side):
        part = lax.dynamic_slice_in_dim(bra_plain, side * half, half, 2)
        return part.reshape(2, batch, CHUNKS, width).transpose(2, 0, 1, 3)

    bra = jnp.stack([rows_of(me), swap(rows_of(1 - me))], axis=1)
    paired_first, paired_rest = pairs(bra[0]), pairs(bra[1:])
    stacked = [jnp.stack([bra[0], paired_first])]
    stacked += [jnp.stack([bra[k], paired_rest[k - 1]]) for k in range(1, CHUNKS)]
    crossed = [across(part) for part in stacked]
    mine = [ket_own, ket_x, ket_y, ket_far_y, ket_far_x]
    ket = mine + [swap(piece) for piece in mine]
    energies = (occ_energy, virt_energy[None, :])

    def up_cast(x):
        return x.astype(jnp.float32)

    near = lax.bitwise_and(col_index, 1)
    held = ()
    own, pair, far, one, two, three, kept, received = ({} for _ in range(8))

    def cross(k):
        two[k] = across((far[k] + up_cast(one[k])).astype(jnp.bfloat16))

    def exchange(k):
        theirs = lax.dynamic_index_in_dim(two[k], 1 - near, 0, keepdims=False)
        three[k] = pairs((pair[k] + up_cast(theirs)).astype(jnp.bfloat16))

    def finish(k):
        ours = lax.dynamic_index_in_dim(two[k], near, 0, keepdims=False)
        total = own[k] + up_cast(ours) + up_cast(three[k])
        kept[k] = total[:batch]
        received[k] = swap(total[batch:])

    for tick in range(CHUNKS + 3):
        if tick < CHUNKS:
            k = tick
            blocks = [bra[k], paired_rest[k - 1] if k else paired_first, crossed[k]]
            if k == 1:
                crossed[1] = tie(own[0], crossed[1])[1]
            blocks.append(outward(crossed[k]))
            if k >= 2:
                one[k - 2], blocks[0] = tie(one[k - 2], blocks[0])
            if k >= 3:
                two[k - 3], blocks[0] = tie(two[k - 3], blocks[0])
            *held, own[k], pair[k], far[k], send = run_chunk(
                k, ket, pieces, blocks, energies, held
            )
            one[k] = inward(send)
        if 1 <= tick <= CHUNKS:
            cross(tick - 1)
    last = CHUNKS - 1
    amplitudes = place(swap(held[1]), held[0])
    exchange(0)
    exchange(1)
    exchange(2)
    exchange(last)
    for k in range(CHUNKS):
        finish(k)
    early = list(range(last))
    gamma = join(early, [kept[k] for k in early], [received[k] for k in early])
    gamma = join([last], [kept[last]], [received[last]], (gamma,))
    return (amplitudes, gamma)


def solution(mesh):
    sizes = mesh.shape

    def on_device(bra_factor, ket_factor, occ_energy, virt_energy):
        fits = (
            sizes["occ"] == 2
            and sizes["row"] == 4
            and sizes["col"] == 4
            and bra_factor.shape[2] % (256 * CHUNKS) == 0
            and ket_factor.shape[2] % 512 == 0
            and bra_factor.shape[0] % 128 == 0
        )
        body = planned if fits else general
        return body(bra_factor, ket_factor, occ_energy, virt_energy)

    placed = (P(("occ", "col"), None, "row"), P(("occ", "row"), None, "col"), P(), P())
    return jax.shard_map(
        on_device,
        mesh=mesh,
        in_specs=placed,
        out_specs=(P(None, None, "row", "col"), P(("occ", "col"), None, "row")),
        check_vma=False,
    )
```

```python
import functools

import jax
import jax.numpy as jnp
from jax import lax
from jax.experimental import pallas as pl
from jax.experimental.pallas import tpu as pltpu
from jax.sharding import PartitionSpec as P


def make_amplitudes(coulomb, occ_energy, virt_first, virt_second):
    denominator = (
        occ_energy[:, None, None, None]
        + occ_energy[None, :, None, None]
        - virt_first[None, None, :, None]
        - virt_second[None, None, None, :]
    )
    return ((2.0 * coulomb - jnp.transpose(coulomb, (1, 0, 2, 3))) / denominator).astype(
        jnp.bfloat16
    )


def general(bra_factor, ket_factor, occ_energy, virt_energy):
    a_width = bra_factor.shape[2]
    b_width = ket_factor.shape[2]
    ket_whole = lax.all_gather(ket_factor, "row", axis=0, tiled=True)
    row_index = lax.axis_index("row")
    col_index = lax.axis_index("col")
    virt_first = lax.dynamic_slice_in_dim(virt_energy, row_index * a_width, a_width, 0)
    virt_second = lax.dynamic_slice_in_dim(virt_energy, col_index * b_width, b_width, 0)
    partial_sum = jnp.einsum(
        "qia,qjb->ijab",
        lax.all_gather(bra_factor, "col", axis=0, tiled=True),
        ket_whole,
        preferred_element_type=jnp.float32,
    )
    batch_count = lax.axis_size("occ")
    pad_rows = (batch_count - a_width % batch_count) % batch_count
    padded = jnp.pad(partial_sum, ((0, 0), (0, 0), (0, pad_rows), (0, 0)))
    share_sum = lax.psum_scatter(padded, "occ", scatter_dimension=2, tiled=True)
    share_len = share_sum.shape[2]
    energy_padded = jnp.pad(virt_first, (0, pad_rows), constant_values=1.0)
    energy_share = lax.dynamic_slice_in_dim(
        energy_padded, lax.axis_index("occ") * share_len, share_len, 0
    )
    share_amps = make_amplitudes(share_sum, occ_energy, energy_share, virt_second)
    collected = lax.all_gather(share_amps, "occ", axis=2, tiled=True)
    amplitudes = collected[:, :, :a_width, :]
    gamma = lax.psum_scatter(
        jnp.einsum("ijab,qjb->qia", amplitudes, ket_whole, preferred_element_type=jnp.float32),
        "col",
        scatter_dimension=0,
        tiled=True,
    )
    return (amplitudes, gamma)


CHUNKS = 4
GROUPS = 4


def chunk_kernel(pieces, chunk, *refs):
    refs = list(refs)
    take = lambda count: [refs.pop(0) for _ in range(count)]
    ket = take(1 if chunk else 2 * len(pieces))
    bra, paired, crossed, handed, occ_ref, virt_ref = take(6)
    if chunk:
        take(2)
    whole_ref, half_ref, own_ref, pair_ref, far_ref, send_ref = take(6)
    if not chunk:
        (ket_all,) = take(1)
    kv, bv, bt, t2, amps, ket_sem, bra_sem, out_sem = refs
    width = bra.shape[3]
    span = ket[0].shape[1] // 2
    half = half_ref.shape[2]
    part = span // GROUPS
    batch = bra.shape[2]
    here_row, here_col = lax.axis_index("row"), lax.axis_index("col")
    me = lax.axis_index("occ")
    pair = lax.bitwise_xor(here_col, 1)
    low = here_col < 2
    middle = jnp.logical_or(here_col == 1, here_col == 2)

    def bra_copies(source, home, slot):
        return [
            pltpu.make_async_copy(
                source.at[q, i],
                bv.at[home, pl.ds(q * batch, batch), pl.ds(i * width, width)],
                bra_sem.at[slot, q, i],
            )
            for q in range(2)
            for i in range(2)
        ]

    for copy in bra_copies(bra, here_col, 0) + bra_copies(paired, pair, 1):
        copy.start()
    for n in range(2):
        home = jnp.where(low, 2 + n, 1 - n)

        @pl.when(middle)
        def _():
            for copy in bra_copies(crossed.at[n], home, 2 + n):
                copy.start()

        @pl.when(jnp.logical_not(middle))
        def _():
            for copy in bra_copies(handed.at[n], home, 2 + n):
                copy.start()

    copies = [[] for _ in range(GROUPS)]
    for group in range(GROUPS):
        for j in range(2):
            columns = pl.ds(j * span + group * part, part)
            if chunk:
                moves = [(ket[0], 0, 8 * batch, 0)]
            else:
                moves = []
                for n in range(2 * len(pieces)):
                    q, index = divmod(n, len(pieces))
                    offset, begin, rows = pieces[index]
                    home = lax.bitwise_xor(here_row, offset) * (2 * batch) + q * batch + begin
                    moves.append((ket[n], pl.multiple_of(home, 16), rows, n))
            for source, home, rows, n in moves:
                copy = pltpu.make_async_copy(
                    source.at[:, columns],
                    kv.at[pl.ds(home, rows), columns],
                    ket_sem.at[group, n, j],
                )
                copy.start()
                copies[group].append(copy)
    for slot in range(4):
        for copy in bra_copies(bra, slot, slot):
            copy.wait()
    first_at = here_row * (2 * half) + me * half + chunk * width
    first = virt_ref[:, pl.ds(pl.multiple_of(first_at, 128), width)]
    first = jnp.broadcast_to(first, (width, width)).T[:, :1]
    for d in range(4):
        bt[:, d * 2 * batch : (d + 1) * 2 * batch] = bv[d].T
    for group in range(GROUPS):
        for copy in copies[group]:
            copy.wait()
        tile = [
            jnp.dot(
                bt[...],
                kv[:, j * span + group * part : j * span + (group + 1) * part],
                preferred_element_type=jnp.float32,
            )
            for j in range(2)
        ]
        second_at = pl.multiple_of(here_col * span + group * part, 128)
        second = virt_ref[:, pl.ds(second_at, part)]
        for i in range(2):
            for j in range(2):
                direct = tile[j][i * width : (i + 1) * width, :]
                exchange = tile[i][j * width : (j + 1) * width, :]
                denominator = ((occ_ref[i] + occ_ref[j]) - first) - second
                block = ((2.0 * direct - exchange) / denominator).astype(jnp.bfloat16)
                amps[i, j, :, group * part : (group + 1) * part] = block
                t2[
                    i * width : (i + 1) * width,
                    j * span + group * part : j * span + (group + 1) * part,
                ] = block
    at = pl.multiple_of(me * half + chunk * width, 16)
    outs = [pltpu.make_async_copy(kv, ket_all, out_sem.at[2])] if not chunk else []
    outs += [
        pltpu.make_async_copy(amps, whole_ref.at[:, :, pl.ds(at, width), :], out_sem.at[0]),
        pltpu.make_async_copy(
            amps, half_ref.at[:, :, pl.ds(chunk * width, width), :], out_sem.at[1]
        ),
    ]
    for copy in outs:
        copy.start()

    def share_of(home):
        rows = pl.ds(pl.multiple_of(home * (2 * batch), 16), 2 * batch)
        return lax.dot_general(
            kv[rows, :],
            t2[...],
            (((1,), (1,)), ((), ())),
            preferred_element_type=jnp.float32,
        )

    for n in range(2):
        share = share_of(jnp.where(low, 2 + n, n))
        far_ref[n] = share
        send_ref[n] = share.astype(jnp.bfloat16)
    pair_ref[...] = share_of(pair)
    own_ref[...] = share_of(here_col)
    for copy in outs:
        copy.wait()


def run_chunk(chunk, ket, pieces, bras, energies, held):
    _, _, batch, width = bras[0].shape
    span = ket[0].shape[1] // 2
    half = width * CHUNKS
    total = 8 * batch
    flops = 2 * 2 * total * 2 * width * 2 * span
    ins = [*ket, *bras]
    any_space = pl.BlockSpec(memory_space=pl.ANY)
    in_vmem = pl.BlockSpec(memory_space=pltpu.VMEM)
    in_hbm = pl.BlockSpec(memory_space=pltpu.HBM)
    return pl.pallas_call(
        functools.partial(chunk_kernel, pieces, chunk),
        out_shape=(
            jax.ShapeDtypeStruct((2, 2, 2 * half, span), jnp.bfloat16),
            jax.ShapeDtypeStruct((2, 2, half, span), jnp.bfloat16),
            jax.ShapeDtypeStruct((2 * batch, 2 * width), jnp.float32),
            jax.ShapeDtypeStruct((2 * batch, 2 * width), jnp.float32),
            jax.ShapeDtypeStruct((2, 2 * batch, 2 * width), jnp.float32),
            jax.ShapeDtypeStruct((2, 2 * batch, 2 * width), jnp.bfloat16),
        )
        + (() if chunk else (jax.ShapeDtypeStruct((total, 2 * span), jnp.bfloat16),)),
        in_specs=[any_space] * len(ins)
        + [pl.BlockSpec(memory_space=pltpu.SMEM), in_vmem]
        + [any_space] * len(held),
        out_specs=(any_space, any_space, in_vmem, in_vmem, in_vmem, in_vmem)
        + (() if chunk else (in_hbm,)),
        scratch_shapes=[
            pltpu.VMEM((total, 2 * span), jnp.bfloat16),
            pltpu.VMEM((4, 2 * batch, 2 * width), jnp.bfloat16),
            pltpu.VMEM((2 * width, total), jnp.bfloat16),
            pltpu.VMEM((2 * width, 2 * span), jnp.bfloat16),
            pltpu.VMEM((2, 2, width, span), jnp.bfloat16),
            pltpu.SemaphoreType.DMA((GROUPS, 2 * len(pieces), 2)),
            pltpu.SemaphoreType.DMA((4, 2, 2)),
            pltpu.SemaphoreType.DMA((3,)),
        ],
        input_output_aliases={len(ins) + 2 + n: n for n in range(len(held))},
        compiler_params=pltpu.CompilerParams(vmem_limit_bytes=30 * 2**20),
        cost_estimate=pl.CostEstimate(
            flops=flops, bytes_accessed=total * 2 * span * 2, transcendentals=0
        ),
    )(*ins, *energies, *held)


def lay_kernel(bra, ket, ket_out, kept_out, given_out):
    span = ket.shape[2]
    half = bra.shape[2] // 2
    width = half // CHUNKS
    me = lax.axis_index("occ")
    for j in range(2):
        ket_out[:, j * span : (j + 1) * span] = ket[:, j, :]
    for side, out in ((1 - me, given_out), (me, kept_out)):
        for k in range(CHUNKS):
            columns = pl.ds(pl.multiple_of(side * half + k * width, 128), width)
            for i in range(2):
                out[k, i] = bra[:, i, columns]


def lay(bra, ket):
    batch, _, columns = bra.shape
    part = jax.ShapeDtypeStruct((CHUNKS, 2, batch, columns // 2 // CHUNKS), bra.dtype)
    return pl.pallas_call(
        lay_kernel,
        out_shape=(jax.ShapeDtypeStruct((batch, 2 * ket.shape[2]), ket.dtype), part, part),
        compiler_params=pltpu.CompilerParams(vmem_limit_bytes=24 * 2**20),
        cost_estimate=pl.CostEstimate(
            flops=0, bytes_accessed=4 * (bra.size + ket.size), transcendentals=0
        ),
    )(bra, ket)


def close_kernel(*refs):
    other, _, *totals = refs[: 2 + 2 * CHUNKS]
    amps, gamma, amp_buffer, gamma_buffer, sems, gamma_sems = refs[2 + 2 * CHUNKS :]
    half = other.shape[2]
    me = lax.axis_index("occ")
    batch, _, columns = gamma.shape
    width = columns // 2 // CHUNKS
    at = pl.multiple_of((1 - me) * half, 16)
    blocks = [(i, j) for i in range(2) for j in range(2)]
    reads = [
        pltpu.make_async_copy(other.at[i, j], amp_buffer.at[i, j], sems.at[0, i, j])
        for i, j in blocks
    ]
    writes = [
        pltpu.make_async_copy(
            amp_buffer.at[i, j], amps.at[i, j, pl.ds(at, half), :], sems.at[1, i, j]
        )
        for i, j in blocks
    ]
    for copy in reads:
        copy.start()
    for n in range(2 * CHUNKS):
        side, k = divmod(n, CHUNKS)
        home = jnp.where(me == side, 0, columns // 2) + k * width
        for i in range(2):
            gamma_buffer[n, :, i, :] = totals[n][:batch, i * width : (i + 1) * width]
        writes.append(
            pltpu.make_async_copy(
                gamma_buffer.at[n],
                gamma.at[:, :, pl.ds(pl.multiple_of(home, 128), width)],
                gamma_sems.at[n],
            )
        )
        if n < len(blocks):
            reads[n].wait()
            writes[n].start()
        writes[-1].start()
    for copy in writes:
        copy.wait()


def close(other, whole, kept, received):
    batch, double = received[0].shape
    any_space = pl.BlockSpec(memory_space=pl.ANY)
    in_vmem = pl.BlockSpec(memory_space=pltpu.VMEM)
    return pl.pallas_call(
        close_kernel,
        out_shape=(
            jax.ShapeDtypeStruct(whole.shape, whole.dtype),
            jax.ShapeDtypeStruct((batch, 2, CHUNKS * double), jnp.float32),
        ),
        in_specs=[any_space, any_space] + [in_vmem] * (2 * CHUNKS),
        out_specs=(any_space, any_space),
        scratch_shapes=[
            pltpu.VMEM(other.shape, other.dtype),
            pltpu.VMEM((2 * CHUNKS, batch, 2, double // 2), jnp.float32),
            pltpu.SemaphoreType.DMA((2, 2, 2)),
            pltpu.SemaphoreType.DMA((2 * CHUNKS,)),
        ],
        input_output_aliases={1: 0},
        compiler_params=pltpu.CompilerParams(vmem_limit_bytes=48 * 2**20),
        cost_estimate=pl.CostEstimate(
            flops=0, bytes_accessed=4 * other.size + 16 * batch * double * CHUNKS, transcendentals=0
        ),
    )(other, whole, *kept, *received)


def swap(x):
    return lax.ppermute(x, "occ", [(0, 1), (1, 0)])


def planar(x, offset):
    return lax.ppermute(x, "row", [(r, r ^ offset) for r in range(4)])


def pairs(x):
    return lax.ppermute(x, "col", [(0, 1), (1, 0), (2, 3), (3, 2)])


def across(x):
    return lax.ppermute(x, "col", [(1, 2), (2, 1)])


def outward(x):
    return lax.ppermute(x, "col", [(1, 0), (2, 3)])


def inward(x):
    return lax.ppermute(x, "col", [(0, 1), (3, 2)])


def tie(*arrays):
    return lax.optimization_barrier(arrays)


def planned(bra_factor, ket_factor, occ_energy, virt_energy):
    batch, _, a_width = bra_factor.shape
    b_width = ket_factor.shape[2]
    half = a_width // 2
    width = half // CHUNKS
    me, row_index, col_index = (lax.axis_index(name) for name in ("occ", "row", "col"))

    ket_own, bra_kept, bra_given = lay(bra_factor, ket_factor)
    ket_x = planar(ket_own, 1)
    ket_y = planar(ket_own, 2)
    cut = batch // 2
    pieces = ((0, 0, batch), (1, 0, batch), (2, 0, batch), (3, 0, cut), (3, cut, batch - cut))

    bra = jnp.stack([bra_kept, swap(bra_given)], axis=1)
    paired_first, paired_some = pairs(bra[0]), pairs(bra[1:3])
    crossed_first = across(jnp.stack([bra[0], paired_first]))
    ket_swapped = swap(ket_own)
    ket_x, ket_y, crossed_first, paired_some, ket_swapped = tie(ket_x, ket_y, crossed_first, paired_some, ket_swapped)
    part_x, part_y, late_x, late_y = tie(ket_x[:cut], ket_y[cut:], ket_x, ket_y)
    ket_far_y, ket_far_x = planar(part_x, 2), planar(part_y, 1)
    straight = swap(jnp.stack([late_x, late_y]))
    mine = [ket_own, ket_x, ket_y, ket_far_y, ket_far_x]
    ket = mine + [ket_swapped, straight[0], straight[1], swap(ket_far_y), swap(ket_far_x)]
    handed_first, bra_last = tie(outward(crossed_first), bra[3])
    paired = [paired_first, paired_some[0], paired_some[1], pairs(bra_last)]
    crossed = [crossed_first]
    crossed += [across(jnp.stack([bra[k], paired[k]])) for k in range(1, CHUNKS)]
    energies = (occ_energy, virt_energy[None, :])

    def up_cast(x):
        return x.astype(jnp.float32)

    near = lax.bitwise_and(col_index, 1)
    held = ()
    own, pair, far, one, two, three, kept, received = ({} for _ in range(8))

    def cross(k):
        two[k] = across((far[k] + up_cast(one[k])).astype(jnp.bfloat16))

    def exchange(k):
        theirs = lax.dynamic_index_in_dim(two[k], 1 - near, 0, keepdims=False)
        three[k] = pairs((pair[k] + up_cast(theirs)).astype(jnp.bfloat16))

    def finish(k):
        ours = lax.dynamic_index_in_dim(two[k], near, 0, keepdims=False)
        total = own[k] + up_cast(ours) + up_cast(three[k])
        kept[k] = total[:batch]
        received[k] = swap(total[batch:])

    for tick in range(CHUNKS + 3):
        if tick < CHUNKS:
            k = tick
            blocks = [bra[k], paired[k], crossed[k]]
            blocks.append(outward(crossed[k]) if k else handed_first)
            if k >= 2:
                one[k - 2], blocks[0] = tie(one[k - 2], blocks[0])
            if k >= 3:
                two[k - 3], blocks[0] = tie(two[k - 3], blocks[0])
            results = run_chunk(k, ket, pieces, blocks, energies, held)
            held = results[:2]
            own[k], pair[k], far[k], send = results[2:6]
            if k == 0:
                ket = [results[6]]
            one[k] = inward(send)
        if 1 <= tick <= CHUNKS:
            cross(tick - 1)
    last = CHUNKS - 1
    one[last], two[1] = tie(one[last], two[1])
    for k in range(CHUNKS):
        exchange(k)
        finish(k)
    every = range(CHUNKS)
    return close(swap(held[1]), held[0], [kept[k] for k in every], [received[k] for k in every])


def solution(mesh):
    sizes = mesh.shape

    def on_device(bra_factor, ket_factor, occ_energy, virt_energy):
        fits = (
            sizes["occ"] == 2
            and sizes["row"] == 4
            and sizes["col"] == 4
            and bra_factor.shape[2] % (256 * CHUNKS) == 0
            and ket_factor.shape[2] % 512 == 0
            and bra_factor.shape[0] % 128 == 0
        )
        body = planned if fits else general
        return body(bra_factor, ket_factor, occ_energy, virt_energy)

    placed = (P(("occ", "col"), None, "row"), P(("occ", "row"), None, "col"), P(), P())
    return jax.shard_map(
        on_device,
        mesh=mesh,
        in_specs=placed,
        out_specs=(P(None, None, "row", "col"), P(("occ", "col"), None, "row")),
        check_vma=False,
    )
```

```python
import functools

import jax
import jax.numpy as jnp
from jax import lax
from jax.experimental import pallas as pl
from jax.experimental.pallas import tpu as pltpu
from jax.sharding import PartitionSpec as P


def make_amplitudes(coulomb, occ_energy, virt_first, virt_second):
    denominator = (
        occ_energy[:, None, None, None]
        + occ_energy[None, :, None, None]
        - virt_first[None, None, :, None]
        - virt_second[None, None, None, :]
    )
    return ((2.0 * coulomb - jnp.transpose(coulomb, (1, 0, 2, 3))) / denominator).astype(
        jnp.bfloat16
    )


def general(bra_factor, ket_factor, occ_energy, virt_energy):
    a_width = bra_factor.shape[2]
    b_width = ket_factor.shape[2]
    ket_whole = lax.all_gather(ket_factor, "row", axis=0, tiled=True)
    row_index = lax.axis_index("row")
    col_index = lax.axis_index("col")
    virt_first = lax.dynamic_slice_in_dim(virt_energy, row_index * a_width, a_width, 0)
    virt_second = lax.dynamic_slice_in_dim(virt_energy, col_index * b_width, b_width, 0)
    partial_sum = jnp.einsum(
        "qia,qjb->ijab",
        lax.all_gather(bra_factor, "col", axis=0, tiled=True),
        ket_whole,
        preferred_element_type=jnp.float32,
    )
    batch_count = lax.axis_size("occ")
    pad_rows = (batch_count - a_width % batch_count) % batch_count
    padded = jnp.pad(partial_sum, ((0, 0), (0, 0), (0, pad_rows), (0, 0)))
    share_sum = lax.psum_scatter(padded, "occ", scatter_dimension=2, tiled=True)
    share_len = share_sum.shape[2]
    energy_padded = jnp.pad(virt_first, (0, pad_rows), constant_values=1.0)
    energy_share = lax.dynamic_slice_in_dim(
        energy_padded, lax.axis_index("occ") * share_len, share_len, 0
    )
    share_amps = make_amplitudes(share_sum, occ_energy, energy_share, virt_second)
    collected = lax.all_gather(share_amps, "occ", axis=2, tiled=True)
    amplitudes = collected[:, :, :a_width, :]
    gamma = lax.psum_scatter(
        jnp.einsum("ijab,qjb->qia", amplitudes, ket_whole, preferred_element_type=jnp.float32),
        "col",
        scatter_dimension=0,
        tiled=True,
    )
    return (amplitudes, gamma)


CHUNKS = 4
TOGETHER = 2
GROUPS = 4


def chunk_kernel(pieces, chunk, *refs):
    refs = list(refs)
    take = lambda count: [refs.pop(0) for _ in range(count)]
    ket = take(1 if chunk else 2 * len(pieces))
    (bra,) = take(1)
    ups, downs = take(3), take(3)
    occ_ref, virt_ref = take(2)
    if chunk:
        take(2)
    whole_ref, half_ref, own_ref, pair_ref, far_ref, send_ref = take(6)
    if not chunk:
        (ket_all,) = take(1)
    kv, bv, bt, t2, amps, ket_sem, bra_sem, out_sem = refs
    width = bra.shape[3]
    span = ket[0].shape[1] // 2
    half = half_ref.shape[2]
    part = span // GROUPS
    batch = bra.shape[2]
    here_row, here_col = lax.axis_index("row"), lax.axis_index("col")
    me = lax.axis_index("occ")
    pair = lax.bitwise_xor(here_col, 1)
    low = here_col < 2
    middle = jnp.logical_or(here_col == 1, here_col == 2)

    def bra_copies(source, home, slot):
        return [
            pltpu.make_async_copy(
                source.at[q, i],
                bv.at[home, pl.ds(q * batch, batch), pl.ds(i * width, width)],
                bra_sem.at[slot, q, i],
            )
            for q in range(2)
            for i in range(2)
        ]

    def fetch(condition, source, home, slot):
        @pl.when(condition)
        def _():
            for copy in bra_copies(source, home, slot):
                copy.start()

    for copy in bra_copies(bra, here_col, 0):
        copy.start()
    place = chunk % TOGETHER
    for d in range(1, 4):
        home = lax.rem(here_col + 4 - d, 4)
        fetch(here_col >= d, ups[d - 1].at[place], home, d)
        fetch(here_col < d, downs[3 - d].at[place], home, d)

    copies = [[] for _ in range(GROUPS)]
    for group in range(GROUPS):
        for j in range(2):
            columns = pl.ds(j * span + group * part, part)
            if chunk:
                moves = [(ket[0], 0, 8 * batch, 0)]
            else:
                moves = []
                for n in range(2 * len(pieces)):
                    q, index = divmod(n, len(pieces))
                    offset, begin, rows = pieces[index]
                    home = lax.bitwise_xor(here_row, offset) * (2 * batch) + q * batch + begin
                    moves.append((ket[n], pl.multiple_of(home, 16), rows, n))
            for source, home, rows, n in moves:
                copy = pltpu.make_async_copy(
                    source.at[:, columns],
                    kv.at[pl.ds(home, rows), columns],
                    ket_sem.at[group, n, j],
                )
                copy.start()
                copies[group].append(copy)
    for slot in range(4):
        for copy in bra_copies(bra, slot, slot):
            copy.wait()
    first_at = here_row * (2 * half) + me * half + chunk * width
    first = virt_ref[:, pl.ds(pl.multiple_of(first_at, 128), width)]
    first = jnp.broadcast_to(first, (width, width)).T[:, :1]
    for d in range(4):
        bt[:, d * 2 * batch : (d + 1) * 2 * batch] = bv[d].T
    for group in range(GROUPS):
        for copy in copies[group]:
            copy.wait()
        tile = [
            jnp.dot(
                bt[...],
                kv[:, j * span + group * part : j * span + (group + 1) * part],
                preferred_element_type=jnp.float32,
            )
            for j in range(2)
        ]
        second_at = pl.multiple_of(here_col * span + group * part, 128)
        second = virt_ref[:, pl.ds(second_at, part)]
        for i in range(2):
            for j in range(2):
                direct = tile[j][i * width : (i + 1) * width, :]
                exchange = tile[i][j * width : (j + 1) * width, :]
                denominator = ((occ_ref[i] + occ_ref[j]) - first) - second
                block = ((2.0 * direct - exchange) / denominator).astype(jnp.bfloat16)
                amps[i, j, :, group * part : (group + 1) * part] = block
                t2[
                    i * width : (i + 1) * width,
                    j * span + group * part : j * span + (group + 1) * part,
                ] = block
    at = pl.multiple_of(me * half + chunk * width, 16)
    outs = [pltpu.make_async_copy(kv, ket_all, out_sem.at[2])] if not chunk else []
    outs += [
        pltpu.make_async_copy(amps, whole_ref.at[:, :, pl.ds(at, width), :], out_sem.at[0]),
        pltpu.make_async_copy(
            amps, half_ref.at[:, :, pl.ds(chunk * width, width), :], out_sem.at[1]
        ),
    ]
    for copy in outs:
        copy.start()

    def share_of(home):
        rows = pl.ds(pl.multiple_of(home * (2 * batch), 16), 2 * batch)
        return lax.dot_general(
            kv[rows, :],
            t2[...],
            (((1,), (1,)), ((), ())),
            preferred_element_type=jnp.float32,
        )

    for n in range(2):
        share = share_of(jnp.where(low, 2 + n, n))
        far_ref[n] = share
        send_ref[n] = share.astype(jnp.bfloat16)
    pair_ref[...] = share_of(pair)
    own_ref[...] = share_of(here_col)
    for copy in outs:
        copy.wait()


def run_chunk(chunk, ket, pieces, bras, energies, held):
    _, _, batch, width = bras[0].shape
    span = ket[0].shape[1] // 2
    half = width * CHUNKS
    total = 8 * batch
    flops = 2 * 2 * total * 2 * width * 2 * span
    ins = [*ket, *bras]
    any_space = pl.BlockSpec(memory_space=pl.ANY)
    in_vmem = pl.BlockSpec(memory_space=pltpu.VMEM)
    in_hbm = pl.BlockSpec(memory_space=pltpu.HBM)
    return pl.pallas_call(
        functools.partial(chunk_kernel, pieces, chunk),
        out_shape=(
            jax.ShapeDtypeStruct((2, 2, 2 * half, span), jnp.bfloat16),
            jax.ShapeDtypeStruct((2, 2, half, span), jnp.bfloat16),
            jax.ShapeDtypeStruct((2 * batch, 2 * width), jnp.float32),
            jax.ShapeDtypeStruct((2 * batch, 2 * width), jnp.float32),
            jax.ShapeDtypeStruct((2, 2 * batch, 2 * width), jnp.float32),
            jax.ShapeDtypeStruct((2, 2 * batch, 2 * width), jnp.bfloat16),
        )
        + (() if chunk else (jax.ShapeDtypeStruct((total, 2 * span), jnp.bfloat16),)),
        in_specs=[in_hbm if chunk else any_space] * len(ket)
        + [any_space] * len(bras)
        + [pl.BlockSpec(memory_space=pltpu.SMEM), in_vmem]
        + [any_space] * len(held),
        out_specs=(any_space, any_space, in_vmem, in_vmem, in_vmem, in_vmem)
        + (() if chunk else (in_hbm,)),
        scratch_shapes=[
            pltpu.VMEM((total, 2 * span), jnp.bfloat16),
            pltpu.VMEM((4, 2 * batch, 2 * width), jnp.bfloat16),
            pltpu.VMEM((2 * width, total), jnp.bfloat16),
            pltpu.VMEM((2 * width, 2 * span), jnp.bfloat16),
            pltpu.VMEM((2, 2, width, span), jnp.bfloat16),
            pltpu.SemaphoreType.DMA((GROUPS, 2 * len(pieces), 2)),
            pltpu.SemaphoreType.DMA((4, 2, 2)),
            pltpu.SemaphoreType.DMA((3,)),
        ],
        input_output_aliases={len(ins) + 2 + n: n for n in range(len(held))},
        compiler_params=pltpu.CompilerParams(vmem_limit_bytes=30 * 2**20),
        cost_estimate=pl.CostEstimate(
            flops=flops, bytes_accessed=total * 2 * span * 2, transcendentals=0
        ),
    )(*ins, *energies, *held)


def pick_kernel(bra, kept_out, given_out):
    _, _, _, width = kept_out.shape
    span = bra.shape[1] // 2
    me = lax.axis_index("occ")
    for side, out in ((1 - me, given_out), (me, kept_out)):
        for k in range(CHUNKS):
            for i in range(2):
                home = i * span + side * (span // 2) + k * width
                out[k, i] = bra[:, pl.ds(pl.multiple_of(home, 128), width)]


def pick(bra):
    batch, columns = bra.shape
    part = jax.ShapeDtypeStruct((CHUNKS, 2, batch, columns // 4 // CHUNKS), bra.dtype)
    return pl.pallas_call(
        pick_kernel,
        out_shape=(part, part),
        compiler_params=pltpu.CompilerParams(vmem_limit_bytes=16 * 2**20),
        cost_estimate=pl.CostEstimate(
            flops=0, bytes_accessed=4 * bra.size, transcendentals=0
        ),
    )(bra)


def close_kernel(*refs):
    other, _, *totals = refs[: 2 + 2 * CHUNKS]
    amps, gamma, amp_buffer, gamma_buffer, sems, gamma_sems = refs[2 + 2 * CHUNKS :]
    half = other.shape[2]
    me = lax.axis_index("occ")
    batch, _, columns = gamma.shape
    width = columns // 2 // CHUNKS
    at = pl.multiple_of((1 - me) * half, 16)
    blocks = [(i, j) for i in range(2) for j in range(2)]
    reads = [
        pltpu.make_async_copy(other.at[i, j], amp_buffer.at[i, j], sems.at[0, i, j])
        for i, j in blocks
    ]
    writes = [
        pltpu.make_async_copy(
            amp_buffer.at[i, j], amps.at[i, j, pl.ds(at, half), :], sems.at[1, i, j]
        )
        for i, j in blocks
    ]
    for copy in reads:
        copy.start()
    for n in range(2 * CHUNKS):
        side, k = divmod(n, CHUNKS)
        home = jnp.where(me == side, 0, columns // 2) + k * width
        for i in range(2):
            gamma_buffer[n, :, i, :] = totals[n][:batch, i * width : (i + 1) * width]
        writes.append(
            pltpu.make_async_copy(
                gamma_buffer.at[n],
                gamma.at[:, :, pl.ds(pl.multiple_of(home, 128), width)],
                gamma_sems.at[n],
            )
        )
        if n < len(blocks):
            reads[n].wait()
            writes[n].start()
        writes[-1].start()
    for copy in writes:
        copy.wait()


def close(other, whole, kept, received):
    batch, double = received[0].shape
    any_space = pl.BlockSpec(memory_space=pl.ANY)
    in_vmem = pl.BlockSpec(memory_space=pltpu.VMEM)
    return pl.pallas_call(
        close_kernel,
        out_shape=(
            jax.ShapeDtypeStruct(whole.shape, whole.dtype),
            jax.ShapeDtypeStruct((batch, 2, CHUNKS * double), jnp.float32),
        ),
        in_specs=[any_space, any_space] + [in_vmem] * (2 * CHUNKS),
        out_specs=(any_space, any_space),
        scratch_shapes=[
            pltpu.VMEM(other.shape, other.dtype),
            pltpu.VMEM((2 * CHUNKS, batch, 2, double // 2), jnp.float32),
            pltpu.SemaphoreType.DMA((2, 2, 2)),
            pltpu.SemaphoreType.DMA((2 * CHUNKS,)),
        ],
        input_output_aliases={1: 0},
        compiler_params=pltpu.CompilerParams(vmem_limit_bytes=48 * 2**20),
        cost_estimate=pl.CostEstimate(
            flops=0, bytes_accessed=4 * other.size + 16 * batch * double * CHUNKS, transcendentals=0
        ),
    )(other, whole, *kept, *received)


def swap(x):
    return lax.ppermute(x, "occ", [(0, 1), (1, 0)])


def planar(x, offset):
    return lax.ppermute(x, "row", [(r, r ^ offset) for r in range(4)])


def hop_up(x, first):
    return lax.ppermute(x, "col", [(c, c + 1) for c in range(first, 3)])


def hop_down(x, first):
    return lax.ppermute(x, "col", [(3 - c, 2 - c) for c in range(first, 3)])


def pairs(x):
    return lax.ppermute(x, "col", [(0, 1), (1, 0), (2, 3), (3, 2)])


def across(x):
    return lax.ppermute(x, "col", [(1, 2), (2, 1)])


def outward(x):
    return lax.ppermute(x, "col", [(1, 0), (2, 3)])


def inward(x):
    return lax.ppermute(x, "col", [(0, 1), (3, 2)])


def tie(*arrays):
    return lax.optimization_barrier(arrays)


def planned(bra_factor, ket_factor, occ_energy, virt_energy):
    batch, _, a_width = bra_factor.shape
    b_width = ket_factor.shape[2]
    half = a_width // 2
    width = half // CHUNKS
    me, row_index, col_index = (lax.axis_index(name) for name in ("occ", "row", "col"))

    bra_kept, bra_given = pick(bra_factor.reshape(batch, 2 * a_width))
    ket_own = ket_factor.reshape(batch, 2 * b_width)
    bra = jnp.stack([bra_kept, swap(bra_given)], axis=1)
    ket_x = planar(ket_own, 1)
    ket_y = planar(ket_own, 2)
    cut = batch // 2
    pieces = ((0, 0, batch), (1, 0, batch), (2, 0, batch), (3, 0, cut), (3, cut, batch - cut))

    blocks = [bra[:TOGETHER], bra[TOGETHER:]]
    ups, downs = [[hop_up(blocks[0], 0)], []], [[hop_down(blocks[0], 0)], []]
    ket_swapped = swap(ket_own)
    ups[0].append(hop_up(ups[0][0], 1))
    downs[0].append(hop_down(downs[0][0], 1))
    ket_x, ket_y, ups[0][1], downs[0][1], ket_swapped = tie(
        ket_x, ket_y, ups[0][1], downs[0][1], ket_swapped
    )
    part_x, part_y, late_x, late_y = tie(ket_x[:cut], ket_y[cut:], ket_x, ket_y)
    ket_far_y, ket_far_x = planar(part_x, 2), planar(part_y, 1)
    ups[0].append(hop_up(ups[0][1], 2))
    downs[0].append(hop_down(downs[0][1], 2))
    mine = [ket_own, ket_x, ket_y]
    ket = [ket_swapped, swap(late_x), swap(late_y)]
    ups[0][2], downs[0][2], *far_pieces = tie(ups[0][2], downs[0][2], ket_far_y, ket_far_x)
    ket = mine + far_pieces + ket + [swap(piece) for piece in far_pieces]
    ups[0][2], downs[0][2], block = tie(ups[0][2], downs[0][2], blocks[1])
    ups[1].append(hop_up(block, 0))
    downs[1].append(hop_down(block, 0))
    energies = (occ_energy, virt_energy[None, :])

    def up_cast(x):
        return x.astype(jnp.float32)

    near = lax.bitwise_and(col_index, 1)
    held = ()
    own, pair, far, one, two, three, kept, received = ({} for _ in range(8))

    def cross(k):
        two[k] = across((far[k] + up_cast(one[k])).astype(jnp.bfloat16))

    def exchange(k):
        theirs = lax.dynamic_index_in_dim(two[k], 1 - near, 0, keepdims=False)
        three[k] = pairs((pair[k] + up_cast(theirs)).astype(jnp.bfloat16))

    def finish(k):
        ours = lax.dynamic_index_in_dim(two[k], near, 0, keepdims=False)
        total = own[k] + up_cast(ours) + up_cast(three[k])
        kept[k] = total[:batch]
        received[k] = swap(total[batch:])

    for tick in range(CHUNKS + 3):
        if tick < CHUNKS:
            k = tick
            group = k // TOGETHER
            arrived = [bra[k], *ups[group], *downs[group]]
            if k >= 2:
                one[k - 2], arrived[0] = tie(one[k - 2], arrived[0])
            if k >= 3:
                exchange(k - 3)
                three[k - 3], arrived[0] = tie(three[k - 3], arrived[0])
            results = run_chunk(k, ket, pieces, arrived, energies, held)
            held = results[:2]
            own[k], pair[k], far[k], send = results[2:6]
            if k == 0:
                ket = [results[6]]
            one[k] = inward(send)
            if k < 2:
                own[k], up, down = tie(own[k], ups[1][k], downs[1][k])
                ups[1].append(hop_up(up, k + 1))
                downs[1].append(hop_down(down, k + 1))
            if k == 1:
                far[0], own[1] = tie(far[0], own[1])
        if 1 <= tick <= CHUNKS:
            cross(tick - 1)
    last = CHUNKS - 1
    one[last], two[1] = tie(one[last], two[1])
    for k in range(1, CHUNKS):
        exchange(k)
    for k in range(CHUNKS):
        finish(k)
    every = range(CHUNKS)
    return close(swap(held[1]), held[0], [kept[k] for k in every], [received[k] for k in every])


def solution(mesh):
    sizes = mesh.shape

    def on_device(bra_factor, ket_factor, occ_energy, virt_energy):
        fits = (
            sizes["occ"] == 2
            and sizes["row"] == 4
            and sizes["col"] == 4
            and bra_factor.shape[2] % (256 * CHUNKS) == 0
            and ket_factor.shape[2] % 512 == 0
            and bra_factor.shape[0] % 128 == 0
        )
        body = planned if fits else general
        return body(bra_factor, ket_factor, occ_energy, virt_energy)

    placed = (P(("occ", "col"), None, "row"), P(("occ", "row"), None, "col"), P(), P())
    return jax.shard_map(
        on_device,
        mesh=mesh,
        in_specs=placed,
        out_specs=(P(None, None, "row", "col"), P(("occ", "col"), None, "row")),
        check_vma=False,
    )
```

```python
import functools

import jax
import jax.numpy as jnp
from jax import lax
from jax.experimental import pallas as pl
from jax.experimental.pallas import tpu as pltpu
from jax.sharding import PartitionSpec as P


def make_amplitudes(coulomb, occ_energy, virt_first, virt_second):
    denominator = (
        occ_energy[:, None, None, None]
        + occ_energy[None, :, None, None]
        - virt_first[None, None, :, None]
        - virt_second[None, None, None, :]
    )
    return ((2.0 * coulomb - jnp.transpose(coulomb, (1, 0, 2, 3))) / denominator).astype(
        jnp.bfloat16
    )


def general(bra_factor, ket_factor, occ_energy, virt_energy):
    a_width = bra_factor.shape[2]
    b_width = ket_factor.shape[2]
    ket_whole = lax.all_gather(ket_factor, "row", axis=0, tiled=True)
    row_index = lax.axis_index("row")
    col_index = lax.axis_index("col")
    virt_first = lax.dynamic_slice_in_dim(virt_energy, row_index * a_width, a_width, 0)
    virt_second = lax.dynamic_slice_in_dim(virt_energy, col_index * b_width, b_width, 0)
    partial_sum = jnp.einsum(
        "qia,qjb->ijab",
        lax.all_gather(bra_factor, "col", axis=0, tiled=True),
        ket_whole,
        preferred_element_type=jnp.float32,
    )
    batch_count = lax.axis_size("occ")
    pad_rows = (batch_count - a_width % batch_count) % batch_count
    padded = jnp.pad(partial_sum, ((0, 0), (0, 0), (0, pad_rows), (0, 0)))
    share_sum = lax.psum_scatter(padded, "occ", scatter_dimension=2, tiled=True)
    share_len = share_sum.shape[2]
    energy_padded = jnp.pad(virt_first, (0, pad_rows), constant_values=1.0)
    energy_share = lax.dynamic_slice_in_dim(
        energy_padded, lax.axis_index("occ") * share_len, share_len, 0
    )
    share_amps = make_amplitudes(share_sum, occ_energy, energy_share, virt_second)
    collected = lax.all_gather(share_amps, "occ", axis=2, tiled=True)
    amplitudes = collected[:, :, :a_width, :]
    gamma = lax.psum_scatter(
        jnp.einsum("ijab,qjb->qia", amplitudes, ket_whole, preferred_element_type=jnp.float32),
        "col",
        scatter_dimension=0,
        tiled=True,
    )
    return (amplitudes, gamma)


GROUPS = 2
SLICES = 4


def group_kernel(pieces, group, *refs):
    refs = list(refs)
    take = lambda count: [refs.pop(0) for _ in range(count)]
    ket = take(1 if group else 2 * len(pieces))
    (bra,) = take(1)
    ups, downs = take(3), take(3)
    occ_ref, virt_ref = take(2)
    other, _ = take(2) if group else (None, None)
    whole_ref, half_ref = take(2)
    own_ref, pair_ref, far_ref, send_ref = (take(2) for _ in range(4))
    (ket_all,) = (None,) if group else take(1)
    kv, bv, bt, t2, amps, given, ket_sem, bra_sem, out_sem = refs
    batch, width = bra.shape[2:]
    span = ket[0].shape[1] // 2
    half = whole_ref.shape[2] // 2
    part = span // SLICES
    here_row, here_col = lax.axis_index("row"), lax.axis_index("col")
    me = lax.axis_index("occ")
    pair = lax.bitwise_xor(here_col, 1)
    low = here_col < 2

    def bra_copies(source, home, slot):
        return [
            pltpu.make_async_copy(
                source.at[q, i],
                bv.at[home, pl.ds(q * batch, batch), pl.ds(i * width, width)],
                bra_sem.at[slot, q, i],
            )
            for q in range(2)
            for i in range(2)
        ]

    def fetch(condition, source, home, slot):
        @pl.when(condition)
        def _():
            for copy in bra_copies(source, home, slot):
                copy.start()

    for copy in bra_copies(bra, here_col, 0):
        copy.start()
    for d in range(1, 4):
        home = lax.rem(here_col + 4 - d, 4)
        fetch(here_col >= d, ups[d - 1], home, d)
        fetch(here_col < d, downs[3 - d], home, d)

    copies = [[] for _ in range(SLICES)]
    for n in range(SLICES):
        for j in range(2):
            columns = pl.ds(j * span + n * part, part)
            if group:
                moves = [(ket[0], 0, 8 * batch, 0)]
            else:
                moves = []
                for index, source in enumerate(ket):
                    q, place = divmod(index, len(pieces))
                    offset, begin, rows = pieces[place]
                    home = lax.bitwise_xor(here_row, offset) * (2 * batch) + q * batch + begin
                    moves.append((source, pl.multiple_of(home, 16), rows, index))
            for source, home, rows, index in moves:
                copy = pltpu.make_async_copy(
                    source.at[:, columns],
                    kv.at[pl.ds(home, rows), columns],
                    ket_sem.at[n, index, j],
                )
                copy.start()
                copies[n].append(copy)
    if group:
        given_in = pltpu.make_async_copy(other, given, out_sem.at[2])
        given_in.start()
    for slot in range(4):
        for copy in bra_copies(bra, slot, slot):
            copy.wait()
    first_at = here_row * (2 * half) + me * half + group * width
    first = virt_ref[:, pl.ds(pl.multiple_of(first_at, 128), width)]
    first = jnp.broadcast_to(first, (width, width)).T[:, :1]
    for d in range(4):
        bt[:, d * 2 * batch : (d + 1) * 2 * batch] = bv[d].T
    for n in range(SLICES):
        for copy in copies[n]:
            copy.wait()
        tile = [
            jnp.dot(
                bt[...],
                kv[:, j * span + n * part : j * span + (n + 1) * part],
                preferred_element_type=jnp.float32,
            )
            for j in range(2)
        ]
        second_at = pl.multiple_of(here_col * span + n * part, 128)
        second = virt_ref[:, pl.ds(second_at, part)]
        for i in range(2):
            for j in range(2):
                direct = tile[j][i * width : (i + 1) * width, :]
                exchange = tile[i][j * width : (j + 1) * width, :]
                denominator = ((occ_ref[i] + occ_ref[j]) - first) - second
                block = ((2.0 * direct - exchange) / denominator).astype(jnp.bfloat16)
                amps[i, j, :, n * part : (n + 1) * part] = block
                t2[
                    i * width : (i + 1) * width,
                    j * span + n * part : j * span + (n + 1) * part,
                ] = block
    at = pl.multiple_of(me * half + group * width, 16)
    outs = [
        pltpu.make_async_copy(amps, whole_ref.at[:, :, pl.ds(at, width), :], out_sem.at[0]),
        pltpu.make_async_copy(amps, half_ref, out_sem.at[1]),
    ]
    if group:
        given_in.wait()
        at = pl.multiple_of((1 - me) * half, 16)
        outs.append(
            pltpu.make_async_copy(given, whole_ref.at[:, :, pl.ds(at, width), :], out_sem.at[2])
        )
    else:
        outs.append(pltpu.make_async_copy(kv, ket_all, out_sem.at[2]))
    for copy in outs:
        copy.start()

    def share_of(home):
        rows = pl.ds(pl.multiple_of(home * (2 * batch), 16), 2 * batch)
        return lax.dot_general(
            kv[rows, :],
            t2[...],
            (((1,), (1,)), ((), ())),
            preferred_element_type=jnp.float32,
        )

    for n in range(2):
        share = share_of(jnp.where(low, 2 + n, n))
        for q in range(2):
            far_ref[q][n] = share[q * batch : (q + 1) * batch]
            send_ref[q][n] = share[q * batch : (q + 1) * batch].astype(jnp.bfloat16)
    for out, home in ((pair_ref, pair), (own_ref, here_col)):
        share = share_of(home)
        for q in range(2):
            out[q][...] = share[q * batch : (q + 1) * batch]
    for copy in outs:
        copy.wait()


def run_group(group, ket, pieces, bras, energies, held):
    _, _, batch, width = bras[0].shape
    span = ket[0].shape[1] // 2
    half = width * GROUPS
    total = 8 * batch
    flops = 2 * 2 * total * 2 * width * 2 * span
    any_space = pl.BlockSpec(memory_space=pl.ANY)
    in_vmem = pl.BlockSpec(memory_space=pltpu.VMEM)
    in_hbm = pl.BlockSpec(memory_space=pltpu.HBM)
    ahead = len(ket) + len(bras) + 2
    block = jax.ShapeDtypeStruct((batch, 2 * width), jnp.float32)
    far = jax.ShapeDtypeStruct((2, batch, 2 * width), jnp.float32)
    send = jax.ShapeDtypeStruct((2, batch, 2 * width), jnp.bfloat16)
    results = pl.pallas_call(
        functools.partial(group_kernel, pieces, group),
        out_shape=(
            jax.ShapeDtypeStruct((2, 2, 2 * half, span), jnp.bfloat16),
            jax.ShapeDtypeStruct((2, 2, width, span), jnp.bfloat16),
        )
        + (block,) * 4
        + (far,) * 2
        + (send,) * 2
        + (() if group else (jax.ShapeDtypeStruct((total, 2 * span), jnp.bfloat16),)),
        in_specs=[in_hbm if group else any_space] * len(ket)
        + [any_space] * len(bras)
        + [pl.BlockSpec(memory_space=pltpu.SMEM), in_vmem]
        + [any_space] * len(held),
        out_specs=(any_space, any_space) + (in_vmem,) * 8 + (() if group else (in_hbm,)),
        scratch_shapes=[
            pltpu.VMEM((total, 2 * span), jnp.bfloat16),
            pltpu.VMEM((4, 2 * batch, 2 * width), jnp.bfloat16),
            pltpu.VMEM((2 * width, total), jnp.bfloat16),
            pltpu.VMEM((2 * width, 2 * span), jnp.bfloat16),
            pltpu.VMEM((2, 2, width, span), jnp.bfloat16),
            pltpu.VMEM((2, 2, width, span), jnp.bfloat16),
            pltpu.SemaphoreType.DMA((SLICES, 2 * len(pieces), 2)),
            pltpu.SemaphoreType.DMA((4, 2, 2)),
            pltpu.SemaphoreType.DMA((3,)),
        ],
        input_output_aliases={ahead + 1: 0} if held else {},
        compiler_params=pltpu.CompilerParams(vmem_limit_bytes=44 * 2**20),
        cost_estimate=pl.CostEstimate(
            flops=flops, bytes_accessed=total * 2 * span * 2, transcendentals=0
        ),
    )(*ket, *bras, *energies, *held)
    return results[:2], *(results[n : n + 2] for n in (2, 4, 6, 8)), results[10:]


def pick_kernel(bra, kept_out, given_out):
    width = kept_out.shape[3]
    span = bra.shape[1] // 2
    me = lax.axis_index("occ")
    for side, out in ((1 - me, given_out), (me, kept_out)):
        for g in range(GROUPS):
            for i in range(2):
                home = i * span + side * (span // 2) + g * width
                out[g, i] = bra[:, pl.ds(pl.multiple_of(home, 128), width)]


def pick(bra):
    batch, columns = bra.shape
    part = jax.ShapeDtypeStruct((GROUPS, 2, batch, columns // 4 // GROUPS), bra.dtype)
    return pl.pallas_call(
        pick_kernel,
        out_shape=(part, part),
        compiler_params=pltpu.CompilerParams(vmem_limit_bytes=16 * 2**20),
        cost_estimate=pl.CostEstimate(
            flops=0, bytes_accessed=4 * bra.size, transcendentals=0
        ),
    )(bra)


def close_kernel(*refs):
    other, _, *totals = refs[: 2 + 2 * GROUPS]
    amps, gamma, amp_buffer, gamma_buffer, sems, gamma_sems = refs[2 + 2 * GROUPS :]
    width = other.shape[2]
    half = width * GROUPS
    me = lax.axis_index("occ")
    at = pl.multiple_of((1 - me) * half + half - width, 16)
    blocks = [(i, j) for i in range(2) for j in range(2)]
    reads = [
        pltpu.make_async_copy(other.at[i, j], amp_buffer.at[i, j], sems.at[0, i, j])
        for i, j in blocks
    ]
    writes = [
        pltpu.make_async_copy(
            amp_buffer.at[i, j], amps.at[i, j, pl.ds(at, width), :], sems.at[1, i, j]
        )
        for i, j in blocks
    ]
    for copy in reads:
        copy.start()
    for n in range(2 * GROUPS):
        side, g = divmod(n, GROUPS)
        home = jnp.where(me == side, 0, half) + g * width
        for i in range(2):
            gamma_buffer[n, :, i, :] = totals[n][:, i * width : (i + 1) * width]
        writes.append(
            pltpu.make_async_copy(
                gamma_buffer.at[n],
                gamma.at[:, :, pl.ds(pl.multiple_of(home, 128), width)],
                gamma_sems.at[n],
            )
        )
        reads[n].wait()
        writes[n].start()
        writes[-1].start()
    for copy in writes:
        copy.wait()


def close(other, whole, kept, received):
    batch, double = received[0].shape
    any_space = pl.BlockSpec(memory_space=pl.ANY)
    in_vmem = pl.BlockSpec(memory_space=pltpu.VMEM)
    return pl.pallas_call(
        close_kernel,
        out_shape=(
            jax.ShapeDtypeStruct(whole.shape, whole.dtype),
            jax.ShapeDtypeStruct((batch, 2, GROUPS * double), jnp.float32),
        ),
        in_specs=[any_space, any_space] + [in_vmem] * (2 * GROUPS),
        out_specs=(any_space, any_space),
        scratch_shapes=[
            pltpu.VMEM(other.shape, other.dtype),
            pltpu.VMEM((2 * GROUPS, batch, 2, double // 2), jnp.float32),
            pltpu.SemaphoreType.DMA((2, 2, 2)),
            pltpu.SemaphoreType.DMA((2 * GROUPS,)),
        ],
        input_output_aliases={1: 0},
        compiler_params=pltpu.CompilerParams(vmem_limit_bytes=48 * 2**20),
        cost_estimate=pl.CostEstimate(
            flops=0, bytes_accessed=4 * other.size + 16 * batch * double * GROUPS, transcendentals=0
        ),
    )(other, whole, *kept, *received)


def swap(x):
    return lax.ppermute(x, "occ", [(0, 1), (1, 0)])


def planar(x, offset):
    return lax.ppermute(x, "row", [(r, r ^ offset) for r in range(4)])


def hop_up(x, first):
    return lax.ppermute(x, "col", [(c, c + 1) for c in range(first, 3)])


def hop_down(x, first):
    return lax.ppermute(x, "col", [(3 - c, 2 - c) for c in range(first, 3)])


def pairs(x):
    return lax.ppermute(x, "col", [(0, 1), (1, 0), (2, 3), (3, 2)])


def across(x):
    return lax.ppermute(x, "col", [(1, 2), (2, 1)])


def outward(x):
    return lax.ppermute(x, "col", [(1, 0), (2, 3)])


def inward(x):
    return lax.ppermute(x, "col", [(0, 1), (3, 2)])


def tie(*arrays):
    return lax.optimization_barrier(arrays)


def planned(bra_factor, ket_factor, occ_energy, virt_energy):
    batch, _, a_width = bra_factor.shape
    b_width = ket_factor.shape[2]

    bra_kept, bra_given = pick(bra_factor.reshape(batch, 2 * a_width))
    ket_own = ket_factor.reshape(batch, 2 * b_width)
    bra = jnp.stack([bra_kept, swap(bra_given)], axis=1)
    ket_x = planar(ket_own, 1)
    ket_y = planar(ket_own, 2)
    cut = batch // 2
    pieces = ((0, 0, batch), (1, 0, batch), (2, 0, batch), (3, 0, cut), (3, cut, batch - cut))

    ups, downs = [[hop_up(bra[0], 0)], []], [[hop_down(bra[0], 0)], []]
    ket_swapped = swap(ket_own)
    ups[0].append(hop_up(ups[0][0], 1))
    downs[0].append(hop_down(downs[0][0], 1))
    ket_x, ket_y, ups[0][1], downs[0][1], ket_swapped = tie(
        ket_x, ket_y, ups[0][1], downs[0][1], ket_swapped
    )
    part_x, part_y, late_x, late_y = tie(ket_x[:cut], ket_y[cut:], ket_x, ket_y)
    far_y, far_x = planar(part_x, 2), planar(part_y, 1)
    late_y, far_y = tie(late_y, far_y)
    ups[0].append(hop_up(ups[0][1], 2))
    downs[0].append(hop_down(downs[0][1], 2))
    straight = [swap(late_x), swap(late_y)]
    ups[0][2], downs[0][2], far_y, far_x = tie(ups[0][2], downs[0][2], far_y, far_x)
    ket = [ket_own, ket_x, ket_y, far_y, far_x, ket_swapped, *straight, swap(far_y), swap(far_x)]
    ups[0][2], downs[0][2], block = tie(ups[0][2], downs[0][2], bra[1])
    ups[1].append(hop_up(block, 0))
    downs[1].append(hop_down(block, 0))
    energies = (occ_energy, virt_energy[None, :])

    def up_cast(x):
        return x.astype(jnp.float32)

    near = lax.bitwise_and(lax.axis_index("col"), 1)

    def cross(far, one):
        return across((far + up_cast(one)).astype(jnp.bfloat16))

    def exchange(pair, two):
        theirs = lax.dynamic_index_in_dim(two, 1 - near, 0, keepdims=False)
        return pairs((pair + up_cast(theirs)).astype(jnp.bfloat16))

    def finish(own, two, three):
        ours = lax.dynamic_index_in_dim(two, near, 0, keepdims=False)
        return own + up_cast(ours) + up_cast(three)

    both = (1, 0)
    arrived = [bra[0], *ups[0], *downs[0]]
    (whole, mine), own0, pair0, far0, send0, (ket_all,) = run_group(
        0, ket, pieces, arrived, energies, ()
    )
    one0 = {q: inward(send0[q]) for q in both}
    own_first, up, down = tie(own0[0], ups[1][0], downs[1][0])
    for hop in (1, 2):
        ups[1].append(hop_up(ups[1][hop - 1] if hop > 1 else up, hop))
        downs[1].append(hop_down(downs[1][hop - 1] if hop > 1 else down, hop))
    other0 = swap(mine)
    two0 = {1: cross(far0[1], one0[1])}
    arrived = [bra[1], *ups[1], *downs[1]]
    two0[1], arrived[0] = tie(two0[1], arrived[0])
    (whole, mine), own1, pair1, far1, send1, _ = run_group(
        1, [ket_all], pieces, arrived, energies, (other0, whole)
    )
    one1 = {q: inward(send1[q]) for q in both}
    other1 = swap(mine)
    two0[0] = cross(far0[0], one0[0])
    two1 = {q: cross(far1[q], one1[q]) for q in both}
    one1[1], two0[0], two0[1] = tie(one1[1], two0[0], two0[1])
    own0 = (own_first, own0[1])
    three0 = {q: exchange(pair0[q], two0[q]) for q in both}
    three1 = {q: exchange(pair1[q], two1[q]) for q in both}
    received = [
        swap(finish(own[1], two[1], three[1]))
        for own, two, three in ((own0, two0, three0), (own1, two1, three1))
    ]
    kept = [
        finish(own[0], two[0], three[0])
        for own, two, three in ((own0, two0, three0), (own1, two1, three1))
    ]
    return close(other1, whole, kept, received)


def solution(mesh):
    sizes = mesh.shape

    def on_device(bra_factor, ket_factor, occ_energy, virt_energy):
        fits = (
            sizes["occ"] == 2
            and sizes["row"] == 4
            and sizes["col"] == 4
            and bra_factor.shape[2] % (256 * GROUPS) == 0
            and ket_factor.shape[2] % 512 == 0
            and bra_factor.shape[0] % 128 == 0
        )
        body = planned if fits else general
        return body(bra_factor, ket_factor, occ_energy, virt_energy)

    placed = (P(("occ", "col"), None, "row"), P(("occ", "row"), None, "col"), P(), P())
    return jax.shard_map(
        on_device,
        mesh=mesh,
        in_specs=placed,
        out_specs=(P(None, None, "row", "col"), P(("occ", "col"), None, "row")),
        check_vma=False,
    )
```

```python
import functools

import jax
import jax.numpy as jnp
from jax import lax
from jax.experimental import pallas as pl
from jax.experimental.pallas import tpu as pltpu
from jax.sharding import PartitionSpec as P


def make_amplitudes(coulomb, occ_energy, virt_first, virt_second):
    denominator = (
        occ_energy[:, None, None, None]
        + occ_energy[None, :, None, None]
        - virt_first[None, None, :, None]
        - virt_second[None, None, None, :]
    )
    return ((2.0 * coulomb - jnp.transpose(coulomb, (1, 0, 2, 3))) / denominator).astype(
        jnp.bfloat16
    )


def general(bra_factor, ket_factor, occ_energy, virt_energy):
    a_width = bra_factor.shape[2]
    b_width = ket_factor.shape[2]
    ket_whole = lax.all_gather(ket_factor, "row", axis=0, tiled=True)
    row_index = lax.axis_index("row")
    col_index = lax.axis_index("col")
    virt_first = lax.dynamic_slice_in_dim(virt_energy, row_index * a_width, a_width, 0)
    virt_second = lax.dynamic_slice_in_dim(virt_energy, col_index * b_width, b_width, 0)
    partial_sum = jnp.einsum(
        "qia,qjb->ijab",
        lax.all_gather(bra_factor, "col", axis=0, tiled=True),
        ket_whole,
        preferred_element_type=jnp.float32,
    )
    batch_count = lax.axis_size("occ")
    pad_rows = (batch_count - a_width % batch_count) % batch_count
    padded = jnp.pad(partial_sum, ((0, 0), (0, 0), (0, pad_rows), (0, 0)))
    share_sum = lax.psum_scatter(padded, "occ", scatter_dimension=2, tiled=True)
    share_len = share_sum.shape[2]
    energy_padded = jnp.pad(virt_first, (0, pad_rows), constant_values=1.0)
    energy_share = lax.dynamic_slice_in_dim(
        energy_padded, lax.axis_index("occ") * share_len, share_len, 0
    )
    share_amps = make_amplitudes(share_sum, occ_energy, energy_share, virt_second)
    collected = lax.all_gather(share_amps, "occ", axis=2, tiled=True)
    amplitudes = collected[:, :, :a_width, :]
    gamma = lax.psum_scatter(
        jnp.einsum("ijab,qjb->qia", amplitudes, ket_whole, preferred_element_type=jnp.float32),
        "col",
        scatter_dimension=0,
        tiled=True,
    )
    return (amplitudes, gamma)


BLOCKS = 2
GROUPS = 3
SLICES = 4
SPLIT = (True, False, True)


def parts_of(group, batch):
    return (slice(batch, 2 * batch), slice(0, batch)) if SPLIT[group] else (slice(0, 2 * batch),)


def place_of(group, block):
    if group == 0:
        return 0, 0, block
    return 1, (group - 1) * (block // 2), block // 2


def group_kernel(pieces, group, *refs):
    refs = list(refs)
    take = lambda count: [refs.pop(0) for _ in range(count)]
    ket = take(1 if group else 2 * len(pieces))
    (bra,) = take(1)
    ups, downs = take(3), take(3)
    occ_ref, virt_ref = take(2)
    aliased = take(2) if group else None
    whole_ref, half_ref = take(2)
    own_ref, pair_ref, far_ref, send_ref = (take(1 + SPLIT[group]) for _ in range(4))
    (ket_all,) = (None,) if group else take(1)
    kv, bv, bt, t2, amps, given, ket_sem, bra_sem, out_sem = refs
    batch, block_width = bra.shape[2:]
    number, start, width = place_of(group, block_width)
    span = ket[0].shape[1] // 2
    half = whole_ref.shape[2] // 2
    part = span // SLICES
    here_row, here_col = lax.axis_index("row"), lax.axis_index("col")
    me = lax.axis_index("occ")
    pair = lax.bitwise_xor(here_col, 1)
    low = here_col < 2

    def bra_copies(source, home, slot):
        return [
            pltpu.make_async_copy(
                source.at[q, i, :, pl.ds(start, width)],
                bv.at[home, pl.ds(q * batch, batch), pl.ds(i * width, width)],
                bra_sem.at[slot, q, i],
            )
            for q in range(2)
            for i in range(2)
        ]

    def fetch(condition, source, home, slot):
        @pl.when(condition)
        def _():
            for copy in bra_copies(source, home, slot):
                copy.start()

    for copy in bra_copies(bra, here_col, 0):
        copy.start()
    for d in range(1, 4):
        home = lax.rem(here_col + 4 - d, 4)
        fetch(here_col >= d, ups[d - 1], home, d)
        fetch(here_col < d, downs[3 - d], home, d)

    copies = [[] for _ in range(SLICES)]
    for n in range(SLICES):
        for j in range(2):
            columns = pl.ds(j * span + n * part, part)
            if group:
                moves = [(ket[0], 0, 8 * batch, 0)]
            else:
                moves = []
                for index, source in enumerate(ket):
                    q, place = divmod(index, len(pieces))
                    offset, begin, rows = pieces[place]
                    home = lax.bitwise_xor(here_row, offset) * (2 * batch) + q * batch + begin
                    moves.append((source, pl.multiple_of(home, 16), rows, index))
            for source, home, rows, index in moves:
                copy = pltpu.make_async_copy(
                    source.at[:, columns],
                    kv.at[pl.ds(home, rows), columns],
                    ket_sem.at[n, index, j],
                )
                copy.start()
                copies[n].append(copy)
    if group == 1:
        given_in = pltpu.make_async_copy(aliased[0], given, out_sem.at[2])
        given_in.start()
    for slot in range(4):
        for copy in bra_copies(bra, slot, slot):
            copy.wait()
    row_at = number * block_width + start
    first_at = here_row * (2 * half) + me * half + row_at
    first = virt_ref[:, pl.ds(pl.multiple_of(first_at, 128), width)]
    first = jnp.broadcast_to(first, (width, width)).T[:, :1]
    for d in range(4):
        bt[:, d * 2 * batch : (d + 1) * 2 * batch] = bv[d].T
    for n in range(SLICES):
        for copy in copies[n]:
            copy.wait()
        tile = [
            jnp.dot(
                bt[...],
                kv[:, j * span + n * part : j * span + (n + 1) * part],
                preferred_element_type=jnp.float32,
            )
            for j in range(2)
        ]
        second_at = pl.multiple_of(here_col * span + n * part, 128)
        second = virt_ref[:, pl.ds(second_at, part)]
        for i in range(2):
            for j in range(2):
                direct = tile[j][i * width : (i + 1) * width, :]
                exchange = tile[i][j * width : (j + 1) * width, :]
                denominator = ((occ_ref[i] + occ_ref[j]) - first) - second
                block = ((2.0 * direct - exchange) / denominator).astype(jnp.bfloat16)
                amps[i, j, :, n * part : (n + 1) * part] = block
                t2[
                    i * width : (i + 1) * width,
                    j * span + n * part : j * span + (n + 1) * part,
                ] = block
    at = pl.multiple_of(me * half + row_at, 16)
    outs = [
        pltpu.make_async_copy(amps, whole_ref.at[:, :, pl.ds(at, width), :], out_sem.at[0]),
        pltpu.make_async_copy(amps, half_ref.at[:, :, pl.ds(start, width), :], out_sem.at[1]),
    ]
    if group == 1:
        given_in.wait()
        at = pl.multiple_of((1 - me) * half, 16)
        outs.append(
            pltpu.make_async_copy(
                given, whole_ref.at[:, :, pl.ds(at, block_width), :], out_sem.at[2]
            )
        )
    if group == 0:
        outs.append(pltpu.make_async_copy(kv, ket_all, out_sem.at[2]))
    for copy in outs:
        copy.start()

    def share_of(home):
        rows = pl.ds(pl.multiple_of(home * (2 * batch), 16), 2 * batch)
        return lax.dot_general(
            kv[rows, :],
            t2[...],
            (((1,), (1,)), ((), ())),
            preferred_element_type=jnp.float32,
        )

    for n in range(2):
        share = share_of(jnp.where(low, 2 + n, n))
        for p, rows in enumerate(parts_of(group, batch)):
            far_ref[p][n] = share[rows]
            send_ref[p][n] = share[rows].astype(jnp.bfloat16)
    for out, home in ((pair_ref, pair), (own_ref, here_col)):
        share = share_of(home)
        for p, rows in enumerate(parts_of(group, batch)):
            out[p][...] = share[rows]
    for copy in outs:
        copy.wait()


def run_group(group, ket, pieces, bras, energies, held):
    _, _, batch, block_width = bras[0].shape
    _, _, width = place_of(group, block_width)
    span = ket[0].shape[1] // 2
    half = block_width * BLOCKS
    total = 8 * batch
    flops = 2 * 2 * total * 2 * width * 2 * span
    any_space = pl.BlockSpec(memory_space=pl.ANY)
    in_vmem = pl.BlockSpec(memory_space=pltpu.VMEM)
    in_hbm = pl.BlockSpec(memory_space=pltpu.HBM)
    ahead = len(ket) + len(bras) + 2
    count = 1 + SPLIT[group]
    rows = 2 * batch // count
    block = jax.ShapeDtypeStruct((rows, 2 * width), jnp.float32)
    far = jax.ShapeDtypeStruct((2, rows, 2 * width), jnp.float32)
    send = jax.ShapeDtypeStruct((2, rows, 2 * width), jnp.bfloat16)
    half_shape = (2, 2, block_width, span)
    results = pl.pallas_call(
        functools.partial(group_kernel, pieces, group),
        out_shape=(
            jax.ShapeDtypeStruct((2, 2, 2 * half, span), jnp.bfloat16),
            jax.ShapeDtypeStruct(half_shape, jnp.bfloat16),
        )
        + (block,) * (2 * count)
        + (far,) * count
        + (send,) * count
        + (() if group else (jax.ShapeDtypeStruct((total, 2 * span), jnp.bfloat16),)),
        in_specs=[in_hbm if group else any_space] * len(ket)
        + [any_space] * len(bras)
        + [pl.BlockSpec(memory_space=pltpu.SMEM), in_vmem]
        + [any_space] * len(held),
        out_specs=(any_space, any_space) + (in_vmem,) * (4 * count) + (() if group else (in_hbm,)),
        scratch_shapes=[
            pltpu.VMEM((total, 2 * span), jnp.bfloat16),
            pltpu.VMEM((4, 2 * batch, 2 * width), jnp.bfloat16),
            pltpu.VMEM((2 * width, total), jnp.bfloat16),
            pltpu.VMEM((2 * width, 2 * span), jnp.bfloat16),
            pltpu.VMEM((2, 2, width, span), jnp.bfloat16),
            pltpu.VMEM(half_shape if group == 1 else (2, 2, 16, 128), jnp.bfloat16),
            pltpu.SemaphoreType.DMA((SLICES, 2 * len(pieces), 2)),
            pltpu.SemaphoreType.DMA((4, 2, 2)),
            pltpu.SemaphoreType.DMA((3,)),
        ],
        input_output_aliases=({}, {ahead + 1: 0}, {ahead: 1, ahead + 1: 0})[group],
        compiler_params=pltpu.CompilerParams(vmem_limit_bytes=44 * 2**20),
        cost_estimate=pl.CostEstimate(
            flops=flops, bytes_accessed=total * 2 * span * 2, transcendentals=0
        ),
    )(*ket, *bras, *energies, *held)
    ends = [2 + n * count for n in range(5)]
    return results[:2], *(results[n : n + count] for n in ends[:4]), results[ends[4] :]


def pick_kernel(bra, kept_out, given_out):
    width = kept_out.shape[3]
    span = bra.shape[1] // 2
    me = lax.axis_index("occ")
    for side, out in ((1 - me, given_out), (me, kept_out)):
        for g in range(BLOCKS):
            for i in range(2):
                home = i * span + side * (span // 2) + g * width
                out[g, i] = bra[:, pl.ds(pl.multiple_of(home, 128), width)]


def pick(bra):
    batch, columns = bra.shape
    part = jax.ShapeDtypeStruct((BLOCKS, 2, batch, columns // 4 // BLOCKS), bra.dtype)
    return pl.pallas_call(
        pick_kernel,
        out_shape=(part, part),
        compiler_params=pltpu.CompilerParams(vmem_limit_bytes=16 * 2**20),
        cost_estimate=pl.CostEstimate(
            flops=0, bytes_accessed=4 * bra.size, transcendentals=0
        ),
    )(bra)


def close_kernel(*refs):
    other, _, *totals = refs[: 2 + 2 * GROUPS]
    amps, gamma, amp_buffer, gamma_buffer, sems, gamma_sems = refs[2 + 2 * GROUPS :]
    block_width = other.shape[2]
    half = block_width * BLOCKS
    batch = gamma.shape[0]
    me = lax.axis_index("occ")
    at = pl.multiple_of((1 - me) * half + half - block_width, 16)
    blocks = [(i, j) for i in range(2) for j in range(2)]
    reads = [
        pltpu.make_async_copy(other.at[i, j], amp_buffer.at[i, j], sems.at[0, i, j])
        for i, j in blocks
    ]
    writes = [
        pltpu.make_async_copy(
            amp_buffer.at[i, j], amps.at[i, j, pl.ds(at, block_width), :], sems.at[1, i, j]
        )
        for i, j in blocks
    ]
    for copy in reads:
        copy.start()
    for n in range(2 * GROUPS):
        side, group = divmod(n, GROUPS)
        number, start, width = place_of(group, block_width)
        at = number * block_width + start
        home = jnp.where(me == side, 0, half) + at
        columns = pl.ds(side * half + at, width)
        for i in range(2):
            gamma_buffer[:, i, columns] = totals[n][:batch, i * width : (i + 1) * width]
        writes.append(
            pltpu.make_async_copy(
                gamma_buffer.at[:, :, columns],
                gamma.at[:, :, pl.ds(pl.multiple_of(home, 128), width)],
                gamma_sems.at[n],
            )
        )
        if n < len(blocks):
            reads[n].wait()
            writes[n].start()
        writes[-1].start()
    for copy in writes:
        copy.wait()


def close(other, whole, kept, received):
    batch = received[0].shape[0]
    columns = whole.shape[2]
    any_space = pl.BlockSpec(memory_space=pl.ANY)
    in_vmem = pl.BlockSpec(memory_space=pltpu.VMEM)
    return pl.pallas_call(
        close_kernel,
        out_shape=(
            jax.ShapeDtypeStruct(whole.shape, whole.dtype),
            jax.ShapeDtypeStruct((batch, 2, columns), jnp.float32),
        ),
        in_specs=[any_space, any_space] + [in_vmem] * (2 * GROUPS),
        out_specs=(any_space, any_space),
        scratch_shapes=[
            pltpu.VMEM(other.shape, other.dtype),
            pltpu.VMEM((batch, 2, columns), jnp.float32),
            pltpu.SemaphoreType.DMA((2, 2, 2)),
            pltpu.SemaphoreType.DMA((2 * GROUPS,)),
        ],
        input_output_aliases={1: 0},
        compiler_params=pltpu.CompilerParams(vmem_limit_bytes=48 * 2**20),
        cost_estimate=pl.CostEstimate(
            flops=0, bytes_accessed=4 * other.size + 16 * batch * columns, transcendentals=0
        ),
    )(other, whole, *kept, *received)


def swap(x):
    return lax.ppermute(x, "occ", [(0, 1), (1, 0)])


def planar(x, offset):
    return lax.ppermute(x, "row", [(r, r ^ offset) for r in range(4)])


def hop_up(x, first):
    return lax.ppermute(x, "col", [(c, c + 1) for c in range(first, 3)])


def hop_down(x, first):
    return lax.ppermute(x, "col", [(3 - c, 2 - c) for c in range(first, 3)])


def pairs(x):
    return lax.ppermute(x, "col", [(0, 1), (1, 0), (2, 3), (3, 2)])


def across(x):
    return lax.ppermute(x, "col", [(1, 2), (2, 1)])


def outward(x):
    return lax.ppermute(x, "col", [(1, 0), (2, 3)])


def inward(x):
    return lax.ppermute(x, "col", [(0, 1), (3, 2)])


def tie(*arrays):
    return lax.optimization_barrier(arrays)


def planned(bra_factor, ket_factor, occ_energy, virt_energy):
    batch, _, a_width = bra_factor.shape
    b_width = ket_factor.shape[2]

    bra_kept, bra_given = pick(bra_factor.reshape(batch, 2 * a_width))
    ket_own = ket_factor.reshape(batch, 2 * b_width)
    bra = jnp.stack([bra_kept, swap(bra_given)], axis=1)
    ket_x = planar(ket_own, 1)
    ket_y = planar(ket_own, 2)
    cut = batch // 2
    pieces = ((0, 0, batch), (1, 0, batch), (2, 0, batch), (3, 0, cut), (3, cut, batch - cut))

    ups, downs = [[hop_up(bra[0], 0)], []], [[hop_down(bra[0], 0)], []]
    ket_swapped = swap(ket_own)
    ups[0].append(hop_up(ups[0][0], 1))
    downs[0].append(hop_down(downs[0][0], 1))
    ket_x, ket_y, ups[0][1], downs[0][1], ket_swapped = tie(
        ket_x, ket_y, ups[0][1], downs[0][1], ket_swapped
    )
    part_x, part_y, late_x, late_y = tie(ket_x[:cut], ket_y[cut:], ket_x, ket_y)
    far_y, far_x = planar(part_x, 2), planar(part_y, 1)
    late_y, far_y = tie(late_y, far_y)
    ups[0].append(hop_up(ups[0][1], 2))
    downs[0].append(hop_down(downs[0][1], 2))
    straight = [swap(late_x), swap(late_y)]
    ups[0][2], downs[0][2], far_y, far_x = tie(ups[0][2], downs[0][2], far_y, far_x)
    ket = [ket_own, ket_x, ket_y, far_y, far_x, ket_swapped, *straight, swap(far_y), swap(far_x)]
    ups[0][2], downs[0][2], block = tie(ups[0][2], downs[0][2], bra[1])
    ups[1].append(hop_up(block, 0))
    downs[1].append(hop_down(block, 0))
    energies = (occ_energy, virt_energy[None, :])

    def up_cast(x):
        return x.astype(jnp.float32)

    near = lax.bitwise_and(lax.axis_index("col"), 1)

    def cross(far, one):
        return across((far + up_cast(one)).astype(jnp.bfloat16))

    def exchange(pair, two):
        theirs = lax.dynamic_index_in_dim(two, 1 - near, 0, keepdims=False)
        return pairs((pair + up_cast(theirs)).astype(jnp.bfloat16))

    def finish(own, two, three):
        ours = lax.dynamic_index_in_dim(two, near, 0, keepdims=False)
        return own + up_cast(ours) + up_cast(three)

    def finish_all(group, own, two, three):
        total = [finish(*part) for part in zip(own, two, three)]
        if not SPLIT[group]:
            total = [total[0][batch:], total[0][:batch]]
        return total[1], swap(total[0])

    arrived = [bra[0], *ups[0], *downs[0]]
    (whole, mine), own0, pair0, far0, send0, (ket_all,) = run_group(
        0, ket, pieces, arrived, energies, ()
    )
    one0 = [inward(send) for send in send0]
    own_last, up, down = tie(own0[1], ups[1][0], downs[1][0])
    own0 = (own0[0], own_last)
    ups[1] += [hop_up(up, 1)]
    downs[1] += [hop_down(down, 1)]
    ups[1] += [hop_up(ups[1][1], 2)]
    downs[1] += [hop_down(downs[1][1], 2)]
    other = swap(mine)
    two0 = [cross(far0[0], one0[0])]
    arrived = [bra[1], *ups[1], *downs[1]]
    two0[0], arrived[0] = tie(two0[0], arrived[0])
    (whole, mine), own1, pair1, far1, send1, _ = run_group(
        1, [ket_all], pieces, arrived, energies, (other, whole)
    )
    one1 = [inward(send) for send in send1]
    arrived = list(arrived)
    (whole, mine), own2, pair2, far2, send2, _ = run_group(
        2, [ket_all], pieces, arrived, energies, (mine, whole)
    )
    one2 = [inward(send) for send in send2]
    other = swap(mine)
    two0.append(cross(far0[1], one0[1]))
    two1 = [cross(*part) for part in zip(far1, one1)]
    two2 = [cross(*part) for part in zip(far2, one2)]
    one2[0], two0[1] = tie(one2[0], two0[1])
    three0 = [exchange(*part) for part in zip(pair0, two0)]
    three1 = [exchange(*part) for part in zip(pair1, two1)]
    three2 = [exchange(*part) for part in zip(pair2, two2)]
    ends = [
        finish_all(0, own0, two0, three0),
        finish_all(1, own1, two1, three1),
        finish_all(2, own2, two2, three2),
    ]
    return close(other, whole, [end[0] for end in ends], [end[1] for end in ends])


def solution(mesh):
    sizes = mesh.shape

    def on_device(bra_factor, ket_factor, occ_energy, virt_energy):
        fits = (
            sizes["occ"] == 2
            and sizes["row"] == 4
            and sizes["col"] == 4
            and bra_factor.shape[2] % 1024 == 0
            and ket_factor.shape[2] % 512 == 0
            and bra_factor.shape[0] % 128 == 0
        )
        body = planned if fits else general
        return body(bra_factor, ket_factor, occ_energy, virt_energy)

    placed = (P(("occ", "col"), None, "row"), P(("occ", "row"), None, "col"), P(), P())
    return jax.shard_map(
        on_device,
        mesh=mesh,
        in_specs=placed,
        out_specs=(P(None, None, "row", "col"), P(("occ", "col"), None, "row")),
        check_vma=False,
    )
```

```python
import functools

import jax
import jax.numpy as jnp
from jax import lax
from jax.experimental import pallas as pl
from jax.experimental.pallas import tpu as pltpu
from jax.sharding import PartitionSpec as P


def make_amplitudes(coulomb, occ_energy, virt_first, virt_second):
    denominator = (
        occ_energy[:, None, None, None]
        + occ_energy[None, :, None, None]
        - virt_first[None, None, :, None]
        - virt_second[None, None, None, :]
    )
    return ((2.0 * coulomb - jnp.transpose(coulomb, (1, 0, 2, 3))) / denominator).astype(
        jnp.bfloat16
    )


def general(bra_factor, ket_factor, occ_energy, virt_energy):
    a_width = bra_factor.shape[2]
    b_width = ket_factor.shape[2]
    ket_whole = lax.all_gather(ket_factor, "row", axis=0, tiled=True)
    row_index = lax.axis_index("row")
    col_index = lax.axis_index("col")
    virt_first = lax.dynamic_slice_in_dim(virt_energy, row_index * a_width, a_width, 0)
    virt_second = lax.dynamic_slice_in_dim(virt_energy, col_index * b_width, b_width, 0)
    partial_sum = jnp.einsum(
        "qia,qjb->ijab",
        lax.all_gather(bra_factor, "col", axis=0, tiled=True),
        ket_whole,
        preferred_element_type=jnp.float32,
    )
    batch_count = lax.axis_size("occ")
    pad_rows = (batch_count - a_width % batch_count) % batch_count
    padded = jnp.pad(partial_sum, ((0, 0), (0, 0), (0, pad_rows), (0, 0)))
    share_sum = lax.psum_scatter(padded, "occ", scatter_dimension=2, tiled=True)
    share_len = share_sum.shape[2]
    energy_padded = jnp.pad(virt_first, (0, pad_rows), constant_values=1.0)
    energy_share = lax.dynamic_slice_in_dim(
        energy_padded, lax.axis_index("occ") * share_len, share_len, 0
    )
    share_amps = make_amplitudes(share_sum, occ_energy, energy_share, virt_second)
    collected = lax.all_gather(share_amps, "occ", axis=2, tiled=True)
    amplitudes = collected[:, :, :a_width, :]
    gamma = lax.psum_scatter(
        jnp.einsum("ijab,qjb->qia", amplitudes, ket_whole, preferred_element_type=jnp.float32),
        "col",
        scatter_dimension=0,
        tiled=True,
    )
    return (amplitudes, gamma)


BLOCKS = 2
GROUPS = 4
SLICES = 4
SPLIT = (False, False, False, True)


def parts_of(group, batch):
    return (slice(batch, 2 * batch), slice(0, batch)) if SPLIT[group] else (slice(0, 2 * batch),)


def place_of(group, block):
    return group // 2, (group % 2) * (block // 2), block // 2


def group_kernel(pieces, group, *refs):
    refs = list(refs)
    take = lambda count: [refs.pop(0) for _ in range(count)]
    ket = take(1 if group else 2 * len(pieces))
    (bra,) = take(1)
    ups, downs = take(3), take(3)
    occ_ref, virt_ref = take(2)
    aliased = take(2) if group else None
    whole_ref, half_ref = take(2)
    own_ref, pair_ref, far_ref, send_ref = (take(1 + SPLIT[group]) for _ in range(4))
    (ket_all,) = (None,) if group else take(1)
    kv, bv, bt, t2, amps, given, ket_sem, bra_sem, out_sem = refs
    batch, block_width = bra.shape[2:]
    number, start, width = place_of(group, block_width)
    span = ket[0].shape[1] // 2
    half = whole_ref.shape[2] // 2
    part = span // SLICES
    here_row, here_col = lax.axis_index("row"), lax.axis_index("col")
    me = lax.axis_index("occ")
    pair = lax.bitwise_xor(here_col, 1)
    low = here_col < 2

    def bra_copies(source, home, slot):
        return [
            pltpu.make_async_copy(
                source.at[q, i, :, pl.ds(start, width)],
                bv.at[home, pl.ds(q * batch, batch), pl.ds(i * width, width)],
                bra_sem.at[slot, q, i],
            )
            for q in range(2)
            for i in range(2)
        ]

    def fetch(condition, source, home, slot):
        @pl.when(condition)
        def _():
            for copy in bra_copies(source, home, slot):
                copy.start()

    for copy in bra_copies(bra, here_col, 0):
        copy.start()
    for d in range(1, 4):
        home = lax.rem(here_col + 4 - d, 4)
        fetch(here_col >= d, ups[d - 1], home, d)
        fetch(here_col < d, downs[3 - d], home, d)

    copies = [[] for _ in range(SLICES)]
    for n in range(SLICES):
        for j in range(2):
            columns = pl.ds(j * span + n * part, part)
            if group:
                moves = [(ket[0], 0, 8 * batch, 0)]
            else:
                moves = []
                for index, source in enumerate(ket):
                    q, place = divmod(index, len(pieces))
                    offset, begin, rows = pieces[place]
                    home = lax.bitwise_xor(here_row, offset) * (2 * batch) + q * batch + begin
                    moves.append((source, pl.multiple_of(home, 16), rows, index))
            for source, home, rows, index in moves:
                copy = pltpu.make_async_copy(
                    source.at[:, columns],
                    kv.at[pl.ds(home, rows), columns],
                    ket_sem.at[n, index, j],
                )
                copy.start()
                copies[n].append(copy)
    if group == 2:
        given_in = pltpu.make_async_copy(aliased[0], given, out_sem.at[2])
        given_in.start()
    for slot in range(4):
        for copy in bra_copies(bra, slot, slot):
            copy.wait()
    row_at = number * block_width + start
    first_at = here_row * (2 * half) + me * half + row_at
    first = virt_ref[:, pl.ds(pl.multiple_of(first_at, 128), width)]
    first = jnp.broadcast_to(first, (width, width)).T[:, :1]
    for d in range(4):
        bt[:, d * 2 * batch : (d + 1) * 2 * batch] = bv[d].T
    for n in range(SLICES):
        for copy in copies[n]:
            copy.wait()
        tile = [
            jnp.dot(
                bt[...],
                kv[:, j * span + n * part : j * span + (n + 1) * part],
                preferred_element_type=jnp.float32,
            )
            for j in range(2)
        ]
        second_at = pl.multiple_of(here_col * span + n * part, 128)
        second = virt_ref[:, pl.ds(second_at, part)]
        for i in range(2):
            for j in range(2):
                direct = tile[j][i * width : (i + 1) * width, :]
                exchange = tile[i][j * width : (j + 1) * width, :]
                denominator = ((occ_ref[i] + occ_ref[j]) - first) - second
                block = ((2.0 * direct - exchange) / denominator).astype(jnp.bfloat16)
                amps[i, j, :, n * part : (n + 1) * part] = block
                t2[
                    i * width : (i + 1) * width,
                    j * span + n * part : j * span + (n + 1) * part,
                ] = block
    at = pl.multiple_of(me * half + row_at, 16)
    outs = [
        pltpu.make_async_copy(amps, whole_ref.at[:, :, pl.ds(at, width), :], out_sem.at[0]),
        pltpu.make_async_copy(amps, half_ref.at[:, :, pl.ds(start, width), :], out_sem.at[1]),
    ]
    if group == 2:
        given_in.wait()
        at = pl.multiple_of((1 - me) * half, 16)
        outs.append(
            pltpu.make_async_copy(
                given, whole_ref.at[:, :, pl.ds(at, block_width), :], out_sem.at[2]
            )
        )
    if group == 0:
        outs.append(pltpu.make_async_copy(kv, ket_all, out_sem.at[2]))
    for copy in outs:
        copy.start()

    def share_of(home):
        rows = pl.ds(pl.multiple_of(home * (2 * batch), 16), 2 * batch)
        return lax.dot_general(
            kv[rows, :],
            t2[...],
            (((1,), (1,)), ((), ())),
            preferred_element_type=jnp.float32,
        )

    for n in range(2):
        share = share_of(jnp.where(low, 2 + n, n))
        for p, rows in enumerate(parts_of(group, batch)):
            far_ref[p][n] = share[rows]
            send_ref[p][n] = share[rows].astype(jnp.bfloat16)
    for out, home in ((pair_ref, pair), (own_ref, here_col)):
        share = share_of(home)
        for p, rows in enumerate(parts_of(group, batch)):
            out[p][...] = share[rows]
    for copy in outs:
        copy.wait()


def run_group(group, ket, pieces, bras, energies, held):
    _, _, batch, block_width = bras[0].shape
    _, _, width = place_of(group, block_width)
    span = ket[0].shape[1] // 2
    half = block_width * BLOCKS
    total = 8 * batch
    flops = 2 * 2 * total * 2 * width * 2 * span
    any_space = pl.BlockSpec(memory_space=pl.ANY)
    in_vmem = pl.BlockSpec(memory_space=pltpu.VMEM)
    in_hbm = pl.BlockSpec(memory_space=pltpu.HBM)
    ahead = len(ket) + len(bras) + 2
    count = 1 + SPLIT[group]
    rows = 2 * batch // count
    block = jax.ShapeDtypeStruct((rows, 2 * width), jnp.float32)
    far = jax.ShapeDtypeStruct((2, rows, 2 * width), jnp.float32)
    send = jax.ShapeDtypeStruct((2, rows, 2 * width), jnp.bfloat16)
    half_shape = (2, 2, block_width, span)
    results = pl.pallas_call(
        functools.partial(group_kernel, pieces, group),
        out_shape=(
            jax.ShapeDtypeStruct((2, 2, 2 * half, span), jnp.bfloat16),
            jax.ShapeDtypeStruct(half_shape, jnp.bfloat16),
        )
        + (block,) * (2 * count)
        + (far,) * count
        + (send,) * count
        + (() if group else (jax.ShapeDtypeStruct((total, 2 * span), jnp.bfloat16),)),
        in_specs=[in_hbm if group else any_space] * len(ket)
        + [any_space] * len(bras)
        + [pl.BlockSpec(memory_space=pltpu.SMEM), in_vmem]
        + [any_space] * len(held),
        out_specs=(any_space, any_space) + (in_vmem,) * (4 * count) + (() if group else (in_hbm,)),
        scratch_shapes=[
            pltpu.VMEM((total, 2 * span), jnp.bfloat16),
            pltpu.VMEM((4, 2 * batch, 2 * width), jnp.bfloat16),
            pltpu.VMEM((2 * width, total), jnp.bfloat16),
            pltpu.VMEM((2 * width, 2 * span), jnp.bfloat16),
            pltpu.VMEM((2, 2, width, span), jnp.bfloat16),
            pltpu.VMEM(half_shape if group == 2 else (2, 2, 16, 128), jnp.bfloat16),
            pltpu.SemaphoreType.DMA((SLICES, 2 * len(pieces), 2)),
            pltpu.SemaphoreType.DMA((4, 2, 2)),
            pltpu.SemaphoreType.DMA((3,)),
        ],
        input_output_aliases={
            **({ahead: 1} if group % 2 else {}),
            **({ahead + 1: 0} if group else {}),
        },
        compiler_params=pltpu.CompilerParams(vmem_limit_bytes=44 * 2**20),
        cost_estimate=pl.CostEstimate(
            flops=flops, bytes_accessed=total * 2 * span * 2, transcendentals=0
        ),
    )(*ket, *bras, *energies, *held)
    ends = [2 + n * count for n in range(5)]
    return results[:2], *(results[n : n + count] for n in ends[:4]), results[ends[4] :]


def pick_kernel(bra, kept_out, given_out):
    width = kept_out.shape[3]
    span = bra.shape[1] // 2
    me = lax.axis_index("occ")
    for side, out in ((1 - me, given_out), (me, kept_out)):
        for g in range(BLOCKS):
            for i in range(2):
                home = i * span + side * (span // 2) + g * width
                out[g, i] = bra[:, pl.ds(pl.multiple_of(home, 128), width)]


def pick(bra):
    batch, columns = bra.shape
    part = jax.ShapeDtypeStruct((BLOCKS, 2, batch, columns // 4 // BLOCKS), bra.dtype)
    return pl.pallas_call(
        pick_kernel,
        out_shape=(part, part),
        compiler_params=pltpu.CompilerParams(vmem_limit_bytes=16 * 2**20),
        cost_estimate=pl.CostEstimate(
            flops=0, bytes_accessed=4 * bra.size, transcendentals=0
        ),
    )(bra)


def close_kernel(*refs):
    other, _, *totals = refs[: 2 + 2 * GROUPS]
    amps, gamma, amp_buffer, gamma_buffer, sems, gamma_sems = refs[2 + 2 * GROUPS :]
    block_width = other.shape[2]
    half = block_width * BLOCKS
    batch = gamma.shape[0]
    me = lax.axis_index("occ")
    at = pl.multiple_of((1 - me) * half + half - block_width, 16)
    blocks = [(i, j) for i in range(2) for j in range(2)]
    reads = [
        pltpu.make_async_copy(other.at[i, j], amp_buffer.at[i, j], sems.at[0, i, j])
        for i, j in blocks
    ]
    writes = [
        pltpu.make_async_copy(
            amp_buffer.at[i, j], amps.at[i, j, pl.ds(at, block_width), :], sems.at[1, i, j]
        )
        for i, j in blocks
    ]
    for copy in reads:
        copy.start()
    for n in range(2 * GROUPS):
        side, group = divmod(n, GROUPS)
        number, start, width = place_of(group, block_width)
        at = number * block_width + start
        home = jnp.where(me == side, 0, half) + at
        columns = pl.ds(side * half + at, width)
        for i in range(2):
            gamma_buffer[:, i, columns] = totals[n][:batch, i * width : (i + 1) * width]
        writes.append(
            pltpu.make_async_copy(
                gamma_buffer.at[:, :, columns],
                gamma.at[:, :, pl.ds(pl.multiple_of(home, 128), width)],
                gamma_sems.at[n],
            )
        )
        if n < len(blocks):
            reads[n].wait()
            writes[n].start()
        writes[-1].start()
    for copy in writes:
        copy.wait()


def close(other, whole, kept, received):
    batch = received[0].shape[0]
    columns = whole.shape[2]
    any_space = pl.BlockSpec(memory_space=pl.ANY)
    in_vmem = pl.BlockSpec(memory_space=pltpu.VMEM)
    return pl.pallas_call(
        close_kernel,
        out_shape=(
            jax.ShapeDtypeStruct(whole.shape, whole.dtype),
            jax.ShapeDtypeStruct((batch, 2, columns), jnp.float32),
        ),
        in_specs=[any_space, any_space] + [in_vmem] * (2 * GROUPS),
        out_specs=(any_space, any_space),
        scratch_shapes=[
            pltpu.VMEM(other.shape, other.dtype),
            pltpu.VMEM((batch, 2, columns), jnp.float32),
            pltpu.SemaphoreType.DMA((2, 2, 2)),
            pltpu.SemaphoreType.DMA((2 * GROUPS,)),
        ],
        input_output_aliases={1: 0},
        compiler_params=pltpu.CompilerParams(vmem_limit_bytes=48 * 2**20),
        cost_estimate=pl.CostEstimate(
            flops=0, bytes_accessed=4 * other.size + 16 * batch * columns, transcendentals=0
        ),
    )(other, whole, *kept, *received)


def swap(x):
    return lax.ppermute(x, "occ", [(0, 1), (1, 0)])


def planar(x, offset):
    return lax.ppermute(x, "row", [(r, r ^ offset) for r in range(4)])


def hop_up(x, first):
    return lax.ppermute(x, "col", [(c, c + 1) for c in range(first, 3)])


def hop_down(x, first):
    return lax.ppermute(x, "col", [(3 - c, 2 - c) for c in range(first, 3)])


def pairs(x):
    return lax.ppermute(x, "col", [(0, 1), (1, 0), (2, 3), (3, 2)])


def across(x):
    return lax.ppermute(x, "col", [(1, 2), (2, 1)])


def outward(x):
    return lax.ppermute(x, "col", [(1, 0), (2, 3)])


def inward(x):
    return lax.ppermute(x, "col", [(0, 1), (3, 2)])


def tie(*arrays):
    return lax.optimization_barrier(arrays)


def planned(bra_factor, ket_factor, occ_energy, virt_energy):
    batch, _, a_width = bra_factor.shape
    b_width = ket_factor.shape[2]

    bra_kept, bra_given = pick(bra_factor.reshape(batch, 2 * a_width))
    ket_own = ket_factor.reshape(batch, 2 * b_width)
    bra = jnp.stack([bra_kept, swap(bra_given)], axis=1)
    ket_x = planar(ket_own, 1)
    ket_y = planar(ket_own, 2)
    cut = batch // 2
    pieces = ((0, 0, batch), (1, 0, batch), (2, 0, batch), (3, 0, cut), (3, cut, batch - cut))

    ups, downs = [[hop_up(bra[0], 0)], []], [[hop_down(bra[0], 0)], []]
    ket_swapped = swap(ket_own)
    ups[0].append(hop_up(ups[0][0], 1))
    downs[0].append(hop_down(downs[0][0], 1))
    ket_x, ket_y, ups[0][1], downs[0][1], ket_swapped = tie(
        ket_x, ket_y, ups[0][1], downs[0][1], ket_swapped
    )
    part_x, part_y, late_x, late_y = tie(ket_x[:cut], ket_y[cut:], ket_x, ket_y)
    far_y, far_x = planar(part_x, 2), planar(part_y, 1)
    late_y, far_y = tie(late_y, far_y)
    ups[0].append(hop_up(ups[0][1], 2))
    downs[0].append(hop_down(downs[0][1], 2))
    straight = [swap(late_x), swap(late_y)]
    ups[0][2], downs[0][2], far_y, far_x = tie(ups[0][2], downs[0][2], far_y, far_x)
    ket = [ket_own, ket_x, ket_y, far_y, far_x, ket_swapped, *straight, swap(far_y), swap(far_x)]
    ups[0][2], downs[0][2], block = tie(ups[0][2], downs[0][2], bra[1])
    ups[1].append(hop_up(block, 0))
    downs[1].append(hop_down(block, 0))
    energies = (occ_energy, virt_energy[None, :])

    def up_cast(x):
        return x.astype(jnp.float32)

    near = lax.bitwise_and(lax.axis_index("col"), 1)

    def cross(far, one):
        return across((far + up_cast(one)).astype(jnp.bfloat16))

    def exchange(pair, two):
        theirs = lax.dynamic_index_in_dim(two, 1 - near, 0, keepdims=False)
        return pairs((pair + up_cast(theirs)).astype(jnp.bfloat16))

    def finish(own, two, three):
        ours = lax.dynamic_index_in_dim(two, near, 0, keepdims=False)
        return own + up_cast(ours) + up_cast(three)

    def finish_all(group, own, two, three):
        total = [finish(*part) for part in zip(own, two, three)]
        if not SPLIT[group]:
            total = [total[0][batch:], total[0][:batch]]
        return total[1], swap(total[0])

    whole = ket_all = mine = other = None
    own, pair, far, one, two = ({} for _ in range(5))

    def begin(group, arrived):
        nonlocal whole, ket_all, mine
        held = () if group == 0 else (other if group == 2 else mine, whole)
        (whole, mine), own[group], pair[group], far[group], send, gathered = run_group(
            group, [ket_all] if group else ket, pieces, arrived, energies, held
        )
        ket_all = gathered[0] if group == 0 else ket_all
        send = list(send)
        if group == 1:
            send[0], ups[1][1], downs[1][1] = tie(send[0], ups[1][1], downs[1][1])
        if group == 3:
            send[0], one[2][0] = tie(send[0], one[2][0])
        one[group] = [inward(part) for part in send]

    def middle(group):
        two[group] = [cross(*part) for part in zip(far[group], one[group])]

    first = [bra[0], *ups[0], *downs[0]]
    begin(0, first)
    for group in range(2):
        if group:
            begin(1, first)
        last_own, up, down = tie(own[group][0], ups[1][group], downs[1][group])
        own[group] = (last_own,)
        ups[1].append(hop_up(up, group + 1))
        downs[1].append(hop_down(down, group + 1))
    other = swap(mine)
    middle(0)
    middle(1)
    arrived = [bra[1], *ups[1], *downs[1]]
    one[1][0], arrived[0] = tie(one[1][0], arrived[0])
    begin(2, arrived)
    two[0][0], arrived[0] = tie(two[0][0], arrived[0])
    begin(3, arrived)
    middle(2)
    middle(3)
    one[3][0], two[1][0] = tie(one[3][0], two[1][0])
    one[3][1], mine = tie(one[3][1], mine)
    other = swap(mine)
    ends = []
    for group in range(GROUPS):
        three = [exchange(*part) for part in zip(pair[group], two[group])]
        ends.append(finish_all(group, own[group], two[group], three))
    return close(other, whole, [end[0] for end in ends], [end[1] for end in ends])


def solution(mesh):
    sizes = mesh.shape

    def on_device(bra_factor, ket_factor, occ_energy, virt_energy):
        fits = (
            sizes["occ"] == 2
            and sizes["row"] == 4
            and sizes["col"] == 4
            and bra_factor.shape[2] % 1024 == 0
            and ket_factor.shape[2] % 512 == 0
            and bra_factor.shape[0] % 128 == 0
        )
        body = planned if fits else general
        return body(bra_factor, ket_factor, occ_energy, virt_energy)

    placed = (P(("occ", "col"), None, "row"), P(("occ", "row"), None, "col"), P(), P())
    return jax.shard_map(
        on_device,
        mesh=mesh,
        in_specs=placed,
        out_specs=(P(None, None, "row", "col"), P(("occ", "col"), None, "row")),
        check_vma=False,
    )
```

```python
import functools

import jax
import jax.numpy as jnp
from jax import lax
from jax.experimental import pallas as pl
from jax.experimental.pallas import tpu as pltpu
from jax.sharding import PartitionSpec as P


def make_amplitudes(coulomb, occ_energy, virt_first, virt_second):
    denominator = (
        occ_energy[:, None, None, None]
        + occ_energy[None, :, None, None]
        - virt_first[None, None, :, None]
        - virt_second[None, None, None, :]
    )
    return ((2.0 * coulomb - jnp.transpose(coulomb, (1, 0, 2, 3))) / denominator).astype(
        jnp.bfloat16
    )


def general(bra_factor, ket_factor, occ_energy, virt_energy):
    a_width = bra_factor.shape[2]
    b_width = ket_factor.shape[2]
    ket_whole = lax.all_gather(ket_factor, "row", axis=0, tiled=True)
    row_index = lax.axis_index("row")
    col_index = lax.axis_index("col")
    virt_first = lax.dynamic_slice_in_dim(virt_energy, row_index * a_width, a_width, 0)
    virt_second = lax.dynamic_slice_in_dim(virt_energy, col_index * b_width, b_width, 0)
    partial_sum = jnp.einsum(
        "qia,qjb->ijab",
        lax.all_gather(bra_factor, "col", axis=0, tiled=True),
        ket_whole,
        preferred_element_type=jnp.float32,
    )
    batch_count = lax.axis_size("occ")
    pad_rows = (batch_count - a_width % batch_count) % batch_count
    padded = jnp.pad(partial_sum, ((0, 0), (0, 0), (0, pad_rows), (0, 0)))
    share_sum = lax.psum_scatter(padded, "occ", scatter_dimension=2, tiled=True)
    share_len = share_sum.shape[2]
    energy_padded = jnp.pad(virt_first, (0, pad_rows), constant_values=1.0)
    energy_share = lax.dynamic_slice_in_dim(
        energy_padded, lax.axis_index("occ") * share_len, share_len, 0
    )
    share_amps = make_amplitudes(share_sum, occ_energy, energy_share, virt_second)
    collected = lax.all_gather(share_amps, "occ", axis=2, tiled=True)
    amplitudes = collected[:, :, :a_width, :]
    gamma = lax.psum_scatter(
        jnp.einsum("ijab,qjb->qia", amplitudes, ket_whole, preferred_element_type=jnp.float32),
        "col",
        scatter_dimension=0,
        tiled=True,
    )
    return (amplitudes, gamma)


BLOCKS = 2
GROUPS = 3
SLICES = 4
SPLIT = (True, False, True)


def parts_of(group, batch):
    return (slice(batch, 2 * batch), slice(0, batch)) if SPLIT[group] else (slice(0, 2 * batch),)


def place_of(group, block):
    if group == 0:
        return 0, 0, block
    return 1, (group - 1) * (block // 2), block // 2


def group_kernel(pieces, group, *refs):
    refs = list(refs)
    take = lambda count: [refs.pop(0) for _ in range(count)]
    ket = take(1 if group else 2 * len(pieces))
    (bra,) = take(1)
    (paired,) = take(1)
    crossed, handed = take(2), take(2)
    occ_ref, virt_ref = take(2)
    aliased = take(2) if group else None
    whole_ref, half_ref = take(2)
    own_ref, pair_ref, far_ref, send_ref = (take(1 + SPLIT[group]) for _ in range(4))
    (ket_all,) = (None,) if group else take(1)
    kv, bv, bt, t2, amps, given, ket_sem, bra_sem, out_sem = refs
    batch, block_width = bra.shape[2:]
    number, start, width = place_of(group, block_width)
    span = ket[0].shape[1] // 2
    half = whole_ref.shape[2] // 2
    part = span // SLICES
    here_row, here_col = lax.axis_index("row"), lax.axis_index("col")
    me = lax.axis_index("occ")
    pair = lax.bitwise_xor(here_col, 1)
    low = here_col < 2
    middle = jnp.logical_or(here_col == 1, here_col == 2)

    def bra_copies(source, home, slot):
        return [
            pltpu.make_async_copy(
                source.at[q, i, :, pl.ds(start, width)],
                bv.at[home, pl.ds(q * batch, batch), pl.ds(i * width, width)],
                bra_sem.at[slot, q, i],
            )
            for q in range(2)
            for i in range(2)
        ]

    def fetch(condition, source, home, slot):
        @pl.when(condition)
        def _():
            for copy in bra_copies(source, home, slot):
                copy.start()

    for copy in bra_copies(bra, here_col, 0) + bra_copies(paired, pair, 1):
        copy.start()
    for n in range(2):
        home = jnp.where(low, 2 + n, 1 - n)
        fetch(middle, crossed[n], home, 2 + n)
        fetch(jnp.logical_not(middle), handed[n], home, 2 + n)

    copies = [[] for _ in range(SLICES)]
    for n in range(SLICES):
        for j in range(2):
            columns = pl.ds(j * span + n * part, part)
            if group:
                moves = [(ket[0], 0, 8 * batch, 0)]
            else:
                moves = []
                for index, source in enumerate(ket):
                    q, place = divmod(index, len(pieces))
                    offset, begin, rows = pieces[place]
                    home = lax.bitwise_xor(here_row, offset) * (2 * batch) + q * batch + begin
                    moves.append((source, pl.multiple_of(home, 16), rows, index))
            for source, home, rows, index in moves:
                copy = pltpu.make_async_copy(
                    source.at[:, columns],
                    kv.at[pl.ds(home, rows), columns],
                    ket_sem.at[n, index, j],
                )
                copy.start()
                copies[n].append(copy)
    if group == 1:
        given_in = pltpu.make_async_copy(aliased[0], given, out_sem.at[2])
        given_in.start()
    for slot in range(4):
        for copy in bra_copies(bra, slot, slot):
            copy.wait()
    row_at = number * block_width + start
    first_at = here_row * (2 * half) + me * half + row_at
    first = virt_ref[:, pl.ds(pl.multiple_of(first_at, 128), width)]
    first = jnp.broadcast_to(first, (width, width)).T[:, :1]
    for d in range(4):
        bt[:, d * 2 * batch : (d + 1) * 2 * batch] = bv[d].T
    for n in range(SLICES):
        for copy in copies[n]:
            copy.wait()
        tile = [
            jnp.dot(
                bt[...],
                kv[:, j * span + n * part : j * span + (n + 1) * part],
                preferred_element_type=jnp.float32,
            )
            for j in range(2)
        ]
        second_at = pl.multiple_of(here_col * span + n * part, 128)
        second = virt_ref[:, pl.ds(second_at, part)]
        for i in range(2):
            for j in range(2):
                direct = tile[j][i * width : (i + 1) * width, :]
                exchange = tile[i][j * width : (j + 1) * width, :]
                denominator = ((occ_ref[i] + occ_ref[j]) - first) - second
                block = ((2.0 * direct - exchange) / denominator).astype(jnp.bfloat16)
                amps[i, j, :, n * part : (n + 1) * part] = block
                t2[
                    i * width : (i + 1) * width,
                    j * span + n * part : j * span + (n + 1) * part,
                ] = block
    at = pl.multiple_of(me * half + row_at, 16)
    outs = [
        pltpu.make_async_copy(amps, whole_ref.at[:, :, pl.ds(at, width), :], out_sem.at[0]),
        pltpu.make_async_copy(amps, half_ref.at[:, :, pl.ds(start, width), :], out_sem.at[1]),
    ]
    if group == 1:
        given_in.wait()
        at = pl.multiple_of((1 - me) * half, 16)
        outs.append(
            pltpu.make_async_copy(
                given, whole_ref.at[:, :, pl.ds(at, block_width), :], out_sem.at[2]
            )
        )
    if group == 0:
        outs.append(pltpu.make_async_copy(kv, ket_all, out_sem.at[2]))
    for copy in outs:
        copy.start()

    def share_of(home):
        rows = pl.ds(pl.multiple_of(home * (2 * batch), 16), 2 * batch)
        return lax.dot_general(
            kv[rows, :],
            t2[...],
            (((1,), (1,)), ((), ())),
            preferred_element_type=jnp.float32,
        )

    for n in range(2):
        share = share_of(jnp.where(low, 2 + n, n))
        for p, rows in enumerate(parts_of(group, batch)):
            far_ref[p][n] = share[rows]
            send_ref[p][n] = share[rows].astype(jnp.bfloat16)
    for out, home in ((pair_ref, pair), (own_ref, here_col)):
        share = share_of(home)
        for p, rows in enumerate(parts_of(group, batch)):
            out[p][...] = share[rows]
    for copy in outs:
        copy.wait()


def run_group(group, ket, pieces, bras, energies, held):
    _, _, batch, block_width = bras[0].shape
    _, _, width = place_of(group, block_width)
    span = ket[0].shape[1] // 2
    half = block_width * BLOCKS
    total = 8 * batch
    flops = 2 * 2 * total * 2 * width * 2 * span
    any_space = pl.BlockSpec(memory_space=pl.ANY)
    in_vmem = pl.BlockSpec(memory_space=pltpu.VMEM)
    in_hbm = pl.BlockSpec(memory_space=pltpu.HBM)
    ahead = len(ket) + len(bras) + 2
    count = 1 + SPLIT[group]
    rows = 2 * batch // count
    block = jax.ShapeDtypeStruct((rows, 2 * width), jnp.float32)
    far = jax.ShapeDtypeStruct((2, rows, 2 * width), jnp.float32)
    send = jax.ShapeDtypeStruct((2, rows, 2 * width), jnp.bfloat16)
    half_shape = (2, 2, block_width, span)
    results = pl.pallas_call(
        functools.partial(group_kernel, pieces, group),
        out_shape=(
            jax.ShapeDtypeStruct((2, 2, 2 * half, span), jnp.bfloat16),
            jax.ShapeDtypeStruct(half_shape, jnp.bfloat16),
        )
        + (block,) * (2 * count)
        + (far,) * count
        + (send,) * count
        + (() if group else (jax.ShapeDtypeStruct((total, 2 * span), jnp.bfloat16),)),
        in_specs=[in_hbm if group else any_space] * len(ket)
        + [any_space] * len(bras)
        + [pl.BlockSpec(memory_space=pltpu.SMEM), in_vmem]
        + [any_space] * len(held),
        out_specs=(any_space, any_space) + (in_vmem,) * (4 * count) + (() if group else (in_hbm,)),
        scratch_shapes=[
            pltpu.VMEM((total, 2 * span), jnp.bfloat16),
            pltpu.VMEM((4, 2 * batch, 2 * width), jnp.bfloat16),
            pltpu.VMEM((2 * width, total), jnp.bfloat16),
            pltpu.VMEM((2 * width, 2 * span), jnp.bfloat16),
            pltpu.VMEM((2, 2, width, span), jnp.bfloat16),
            pltpu.VMEM(half_shape if group == 1 else (2, 2, 16, 128), jnp.bfloat16),
            pltpu.SemaphoreType.DMA((SLICES, 2 * len(pieces), 2)),
            pltpu.SemaphoreType.DMA((4, 2, 2)),
            pltpu.SemaphoreType.DMA((3,)),
        ],
        input_output_aliases=({}, {ahead + 1: 0}, {ahead: 1, ahead + 1: 0})[group],
        compiler_params=pltpu.CompilerParams(vmem_limit_bytes=44 * 2**20),
        cost_estimate=pl.CostEstimate(
            flops=flops, bytes_accessed=total * 2 * span * 2, transcendentals=0
        ),
    )(*ket, *bras, *energies, *held)
    ends = [2 + n * count for n in range(5)]
    return results[:2], *(results[n : n + count] for n in ends[:4]), results[ends[4] :]


def pick_kernel(bra, kept_out, given_out):
    width = kept_out.shape[3]
    span = bra.shape[1] // 2
    me = lax.axis_index("occ")
    for side, out in ((1 - me, given_out), (me, kept_out)):
        for g in range(BLOCKS):
            for i in range(2):
                home = i * span + side * (span // 2) + g * width
                out[g, i] = bra[:, pl.ds(pl.multiple_of(home, 128), width)]


def pick(bra):
    batch, columns = bra.shape
    part = jax.ShapeDtypeStruct((BLOCKS, 2, batch, columns // 4 // BLOCKS), bra.dtype)
    return pl.pallas_call(
        pick_kernel,
        out_shape=(part, part),
        compiler_params=pltpu.CompilerParams(vmem_limit_bytes=16 * 2**20),
        cost_estimate=pl.CostEstimate(
            flops=0, bytes_accessed=4 * bra.size, transcendentals=0
        ),
    )(bra)


def close_kernel(*refs):
    other, _, *totals = refs[: 2 + 2 * GROUPS]
    amps, gamma, amp_buffer, gamma_buffer, sems, gamma_sems = refs[2 + 2 * GROUPS :]
    block_width = other.shape[2]
    half = block_width * BLOCKS
    batch = gamma.shape[0]
    me = lax.axis_index("occ")
    at = pl.multiple_of((1 - me) * half + half - block_width, 16)
    blocks = [(i, j) for i in range(2) for j in range(2)]
    reads = [
        pltpu.make_async_copy(other.at[i, j], amp_buffer.at[i, j], sems.at[0, i, j])
        for i, j in blocks
    ]
    writes = [
        pltpu.make_async_copy(
            amp_buffer.at[i, j], amps.at[i, j, pl.ds(at, block_width), :], sems.at[1, i, j]
        )
        for i, j in blocks
    ]
    for copy in reads:
        copy.start()
    for n in range(2 * GROUPS):
        side, group = divmod(n, GROUPS)
        number, start, width = place_of(group, block_width)
        at = number * block_width + start
        home = jnp.where(me == side, 0, half) + at
        columns = pl.ds(side * half + at, width)
        for i in range(2):
            gamma_buffer[:, i, columns] = totals[n][:batch, i * width : (i + 1) * width]
        writes.append(
            pltpu.make_async_copy(
                gamma_buffer.at[:, :, columns],
                gamma.at[:, :, pl.ds(pl.multiple_of(home, 128), width)],
                gamma_sems.at[n],
            )
        )
        if n < len(blocks):
            reads[n].wait()
            writes[n].start()
        writes[-1].start()
    for copy in writes:
        copy.wait()


def close(other, whole, kept, received):
    batch = received[0].shape[0]
    columns = whole.shape[2]
    any_space = pl.BlockSpec(memory_space=pl.ANY)
    in_vmem = pl.BlockSpec(memory_space=pltpu.VMEM)
    return pl.pallas_call(
        close_kernel,
        out_shape=(
            jax.ShapeDtypeStruct(whole.shape, whole.dtype),
            jax.ShapeDtypeStruct((batch, 2, columns), jnp.float32),
        ),
        in_specs=[any_space, any_space] + [in_vmem] * (2 * GROUPS),
        out_specs=(any_space, any_space),
        scratch_shapes=[
            pltpu.VMEM(other.shape, other.dtype),
            pltpu.VMEM((batch, 2, columns), jnp.float32),
            pltpu.SemaphoreType.DMA((2, 2, 2)),
            pltpu.SemaphoreType.DMA((2 * GROUPS,)),
        ],
        input_output_aliases={1: 0},
        compiler_params=pltpu.CompilerParams(vmem_limit_bytes=48 * 2**20),
        cost_estimate=pl.CostEstimate(
            flops=0, bytes_accessed=4 * other.size + 16 * batch * columns, transcendentals=0
        ),
    )(other, whole, *kept, *received)


def swap(x):
    return lax.ppermute(x, "occ", [(0, 1), (1, 0)])


def planar(x, offset):
    return lax.ppermute(x, "row", [(r, r ^ offset) for r in range(4)])


def pairs(x):
    return lax.ppermute(x, "col", [(0, 1), (1, 0), (2, 3), (3, 2)])


def across(x):
    return lax.ppermute(x, "col", [(1, 2), (2, 1)])


def outward(x):
    return lax.ppermute(x, "col", [(1, 0), (2, 3)])


def inward(x):
    return lax.ppermute(x, "col", [(0, 1), (3, 2)])


def tie(*arrays):
    return lax.optimization_barrier(arrays)


def planned(bra_factor, ket_factor, occ_energy, virt_energy):
    batch, _, a_width = bra_factor.shape
    b_width = ket_factor.shape[2]

    bra_kept, bra_given = pick(bra_factor.reshape(batch, 2 * a_width))
    ket_own = ket_factor.reshape(batch, 2 * b_width)
    bra = jnp.stack([bra_kept, swap(bra_given)], axis=1)
    ket_x = planar(ket_own, 1)
    ket_y = planar(ket_own, 2)
    cut = batch // 2
    pieces = ((0, 0, batch), (1, 0, batch), (2, 0, batch), (3, 0, cut), (3, cut, batch - cut))

    block, later = bra[0], bra[1]
    paired, crossed = pairs(block), [across(block)]
    ket_swapped = swap(ket_own)
    crossed.append(across(paired))
    handed = [outward(crossed[0])]
    ket_x, ket_y, crossed[1], handed[0], ket_swapped = tie(
        ket_x, ket_y, crossed[1], handed[0], ket_swapped
    )
    part_x, part_y, late_x, late_y = tie(ket_x[:cut], ket_y[cut:], ket_x, ket_y)
    far_y, far_x = planar(part_x, 2), planar(part_y, 1)
    late_y, far_y = tie(late_y, far_y)
    handed.append(outward(crossed[1]))
    crossed[1], early = tie(crossed[1], later)
    later_crossed = [across(early)]
    straight = [swap(late_x), swap(late_y)]
    handed[1], later_crossed[0], far_y, far_x = tie(handed[1], later_crossed[0], far_y, far_x)
    ket = [ket_own, ket_x, ket_y, far_y, far_x, ket_swapped, *straight, swap(far_y), swap(far_x)]
    handed[1], early, cross_first = tie(handed[1], later, later_crossed[0])
    later_paired = pairs(early)
    later_handed = [outward(cross_first)]
    first = [block, paired, *crossed, *handed]
    energies = (occ_energy, virt_energy[None, :])

    def up_cast(x):
        return x.astype(jnp.float32)

    near = lax.bitwise_and(lax.axis_index("col"), 1)

    def cross(far, one):
        return across((far + up_cast(one)).astype(jnp.bfloat16))

    def exchange(pair, two):
        theirs = lax.dynamic_index_in_dim(two, 1 - near, 0, keepdims=False)
        return pairs((pair + up_cast(theirs)).astype(jnp.bfloat16))

    def finish(own, two, three):
        ours = lax.dynamic_index_in_dim(two, near, 0, keepdims=False)
        return own + up_cast(ours) + up_cast(three)

    def finish_all(group, own, two, three):
        total = [finish(*part) for part in zip(own, two, three)]
        if not SPLIT[group]:
            total = [total[0][batch:], total[0][:batch]]
        return total[1], swap(total[0])

    (whole, mine), own0, pair0, far0, send0, (ket_all,) = run_group(
        0, ket, pieces, first, energies, ()
    )
    send_last, later_handed[0] = tie(send0[1], later_handed[0])
    one0 = [inward(send0[0]), inward(send_last)]
    own_last, later_paired = tie(own0[1], later_paired)
    own0 = (own0[0], own_last)
    later_crossed.append(across(later_paired))
    later_handed.append(outward(later_crossed[1]))
    other = swap(mine)
    two0 = [cross(far0[0], one0[0])]
    arrived = [later, later_paired, *later_crossed, *later_handed]
    two0[0], arrived[0] = tie(two0[0], arrived[0])
    (whole, mine), own1, pair1, far1, send1, _ = run_group(
        1, [ket_all], pieces, arrived, energies, (other, whole)
    )
    one1 = [inward(send) for send in send1]
    arrived = list(arrived)
    (whole, mine), own2, pair2, far2, send2, _ = run_group(
        2, [ket_all], pieces, arrived, energies, (mine, whole)
    )
    one2 = [inward(send) for send in send2]
    other = swap(mine)
    two0.append(cross(far0[1], one0[1]))
    two1 = [cross(*part) for part in zip(far1, one1)]
    two2 = [cross(*part) for part in zip(far2, one2)]
    one2[0], two0[1] = tie(one2[0], two0[1])
    three0 = [exchange(*part) for part in zip(pair0, two0)]
    three1 = [exchange(*part) for part in zip(pair1, two1)]
    three2 = [exchange(*part) for part in zip(pair2, two2)]
    ends = [
        finish_all(0, own0, two0, three0),
        finish_all(1, own1, two1, three1),
        finish_all(2, own2, two2, three2),
    ]
    return close(other, whole, [end[0] for end in ends], [end[1] for end in ends])


def solution(mesh):
    sizes = mesh.shape

    def on_device(bra_factor, ket_factor, occ_energy, virt_energy):
        fits = (
            sizes["occ"] == 2
            and sizes["row"] == 4
            and sizes["col"] == 4
            and bra_factor.shape[2] % 1024 == 0
            and ket_factor.shape[2] % 512 == 0
            and bra_factor.shape[0] % 128 == 0
        )
        body = planned if fits else general
        return body(bra_factor, ket_factor, occ_energy, virt_energy)

    placed = (P(("occ", "col"), None, "row"), P(("occ", "row"), None, "col"), P(), P())
    return jax.shard_map(
        on_device,
        mesh=mesh,
        in_specs=placed,
        out_specs=(P(None, None, "row", "col"), P(("occ", "col"), None, "row")),
        check_vma=False,
    )
```

```python
import functools

import jax
import jax.numpy as jnp
from jax import lax
from jax.experimental import pallas as pl
from jax.experimental.pallas import tpu as pltpu
from jax.sharding import PartitionSpec as P


def make_amplitudes(coulomb, occ_energy, virt_first, virt_second):
    denominator = (
        occ_energy[:, None, None, None]
        + occ_energy[None, :, None, None]
        - virt_first[None, None, :, None]
        - virt_second[None, None, None, :]
    )
    return ((2.0 * coulomb - jnp.transpose(coulomb, (1, 0, 2, 3))) / denominator).astype(
        jnp.bfloat16
    )


def general(bra_factor, ket_factor, occ_energy, virt_energy):
    a_width = bra_factor.shape[2]
    b_width = ket_factor.shape[2]
    ket_whole = lax.all_gather(ket_factor, "row", axis=0, tiled=True)
    row_index = lax.axis_index("row")
    col_index = lax.axis_index("col")
    virt_first = lax.dynamic_slice_in_dim(virt_energy, row_index * a_width, a_width, 0)
    virt_second = lax.dynamic_slice_in_dim(virt_energy, col_index * b_width, b_width, 0)
    partial_sum = jnp.einsum(
        "qia,qjb->ijab",
        lax.all_gather(bra_factor, "col", axis=0, tiled=True),
        ket_whole,
        preferred_element_type=jnp.float32,
    )
    batch_count = lax.axis_size("occ")
    pad_rows = (batch_count - a_width % batch_count) % batch_count
    padded = jnp.pad(partial_sum, ((0, 0), (0, 0), (0, pad_rows), (0, 0)))
    share_sum = lax.psum_scatter(padded, "occ", scatter_dimension=2, tiled=True)
    share_len = share_sum.shape[2]
    energy_padded = jnp.pad(virt_first, (0, pad_rows), constant_values=1.0)
    energy_share = lax.dynamic_slice_in_dim(
        energy_padded, lax.axis_index("occ") * share_len, share_len, 0
    )
    share_amps = make_amplitudes(share_sum, occ_energy, energy_share, virt_second)
    collected = lax.all_gather(share_amps, "occ", axis=2, tiled=True)
    amplitudes = collected[:, :, :a_width, :]
    gamma = lax.psum_scatter(
        jnp.einsum("ijab,qjb->qia", amplitudes, ket_whole, preferred_element_type=jnp.float32),
        "col",
        scatter_dimension=0,
        tiled=True,
    )
    return (amplitudes, gamma)


BLOCKS = 2
GROUPS = 3
SLICES = 4
SPLIT = (True, False, True)


def parts_of(group, batch):
    return (slice(batch, 2 * batch), slice(0, batch)) if SPLIT[group] else (slice(0, 2 * batch),)


def place_of(group, block):
    if group == 0:
        return 0, 0, block
    return 1, (group - 1) * (block // 2), block // 2


def group_kernel(pieces, group, *refs):
    refs = list(refs)
    take = lambda count: [refs.pop(0) for _ in range(count)]
    ket = take(1 if group else 2 * len(pieces))
    (bra,) = take(1)
    ups, downs = take(3), take(3)
    occ_ref, virt_ref = take(2)
    aliased = take(2) if group else None
    whole_ref, half_ref = take(2)
    own_ref, pair_ref, far_ref, send_ref = (take(1 + SPLIT[group]) for _ in range(4))
    (ket_all,) = (None,) if group else take(1)
    kv, bt, t2, amps, given, *tiles, ket_sem, bra_sem, out_sem = refs
    block_width, batch = bra.shape[2:]
    number, start, width = place_of(group, block_width)
    span = ket[0].shape[1] // 2
    half = whole_ref.shape[2] // 2
    part = span // SLICES
    here_row, here_col = lax.axis_index("row"), lax.axis_index("col")
    me = lax.axis_index("occ")
    pair = lax.bitwise_xor(here_col, 1)
    low = here_col < 2

    def bra_copies(source, home, slot):
        return [
            pltpu.make_async_copy(
                source.at[q, i, pl.ds(start, width), :],
                bt.at[
                    pl.ds(i * width, width),
                    pl.ds(pl.multiple_of((2 * home + q) * batch, 128), batch),
                ],
                bra_sem.at[slot, q, i],
            )
            for q in range(2)
            for i in range(2)
        ]

    def fetch(condition, source, home, slot):
        @pl.when(condition)
        def _():
            for copy in bra_copies(source, home, slot):
                copy.start()

    for copy in bra_copies(bra, here_col, 0):
        copy.start()
    for d in range(1, 4):
        home = lax.rem(here_col + 4 - d, 4)
        fetch(here_col >= d, ups[d - 1], home, d)
        fetch(here_col < d, downs[3 - d], home, d)

    copies = [[] for _ in range(SLICES)]
    for n in range(SLICES):
        for j in range(2):
            columns = pl.ds(j * span + n * part, part)
            if group:
                moves = [(ket[0], 0, 8 * batch, 0)]
            else:
                moves = []
                for index, source in enumerate(ket):
                    q, place = divmod(index, len(pieces))
                    offset, begin, rows = pieces[place]
                    home = lax.bitwise_xor(here_row, offset) * (2 * batch) + q * batch + begin
                    moves.append((source, pl.multiple_of(home, 16), rows, index))
            for source, home, rows, index in moves:
                copy = pltpu.make_async_copy(
                    source.at[:, columns],
                    kv.at[pl.ds(home, rows), columns],
                    ket_sem.at[n, index, j],
                )
                copy.start()
                copies[n].append(copy)
    if group == 1:
        given_in = pltpu.make_async_copy(aliased[0], given, out_sem.at[2])
        given_in.start()
    for slot in range(4):
        for copy in bra_copies(bra, slot, slot):
            copy.wait()
    row_at = number * block_width + start
    first_at = here_row * (2 * half) + me * half + row_at
    first = virt_ref[:, pl.ds(pl.multiple_of(first_at, 128), width)]
    first = jnp.broadcast_to(first, (width, width)).T[:, :1]

    def amplitudes_of(n):
        tile = tiles[n % 2]
        columns = slice(n * part, (n + 1) * part)
        second_at = pl.multiple_of(here_col * span + n * part, 128)
        second = virt_ref[:, pl.ds(second_at, part)]
        for i in range(2):
            for j in range(i, 2):
                inverse = 1.0 / (((occ_ref[i] + occ_ref[j]) - first) - second)
                for one, two in ((i, j), (j, i))[: 1 + (i != j)]:
                    direct = tile[two, one * width : (one + 1) * width, :]
                    exchange = tile[one, two * width : (two + 1) * width, :]
                    block = ((2.0 * direct - exchange) * inverse).astype(jnp.bfloat16)
                    amps[one, two, :, columns] = block
                    t2[
                        one * width : (one + 1) * width,
                        two * span + n * part : two * span + (n + 1) * part,
                    ] = block

    for n in range(SLICES):
        for copy in copies[n]:
            copy.wait()
        if n:
            amplitudes_of(n - 1)
        for j in range(2):
            tiles[n % 2][j] = jnp.dot(
                bt[...],
                kv[:, j * span + n * part : j * span + (n + 1) * part],
                preferred_element_type=jnp.float32,
            )
    amplitudes_of(SLICES - 1)
    at = pl.multiple_of(me * half + row_at, 16)
    outs = [
        pltpu.make_async_copy(amps, whole_ref.at[:, :, pl.ds(at, width), :], out_sem.at[0]),
        pltpu.make_async_copy(amps, half_ref.at[:, :, pl.ds(start, width), :], out_sem.at[1]),
    ]
    if group == 1:
        given_in.wait()
        at = pl.multiple_of((1 - me) * half, 16)
        outs.append(
            pltpu.make_async_copy(
                given, whole_ref.at[:, :, pl.ds(at, block_width), :], out_sem.at[2]
            )
        )
    if group == 0:
        outs.append(pltpu.make_async_copy(kv, ket_all, out_sem.at[2]))
    for copy in outs:
        copy.start()

    def share_of(home):
        rows = pl.ds(pl.multiple_of(home * (2 * batch), 16), 2 * batch)
        return lax.dot_general(
            kv[rows, :],
            t2[...],
            (((1,), (1,)), ((), ())),
            preferred_element_type=jnp.float32,
        )

    for n in range(2):
        share = share_of(jnp.where(low, 2 + n, n))
        for p, rows in enumerate(parts_of(group, batch)):
            far_ref[p][n] = share[rows]
            send_ref[p][n] = share[rows].astype(jnp.bfloat16)
    for out, home in ((pair_ref, pair), (own_ref, here_col)):
        share = share_of(home)
        for p, rows in enumerate(parts_of(group, batch)):
            out[p][...] = share[rows]
    for copy in outs:
        copy.wait()


def run_group(group, ket, pieces, bras, energies, held):
    _, _, block_width, batch = bras[0].shape
    _, _, width = place_of(group, block_width)
    span = ket[0].shape[1] // 2
    half = block_width * BLOCKS
    total = 8 * batch
    flops = 2 * 2 * total * 2 * width * 2 * span
    any_space = pl.BlockSpec(memory_space=pl.ANY)
    in_vmem = pl.BlockSpec(memory_space=pltpu.VMEM)
    in_hbm = pl.BlockSpec(memory_space=pltpu.HBM)
    ahead = len(ket) + len(bras) + 2
    count = 1 + SPLIT[group]
    rows = 2 * batch // count
    block = jax.ShapeDtypeStruct((rows, 2 * width), jnp.float32)
    far = jax.ShapeDtypeStruct((2, rows, 2 * width), jnp.float32)
    send = jax.ShapeDtypeStruct((2, rows, 2 * width), jnp.bfloat16)
    half_shape = (2, 2, block_width, span)
    results = pl.pallas_call(
        functools.partial(group_kernel, pieces, group),
        out_shape=(
            jax.ShapeDtypeStruct((2, 2, 2 * half, span), jnp.bfloat16),
            jax.ShapeDtypeStruct(half_shape, jnp.bfloat16),
        )
        + (block,) * (2 * count)
        + (far,) * count
        + (send,) * count
        + (() if group else (jax.ShapeDtypeStruct((total, 2 * span), jnp.bfloat16),)),
        in_specs=[in_hbm if group else any_space] * len(ket)
        + [any_space] * len(bras)
        + [pl.BlockSpec(memory_space=pltpu.SMEM), in_vmem]
        + [any_space] * len(held),
        out_specs=(any_space, any_space) + (in_vmem,) * (4 * count) + (() if group else (in_hbm,)),
        scratch_shapes=[
            pltpu.VMEM((total, 2 * span), jnp.bfloat16),
            pltpu.VMEM((2 * width, total), jnp.bfloat16),
            pltpu.VMEM((2 * width, 2 * span), jnp.bfloat16),
            pltpu.VMEM((2, 2, width, span), jnp.bfloat16),
            pltpu.VMEM(half_shape if group == 1 else (2, 2, 16, 128), jnp.bfloat16),
            pltpu.VMEM((2, 2 * width, span // SLICES), jnp.float32),
            pltpu.VMEM((2, 2 * width, span // SLICES), jnp.float32),
            pltpu.SemaphoreType.DMA((SLICES, 2 * len(pieces), 2)),
            pltpu.SemaphoreType.DMA((4, 2, 2)),
            pltpu.SemaphoreType.DMA((3,)),
        ],
        input_output_aliases=({}, {ahead + 1: 0}, {ahead: 1, ahead + 1: 0})[group],
        compiler_params=pltpu.CompilerParams(vmem_limit_bytes=44 * 2**20),
        cost_estimate=pl.CostEstimate(
            flops=flops, bytes_accessed=total * 2 * span * 2, transcendentals=0
        ),
    )(*ket, *bras, *energies, *held)
    ends = [2 + n * count for n in range(5)]
    return results[:2], *(results[n : n + count] for n in ends[:4]), results[ends[4] :]


def pick_kernel(bra, kept_out, given_out):
    width = kept_out.shape[2]
    span = bra.shape[1] // 2
    me = lax.axis_index("occ")
    for side, out in ((1 - me, given_out), (me, kept_out)):
        for g in range(BLOCKS):
            for i in range(2):
                home = i * span + side * (span // 2) + g * width
                out[g, i] = bra[:, pl.ds(pl.multiple_of(home, 128), width)].T


def pick(bra):
    batch, columns = bra.shape
    part = jax.ShapeDtypeStruct((BLOCKS, 2, columns // 4 // BLOCKS, batch), bra.dtype)
    return pl.pallas_call(
        pick_kernel,
        out_shape=(part, part),
        compiler_params=pltpu.CompilerParams(vmem_limit_bytes=16 * 2**20),
        cost_estimate=pl.CostEstimate(
            flops=0, bytes_accessed=4 * bra.size, transcendentals=0
        ),
    )(bra)


def close_kernel(*refs):
    other, _, *totals = refs[: 2 + 2 * GROUPS]
    amps, gamma, amp_buffer, gamma_buffer, sems, gamma_sems = refs[2 + 2 * GROUPS :]
    block_width = other.shape[2]
    half = block_width * BLOCKS
    batch = gamma.shape[0]
    me = lax.axis_index("occ")
    at = pl.multiple_of((1 - me) * half + half - block_width, 16)
    blocks = [(i, j) for i in range(2) for j in range(2)]
    reads = [
        pltpu.make_async_copy(other.at[i, j], amp_buffer.at[i, j], sems.at[0, i, j])
        for i, j in blocks
    ]
    writes = [
        pltpu.make_async_copy(
            amp_buffer.at[i, j], amps.at[i, j, pl.ds(at, block_width), :], sems.at[1, i, j]
        )
        for i, j in blocks
    ]
    for copy in reads:
        copy.start()
    for n in range(2 * GROUPS):
        side, group = divmod(n, GROUPS)
        number, start, width = place_of(group, block_width)
        at = number * block_width + start
        home = jnp.where(me == side, 0, half) + at
        columns = pl.ds(side * half + at, width)
        for i in range(2):
            gamma_buffer[:, i, columns] = totals[n][:batch, i * width : (i + 1) * width]
        writes.append(
            pltpu.make_async_copy(
                gamma_buffer.at[:, :, columns],
                gamma.at[:, :, pl.ds(pl.multiple_of(home, 128), width)],
                gamma_sems.at[n],
            )
        )
        if n < len(blocks):
            reads[n].wait()
            writes[n].start()
        writes[-1].start()
    for copy in writes:
        copy.wait()


def close(other, whole, kept, received):
    batch = received[0].shape[0]
    columns = whole.shape[2]
    any_space = pl.BlockSpec(memory_space=pl.ANY)
    in_vmem = pl.BlockSpec(memory_space=pltpu.VMEM)
    return pl.pallas_call(
        close_kernel,
        out_shape=(
            jax.ShapeDtypeStruct(whole.shape, whole.dtype),
            jax.ShapeDtypeStruct((batch, 2, columns), jnp.float32),
        ),
        in_specs=[any_space, any_space] + [in_vmem] * (2 * GROUPS),
        out_specs=(any_space, any_space),
        scratch_shapes=[
            pltpu.VMEM(other.shape, other.dtype),
            pltpu.VMEM((batch, 2, columns), jnp.float32),
            pltpu.SemaphoreType.DMA((2, 2, 2)),
            pltpu.SemaphoreType.DMA((2 * GROUPS,)),
        ],
        input_output_aliases={1: 0},
        compiler_params=pltpu.CompilerParams(vmem_limit_bytes=48 * 2**20),
        cost_estimate=pl.CostEstimate(
            flops=0, bytes_accessed=4 * other.size + 16 * batch * columns, transcendentals=0
        ),
    )(other, whole, *kept, *received)


def swap(x):
    return lax.ppermute(x, "occ", [(0, 1), (1, 0)])


def planar(x, offset):
    return lax.ppermute(x, "row", [(r, r ^ offset) for r in range(4)])


def hop_up(x, first):
    return lax.ppermute(x, "col", [(c, c + 1) for c in range(first, 3)])


def hop_down(x, first):
    return lax.ppermute(x, "col", [(3 - c, 2 - c) for c in range(first, 3)])


def pairs(x):
    return lax.ppermute(x, "col", [(0, 1), (1, 0), (2, 3), (3, 2)])


def across(x):
    return lax.ppermute(x, "col", [(1, 2), (2, 1)])


def outward(x):
    return lax.ppermute(x, "col", [(1, 0), (2, 3)])


def inward(x):
    return lax.ppermute(x, "col", [(0, 1), (3, 2)])


def tie(*arrays):
    return lax.optimization_barrier(arrays)


def planned(bra_factor, ket_factor, occ_energy, virt_energy):
    batch, _, a_width = bra_factor.shape
    b_width = ket_factor.shape[2]

    bra_kept, bra_given = pick(bra_factor.reshape(batch, 2 * a_width))
    ket_own = ket_factor.reshape(batch, 2 * b_width)
    bra = jnp.stack([bra_kept, swap(bra_given)], axis=1)
    ket_x = planar(ket_own, 1)
    ket_y = planar(ket_own, 2)
    cut = batch // 2
    pieces = ((0, 0, batch), (1, 0, batch), (2, 0, batch), (3, 0, cut), (3, cut, batch - cut))

    ups, downs = [[hop_up(bra[0], 0)], []], [[hop_down(bra[0], 0)], []]
    ket_swapped = swap(ket_own)
    ups[0].append(hop_up(ups[0][0], 1))
    downs[0].append(hop_down(downs[0][0], 1))
    ket_x, ket_y, ups[0][1], downs[0][1], ket_swapped = tie(
        ket_x, ket_y, ups[0][1], downs[0][1], ket_swapped
    )
    part_x, part_y, late_x, late_y = tie(ket_x[:cut], ket_y[cut:], ket_x, ket_y)
    far_y, far_x = planar(part_x, 2), planar(part_y, 1)
    late_y, far_y = tie(late_y, far_y)
    ups[0].append(hop_up(ups[0][1], 2))
    downs[0].append(hop_down(downs[0][1], 2))
    straight = [swap(late_x), swap(late_y)]
    ups[0][2], downs[0][2], far_y, far_x = tie(ups[0][2], downs[0][2], far_y, far_x)
    ket = [ket_own, ket_x, ket_y, far_y, far_x, ket_swapped, *straight, swap(far_y), swap(far_x)]
    ups[0][2], downs[0][2], block = tie(ups[0][2], downs[0][2], bra[1])
    ups[1].append(hop_up(block, 0))
    downs[1].append(hop_down(block, 0))
    energies = (occ_energy, virt_energy[None, :])

    def up_cast(x):
        return x.astype(jnp.float32)

    near = lax.bitwise_and(lax.axis_index("col"), 1)

    def cross(far, one):
        return across((far + up_cast(one)).astype(jnp.bfloat16))

    def exchange(pair, two):
        theirs = lax.dynamic_index_in_dim(two, 1 - near, 0, keepdims=False)
        return pairs((pair + up_cast(theirs)).astype(jnp.bfloat16))

    def finish(own, two, three):
        ours = lax.dynamic_index_in_dim(two, near, 0, keepdims=False)
        return own + up_cast(ours) + up_cast(three)

    def finish_all(group, own, two, three):
        total = [finish(*part) for part in zip(own, two, three)]
        if not SPLIT[group]:
            total = [total[0][batch:], total[0][:batch]]
        return total[1], swap(total[0])

    arrived = [bra[0], *ups[0], *downs[0]]
    (whole, mine), own0, pair0, far0, send0, (ket_all,) = run_group(
        0, ket, pieces, arrived, energies, ()
    )
    one0 = [inward(send) for send in send0]
    own_last, up, down = tie(own0[1], ups[1][0], downs[1][0])
    own0 = (own0[0], own_last)
    ups[1] += [hop_up(up, 1)]
    downs[1] += [hop_down(down, 1)]
    ups[1] += [hop_up(ups[1][1], 2)]
    downs[1] += [hop_down(downs[1][1], 2)]
    other = swap(mine)
    two0 = [cross(far0[0], one0[0])]
    arrived = [bra[1], *ups[1], *downs[1]]
    two0[0], arrived[0] = tie(two0[0], arrived[0])
    (whole, mine), own1, pair1, far1, send1, _ = run_group(
        1, [ket_all], pieces, arrived, energies, (other, whole)
    )
    one1 = [inward(send) for send in send1]
    arrived = list(arrived)
    (whole, mine), own2, pair2, far2, send2, _ = run_group(
        2, [ket_all], pieces, arrived, energies, (mine, whole)
    )
    one2 = [inward(send) for send in send2]
    other = swap(mine)
    two0.append(cross(far0[1], one0[1]))
    two1 = [cross(*part) for part in zip(far1, one1)]
    two2 = [cross(*part) for part in zip(far2, one2)]
    one2[0], two0[1] = tie(one2[0], two0[1])
    three0 = [exchange(*part) for part in zip(pair0, two0)]
    three1 = [exchange(*part) for part in zip(pair1, two1)]
    three2 = [exchange(*part) for part in zip(pair2, two2)]
    ends = [
        finish_all(0, own0, two0, three0),
        finish_all(1, own1, two1, three1),
        finish_all(2, own2, two2, three2),
    ]
    return close(other, whole, [end[0] for end in ends], [end[1] for end in ends])


def solution(mesh):
    sizes = mesh.shape

    def on_device(bra_factor, ket_factor, occ_energy, virt_energy):
        fits = (
            sizes["occ"] == 2
            and sizes["row"] == 4
            and sizes["col"] == 4
            and bra_factor.shape[2] % 1024 == 0
            and ket_factor.shape[2] % 512 == 0
            and bra_factor.shape[0] % 128 == 0
        )
        body = planned if fits else general
        return body(bra_factor, ket_factor, occ_energy, virt_energy)

    placed = (P(("occ", "col"), None, "row"), P(("occ", "row"), None, "col"), P(), P())
    return jax.shard_map(
        on_device,
        mesh=mesh,
        in_specs=placed,
        out_specs=(P(None, None, "row", "col"), P(("occ", "col"), None, "row")),
        check_vma=False,
    )
```

```python
import functools

import jax
import jax.numpy as jnp
from jax import lax
from jax.experimental import pallas as pl
from jax.experimental.pallas import tpu as pltpu
from jax.sharding import PartitionSpec as P


def make_amplitudes(coulomb, occ_energy, virt_first, virt_second):
    denominator = (
        occ_energy[:, None, None, None]
        + occ_energy[None, :, None, None]
        - virt_first[None, None, :, None]
        - virt_second[None, None, None, :]
    )
    return ((2.0 * coulomb - jnp.transpose(coulomb, (1, 0, 2, 3))) / denominator).astype(
        jnp.bfloat16
    )


def general(bra_factor, ket_factor, occ_energy, virt_energy):
    a_width = bra_factor.shape[2]
    b_width = ket_factor.shape[2]
    ket_whole = lax.all_gather(ket_factor, "row", axis=0, tiled=True)
    row_index = lax.axis_index("row")
    col_index = lax.axis_index("col")
    virt_first = lax.dynamic_slice_in_dim(virt_energy, row_index * a_width, a_width, 0)
    virt_second = lax.dynamic_slice_in_dim(virt_energy, col_index * b_width, b_width, 0)
    partial_sum = jnp.einsum(
        "qia,qjb->ijab",
        lax.all_gather(bra_factor, "col", axis=0, tiled=True),
        ket_whole,
        preferred_element_type=jnp.float32,
    )
    batch_count = lax.axis_size("occ")
    pad_rows = (batch_count - a_width % batch_count) % batch_count
    padded = jnp.pad(partial_sum, ((0, 0), (0, 0), (0, pad_rows), (0, 0)))
    share_sum = lax.psum_scatter(padded, "occ", scatter_dimension=2, tiled=True)
    share_len = share_sum.shape[2]
    energy_padded = jnp.pad(virt_first, (0, pad_rows), constant_values=1.0)
    energy_share = lax.dynamic_slice_in_dim(
        energy_padded, lax.axis_index("occ") * share_len, share_len, 0
    )
    share_amps = make_amplitudes(share_sum, occ_energy, energy_share, virt_second)
    collected = lax.all_gather(share_amps, "occ", axis=2, tiled=True)
    amplitudes = collected[:, :, :a_width, :]
    gamma = lax.psum_scatter(
        jnp.einsum("ijab,qjb->qia", amplitudes, ket_whole, preferred_element_type=jnp.float32),
        "col",
        scatter_dimension=0,
        tiled=True,
    )
    return (amplitudes, gamma)


GROUPS = 4
SLICES = 4
SPLIT = (False, False, False, True)


def parts_of(group, batch):
    return (slice(batch, 2 * batch), slice(0, batch)) if SPLIT[group] else (slice(0, 2 * batch),)


def group_kernel(pieces, group, *refs):
    refs = list(refs)
    take = lambda count: [refs.pop(0) for _ in range(count)]
    ket = take(1 if group else 2 * len(pieces))
    (bra,) = take(1)
    ups, downs = take(3), take(3)
    occ_ref, virt_ref = take(2)
    aliased = take((group % 2) + (group == 3) + (group > 0))
    whole_ref, half_ref = take(2)
    own_ref, pair_ref, far_ref, send_ref = (take(1 + SPLIT[group]) for _ in range(4))
    (ket_all,) = (None,) if group else take(1)
    kv, bt, t2, amps, given, *tiles, ket_sem, bra_sem, out_sem = refs
    batch = bra.shape[3]
    width = whole_ref.shape[2] // 2 // GROUPS
    start = max(group - 1, 0) * width
    span = ket[0].shape[1] // 2
    half = whole_ref.shape[2] // 2
    part = span // SLICES
    here_row, here_col = lax.axis_index("row"), lax.axis_index("col")
    me = lax.axis_index("occ")
    pair = lax.bitwise_xor(here_col, 1)
    low = here_col < 2

    def bra_copies(source, home, slot):
        return [
            pltpu.make_async_copy(
                source.at[q, i, pl.ds(start, width), :],
                bt.at[
                    pl.ds(i * width, width),
                    pl.ds(pl.multiple_of((2 * home + q) * batch, 128), batch),
                ],
                bra_sem.at[slot, q, i],
            )
            for q in range(2)
            for i in range(2)
        ]

    def fetch(condition, source, home, slot):
        @pl.when(condition)
        def _():
            for copy in bra_copies(source, home, slot):
                copy.start()

    for copy in bra_copies(bra, here_col, 0):
        copy.start()
    for d in range(1, 4):
        home = lax.rem(here_col + 4 - d, 4)
        fetch(here_col >= d, ups[d - 1], home, d)
        fetch(here_col < d, downs[3 - d], home, d)

    copies = [[] for _ in range(SLICES)]
    for n in range(SLICES):
        for j in range(2):
            columns = pl.ds(j * span + n * part, part)
            if group:
                moves = [(ket[0], 0, 8 * batch, 0)]
            else:
                moves = []
                for index, source in enumerate(ket):
                    q, place = divmod(index, len(pieces))
                    offset, begin, rows = pieces[place]
                    home = lax.bitwise_xor(here_row, offset) * (2 * batch) + q * batch + begin
                    moves.append((source, pl.multiple_of(home, 16), rows, index))
            for source, home, rows, index in moves:
                copy = pltpu.make_async_copy(
                    source.at[:, columns],
                    kv.at[pl.ds(home, rows), columns],
                    ket_sem.at[n, index, j],
                )
                copy.start()
                copies[n].append(copy)
    if group == 3:
        given_in = pltpu.make_async_copy(aliased[1], given, out_sem.at[2])
        given_in.start()
    for slot in range(4):
        for copy in bra_copies(bra, slot, slot):
            copy.wait()
    row_at = group * width
    first_at = here_row * (2 * half) + me * half + row_at
    first = virt_ref[:, pl.ds(pl.multiple_of(first_at, 128), width)]
    first = jnp.broadcast_to(first, (width, width)).T[:, :1]

    def amplitudes_of(n):
        tile = tiles[n % 2]
        columns = slice(n * part, (n + 1) * part)
        second_at = pl.multiple_of(here_col * span + n * part, 128)
        second = virt_ref[:, pl.ds(second_at, part)]
        for i in range(2):
            for j in range(i, 2):
                inverse = 1.0 / (((occ_ref[i] + occ_ref[j]) - first) - second)
                for one, two in ((i, j), (j, i))[: 1 + (i != j)]:
                    direct = tile[two, one * width : (one + 1) * width, :]
                    exchange = tile[one, two * width : (two + 1) * width, :]
                    block = ((2.0 * direct - exchange) * inverse).astype(jnp.bfloat16)
                    amps[one, two, :, columns] = block
                    t2[
                        one * width : (one + 1) * width,
                        two * span + n * part : two * span + (n + 1) * part,
                    ] = block

    for n in range(SLICES):
        for copy in copies[n]:
            copy.wait()
        if n:
            amplitudes_of(n - 1)
        for j in range(2):
            tiles[n % 2][j] = jnp.dot(
                bt[...],
                kv[:, j * span + n * part : j * span + (n + 1) * part],
                preferred_element_type=jnp.float32,
            )
    amplitudes_of(SLICES - 1)
    at = pl.multiple_of(me * half + row_at, 16)
    outs = [
        pltpu.make_async_copy(amps, whole_ref.at[:, :, pl.ds(at, width), :], out_sem.at[0]),
        pltpu.make_async_copy(
            amps, half_ref.at[:, :, pl.ds((group % 2) * width, width), :], out_sem.at[1]
        ),
    ]
    if group == 3:
        given_in.wait()
        at = pl.multiple_of((1 - me) * half, 16)
        outs.append(
            pltpu.make_async_copy(
                given, whole_ref.at[:, :, pl.ds(at, 2 * width), :], out_sem.at[2]
            )
        )
    if group == 0:
        outs.append(pltpu.make_async_copy(kv, ket_all, out_sem.at[2]))
    for copy in outs:
        copy.start()

    def share_of(home):
        rows = pl.ds(pl.multiple_of(home * (2 * batch), 16), 2 * batch)
        return lax.dot_general(
            kv[rows, :],
            t2[...],
            (((1,), (1,)), ((), ())),
            preferred_element_type=jnp.float32,
        )

    for n in range(2):
        share = share_of(jnp.where(low, 2 + n, n))
        for p, rows in enumerate(parts_of(group, batch)):
            far_ref[p][n] = share[rows]
            send_ref[p][n] = share[rows].astype(jnp.bfloat16)
    for out, home in ((pair_ref, pair), (own_ref, here_col)):
        share = share_of(home)
        for p, rows in enumerate(parts_of(group, batch)):
            out[p][...] = share[rows]
    for copy in outs:
        copy.wait()


def run_group(group, half, ket, pieces, bras, energies, held):
    batch = bras[0].shape[3]
    width = half // GROUPS
    span = ket[0].shape[1] // 2
    total = 8 * batch
    flops = 2 * 2 * total * 2 * width * 2 * span
    any_space = pl.BlockSpec(memory_space=pl.ANY)
    in_vmem = pl.BlockSpec(memory_space=pltpu.VMEM)
    in_hbm = pl.BlockSpec(memory_space=pltpu.HBM)
    ahead = len(ket) + len(bras) + 2
    count = 1 + SPLIT[group]
    rows = 2 * batch // count
    block = jax.ShapeDtypeStruct((rows, 2 * width), jnp.float32)
    far = jax.ShapeDtypeStruct((2, rows, 2 * width), jnp.float32)
    send = jax.ShapeDtypeStruct((2, rows, 2 * width), jnp.bfloat16)
    half_shape = (2, 2, 2 * width, span)
    results = pl.pallas_call(
        functools.partial(group_kernel, pieces, group),
        out_shape=(
            jax.ShapeDtypeStruct((2, 2, 2 * half, span), jnp.bfloat16),
            jax.ShapeDtypeStruct(half_shape, jnp.bfloat16),
        )
        + (block,) * (2 * count)
        + (far,) * count
        + (send,) * count
        + (() if group else (jax.ShapeDtypeStruct((total, 2 * span), jnp.bfloat16),)),
        in_specs=[in_hbm if group else any_space] * len(ket)
        + [any_space] * len(bras)
        + [pl.BlockSpec(memory_space=pltpu.SMEM), in_vmem]
        + [any_space] * len(held),
        out_specs=(any_space, any_space) + (in_vmem,) * (4 * count) + (() if group else (in_hbm,)),
        scratch_shapes=[
            pltpu.VMEM((total, 2 * span), jnp.bfloat16),
            pltpu.VMEM((2 * width, total), jnp.bfloat16),
            pltpu.VMEM((2 * width, 2 * span), jnp.bfloat16),
            pltpu.VMEM((2, 2, width, span), jnp.bfloat16),
            pltpu.VMEM(half_shape if group == 3 else (2, 2, 16, 128), jnp.bfloat16),
            pltpu.VMEM((2, 2 * width, span // SLICES), jnp.float32),
            pltpu.VMEM((2, 2 * width, span // SLICES), jnp.float32),
            pltpu.SemaphoreType.DMA((SLICES, 2 * len(pieces), 2)),
            pltpu.SemaphoreType.DMA((4, 2, 2)),
            pltpu.SemaphoreType.DMA((3,)),
        ],
        input_output_aliases={
            **({ahead: 1} if group % 2 else {}),
            **({ahead + len(held) - 1: 0} if group else {}),
        },
        compiler_params=pltpu.CompilerParams(vmem_limit_bytes=44 * 2**20),
        cost_estimate=pl.CostEstimate(
            flops=flops, bytes_accessed=total * 2 * span * 2, transcendentals=0
        ),
    )(*ket, *bras, *energies, *held)
    ends = [2 + n * count for n in range(5)]
    return results[:2], *(results[n : n + count] for n in ends[:4]), results[ends[4] :]


def pick_kernel(bra, *outs):
    span = bra.shape[1] // 2
    half = span // 2
    me = lax.axis_index("occ")
    for side, blocks in ((1 - me, outs[2:]), (me, outs[:2])):
        for out, start in zip(blocks, (0, half // GROUPS)):
            width = out.shape[1]
            for i in range(2):
                home = pl.multiple_of(i * span + side * half + start, 128)
                out[i] = bra[:, pl.ds(home, width)].T


def pick(bra):
    batch, columns = bra.shape
    half = columns // 4
    blocks = tuple(
        jax.ShapeDtypeStruct((2, rows, batch), bra.dtype)
        for rows in (half // GROUPS, half - half // GROUPS)
    )
    return pl.pallas_call(
        pick_kernel,
        out_shape=blocks * 2,
        compiler_params=pltpu.CompilerParams(vmem_limit_bytes=16 * 2**20),
        cost_estimate=pl.CostEstimate(
            flops=0, bytes_accessed=4 * bra.size, transcendentals=0
        ),
    )(bra)


def close_kernel(*refs):
    other, _, *totals = refs[: 2 + 2 * GROUPS]
    amps, gamma, amp_buffer, gamma_buffer, sems, gamma_sems = refs[2 + 2 * GROUPS :]
    half = 2 * other.shape[2]
    width = half // GROUPS
    batch = gamma.shape[0]
    me = lax.axis_index("occ")
    at = pl.multiple_of((1 - me) * half + half // 2, 16)
    blocks = [(i, j) for i in range(2) for j in range(2)]
    reads = [
        pltpu.make_async_copy(other.at[i, j], amp_buffer.at[i, j], sems.at[0, i, j])
        for i, j in blocks
    ]
    writes = [
        pltpu.make_async_copy(
            amp_buffer.at[i, j], amps.at[i, j, pl.ds(at, half // 2), :], sems.at[1, i, j]
        )
        for i, j in blocks
    ]
    for copy in reads:
        copy.start()
    for n in range(2 * GROUPS):
        side, group = divmod(n, GROUPS)
        at = group * width
        home = jnp.where(me == side, 0, half) + at
        columns = pl.ds(side * half + at, width)
        for i in range(2):
            gamma_buffer[:, i, columns] = totals[n][:batch, i * width : (i + 1) * width]
        writes.append(
            pltpu.make_async_copy(
                gamma_buffer.at[:, :, columns],
                gamma.at[:, :, pl.ds(pl.multiple_of(home, 128), width)],
                gamma_sems.at[n],
            )
        )
        if n < len(blocks):
            reads[n].wait()
            writes[n].start()
        writes[-1].start()
    for copy in writes:
        copy.wait()


def close(other, whole, kept, received):
    batch = received[0].shape[0]
    columns = whole.shape[2]
    any_space = pl.BlockSpec(memory_space=pl.ANY)
    in_vmem = pl.BlockSpec(memory_space=pltpu.VMEM)
    return pl.pallas_call(
        close_kernel,
        out_shape=(
            jax.ShapeDtypeStruct(whole.shape, whole.dtype),
            jax.ShapeDtypeStruct((batch, 2, columns), jnp.float32),
        ),
        in_specs=[any_space, any_space] + [in_vmem] * (2 * GROUPS),
        out_specs=(any_space, any_space),
        scratch_shapes=[
            pltpu.VMEM(other.shape, other.dtype),
            pltpu.VMEM((batch, 2, columns), jnp.float32),
            pltpu.SemaphoreType.DMA((2, 2, 2)),
            pltpu.SemaphoreType.DMA((2 * GROUPS,)),
        ],
        input_output_aliases={1: 0},
        compiler_params=pltpu.CompilerParams(vmem_limit_bytes=48 * 2**20),
        cost_estimate=pl.CostEstimate(
            flops=0, bytes_accessed=4 * other.size + 16 * batch * columns, transcendentals=0
        ),
    )(other, whole, *kept, *received)


def swap(x):
    return lax.ppermute(x, "occ", [(0, 1), (1, 0)])


def planar(x, offset):
    return lax.ppermute(x, "row", [(r, r ^ offset) for r in range(4)])


def hop_up(x, first):
    return lax.ppermute(x, "col", [(c, c + 1) for c in range(first, 3)])


def hop_down(x, first):
    return lax.ppermute(x, "col", [(3 - c, 2 - c) for c in range(first, 3)])


def pairs(x):
    return lax.ppermute(x, "col", [(0, 1), (1, 0), (2, 3), (3, 2)])


def across(x):
    return lax.ppermute(x, "col", [(1, 2), (2, 1)])


def outward(x):
    return lax.ppermute(x, "col", [(1, 0), (2, 3)])


def inward(x):
    return lax.ppermute(x, "col", [(0, 1), (3, 2)])


def tie(*arrays):
    return lax.optimization_barrier(arrays)


def planned(bra_factor, ket_factor, occ_energy, virt_energy):
    batch, _, a_width = bra_factor.shape
    b_width = ket_factor.shape[2]

    half = a_width // 2
    ket_own, bra_factor = tie(ket_factor.reshape(batch, 2 * b_width), bra_factor)
    *bra_kept, first_given, later_given = pick(bra_factor.reshape(batch, 2 * a_width))
    ket_x = planar(ket_own, 1)
    ket_y = planar(ket_own, 2)
    cut = batch // 2
    pieces = ((0, 0, batch), (1, 0, batch), (2, 0, batch), (3, 0, cut), (3, cut, batch - cut))

    bra = [jnp.stack([kept, swap(given)]) for kept, given in zip(bra_kept, (first_given, later_given))]
    ups, downs = [[hop_up(bra[0], 0)], []], [[hop_down(bra[0], 0)], []]
    for step in (1, 2):
        ups[0].append(hop_up(ups[0][step - 1], step))
        downs[0].append(hop_down(downs[0][step - 1], step))
    ket_x, ket_y, ket_late, ups[0][2], downs[0][2], block = tie(
        ket_x, ket_y, ket_own, ups[0][2], downs[0][2], bra[1]
    )
    ups[1].append(hop_up(block, 0))
    downs[1].append(hop_down(block, 0))
    ket_swapped = swap(ket_late)
    part_x, part_y, late_x, late_y = tie(ket_x[:cut], ket_y[cut:], ket_x, ket_y)
    far_y, far_x = planar(part_x, 2), planar(part_y, 1)
    late_y, far_y = tie(late_y, far_y)
    straight = [swap(late_x), swap(late_y)]
    ket = [ket_own, ket_x, ket_y, far_y, far_x, ket_swapped, *straight, swap(far_y), swap(far_x)]
    ups[1].append(hop_up(ups[1][0], 1))
    downs[1].append(hop_down(downs[1][0], 1))
    energies = (occ_energy, virt_energy[None, :])

    def up_cast(x):
        return x.astype(jnp.float32)

    near = lax.bitwise_and(lax.axis_index("col"), 1)

    def cross(far, one):
        return across((far + up_cast(one)).astype(jnp.bfloat16))

    def exchange(pair, two):
        theirs = lax.dynamic_index_in_dim(two, 1 - near, 0, keepdims=False)
        return pairs((pair + up_cast(theirs)).astype(jnp.bfloat16))

    def finish(own, two, three):
        ours = lax.dynamic_index_in_dim(two, near, 0, keepdims=False)
        return own + up_cast(ours) + up_cast(three)

    def finish_all(group, own, two, three):
        total = [finish(*part) for part in zip(own, two, three)]
        if not SPLIT[group]:
            total = [total[0][batch:], total[0][:batch]]
        return total[1], swap(total[0])

    whole = ket_all = mine = other = None
    own, pair, far, one, two = ({} for _ in range(5))

    def begin(group, arrived):
        nonlocal whole, ket_all, mine
        held = ([mine] if group % 2 else []) + ([other] if group == 3 else [])
        held += [whole] if group else []
        (whole, mine), own[group], pair[group], far[group], send, gathered = run_group(
            group, half, [ket_all] if group else ket, pieces, arrived, energies, held
        )
        ket_all = ket_all if group else gathered[0]
        send = list(send)
        if group == 0:
            send[0], ups[1][1], downs[1][1] = tie(send[0], ups[1][1], downs[1][1])
        if group == 3:
            send[0], one[2][0], two[1][0] = tie(send[0], one[2][0], two[1][0])
        one[group] = [inward(part) for part in send]

    def middle(group):
        two[group] = [cross(*part) for part in zip(far[group], one[group])]

    begin(0, [bra[0], *ups[0], *downs[0]])
    middle(0)
    last_own, up, down = tie(own[0][0], ups[1][1], downs[1][1])
    own[0] = (last_own,)
    ups[1].append(hop_up(up, 2))
    downs[1].append(hop_down(down, 2))
    arrived = [bra[1], *ups[1], *downs[1]]
    one[0][0], arrived[0] = tie(one[0][0], arrived[0])
    begin(1, arrived)
    other = swap(mine)
    two[0][0], arrived[0] = tie(two[0][0], arrived[0])
    begin(2, arrived)
    middle(1)
    one[1][0], arrived[0] = tie(one[1][0], arrived[0])
    begin(3, arrived)
    middle(2)
    middle(3)
    one[3][0], two[1][0] = tie(one[3][0], two[1][0])
    one[3][1], mine = tie(one[3][1], mine)
    other = swap(mine)
    ends = []
    for group in range(GROUPS):
        three = [exchange(*part) for part in zip(pair[group], two[group])]
        ends.append(finish_all(group, own[group], two[group], three))
    return close(other, whole, [end[0] for end in ends], [end[1] for end in ends])


def solution(mesh):
    sizes = mesh.shape

    def on_device(bra_factor, ket_factor, occ_energy, virt_energy):
        fits = (
            sizes["occ"] == 2
            and sizes["row"] == 4
            and sizes["col"] == 4
            and bra_factor.shape[2] % (256 * GROUPS) == 0
            and ket_factor.shape[2] % 512 == 0
            and bra_factor.shape[0] % 128 == 0
        )
        body = planned if fits else general
        return body(bra_factor, ket_factor, occ_energy, virt_energy)

    placed = (P(("occ", "col"), None, "row"), P(("occ", "row"), None, "col"), P(), P())
    return jax.shard_map(
        on_device,
        mesh=mesh,
        in_specs=placed,
        out_specs=(P(None, None, "row", "col"), P(("occ", "col"), None, "row")),
        check_vma=False,
    )
```

```python
import functools

import jax
import jax.numpy as jnp
from jax import lax
from jax.experimental import pallas as pl
from jax.experimental.pallas import tpu as pltpu
from jax.sharding import PartitionSpec as P


def make_amplitudes(coulomb, occ_energy, virt_first, virt_second):
    denominator = (
        occ_energy[:, None, None, None]
        + occ_energy[None, :, None, None]
        - virt_first[None, None, :, None]
        - virt_second[None, None, None, :]
    )
    return ((2.0 * coulomb - jnp.transpose(coulomb, (1, 0, 2, 3))) / denominator).astype(
        jnp.bfloat16
    )


def general(bra_factor, ket_factor, occ_energy, virt_energy):
    a_width = bra_factor.shape[2]
    b_width = ket_factor.shape[2]
    ket_whole = lax.all_gather(ket_factor, "row", axis=0, tiled=True)
    row_index = lax.axis_index("row")
    col_index = lax.axis_index("col")
    virt_first = lax.dynamic_slice_in_dim(virt_energy, row_index * a_width, a_width, 0)
    virt_second = lax.dynamic_slice_in_dim(virt_energy, col_index * b_width, b_width, 0)
    partial_sum = jnp.einsum(
        "qia,qjb->ijab",
        lax.all_gather(bra_factor, "col", axis=0, tiled=True),
        ket_whole,
        preferred_element_type=jnp.float32,
    )
    batch_count = lax.axis_size("occ")
    pad_rows = (batch_count - a_width % batch_count) % batch_count
    padded = jnp.pad(partial_sum, ((0, 0), (0, 0), (0, pad_rows), (0, 0)))
    share_sum = lax.psum_scatter(padded, "occ", scatter_dimension=2, tiled=True)
    share_len = share_sum.shape[2]
    energy_padded = jnp.pad(virt_first, (0, pad_rows), constant_values=1.0)
    energy_share = lax.dynamic_slice_in_dim(
        energy_padded, lax.axis_index("occ") * share_len, share_len, 0
    )
    share_amps = make_amplitudes(share_sum, occ_energy, energy_share, virt_second)
    collected = lax.all_gather(share_amps, "occ", axis=2, tiled=True)
    amplitudes = collected[:, :, :a_width, :]
    gamma = lax.psum_scatter(
        jnp.einsum("ijab,qjb->qia", amplitudes, ket_whole, preferred_element_type=jnp.float32),
        "col",
        scatter_dimension=0,
        tiled=True,
    )
    return (amplitudes, gamma)


BLOCKS = 2
GROUPS = 3
SLICES = 4
SPLIT = (True, False, True)


def parts_of(group, batch):
    return (slice(batch, 2 * batch), slice(0, batch)) if SPLIT[group] else (slice(0, 2 * batch),)


def place_of(group, block):
    if group == 0:
        return 0, 0, block
    return 1, (group - 1) * (block // 2), block // 2


def group_kernel(pieces, group, *refs):
    refs = list(refs)
    take = lambda count: [refs.pop(0) for _ in range(count)]
    ket = take(1 if group else 2 * len(pieces))
    (bra,) = take(1)
    ups, downs = take(3), take(3)
    occ_ref, virt_ref = take(2)
    aliased = take(2) if group else None
    whole_ref, half_ref = take(2)
    own_ref, pair_ref, far_ref, send_ref = (take(1 + SPLIT[group]) for _ in range(4))
    (ket_all,) = (None,) if group else take(1)
    kv, bt, t2, amps, given, *tiles, ket_sem, bra_sem, out_sem = refs
    block_width, batch = bra.shape[2:]
    number, start, width = place_of(group, block_width)
    span = ket[0].shape[1] // 2
    half = whole_ref.shape[2] // 2
    part = span // SLICES
    here_row, here_col = lax.axis_index("row"), lax.axis_index("col")
    me = lax.axis_index("occ")
    pair = lax.bitwise_xor(here_col, 1)
    low = here_col < 2

    def bra_copies(source, home, slot):
        return [
            pltpu.make_async_copy(
                source.at[q, i, pl.ds(start, width), :],
                bt.at[
                    pl.ds(i * width, width),
                    pl.ds(pl.multiple_of((2 * home + q) * batch, 128), batch),
                ],
                bra_sem.at[slot, q, i],
            )
            for q in range(2)
            for i in range(2)
        ]

    def fetch(condition, source, home, slot):
        @pl.when(condition)
        def _():
            for copy in bra_copies(source, home, slot):
                copy.start()

    for copy in bra_copies(bra, here_col, 0):
        copy.start()
    for d in range(1, 4):
        home = lax.rem(here_col + 4 - d, 4)
        fetch(here_col >= d, ups[d - 1], home, d)
        fetch(here_col < d, downs[3 - d], home, d)

    copies = [[] for _ in range(SLICES)]
    for n in range(SLICES):
        for j in range(2):
            columns = pl.ds(j * span + n * part, part)
            if group:
                moves = [(ket[0], 0, 8 * batch, 0)]
            else:
                moves = []
                for index, source in enumerate(ket):
                    q, place = divmod(index, len(pieces))
                    offset, begin, rows = pieces[place]
                    home = lax.bitwise_xor(here_row, offset) * (2 * batch) + q * batch + begin
                    moves.append((source, pl.multiple_of(home, 16), rows, index))
            for source, home, rows, index in moves:
                copy = pltpu.make_async_copy(
                    source.at[:, columns],
                    kv.at[pl.ds(home, rows), columns],
                    ket_sem.at[n, index, j],
                )
                copy.start()
                copies[n].append(copy)
    if group == 1:
        given_in = pltpu.make_async_copy(aliased[0], given, out_sem.at[2])
        given_in.start()
    for slot in range(4):
        for copy in bra_copies(bra, slot, slot):
            copy.wait()
    row_at = number * block_width + start
    first_at = here_row * (2 * half) + me * half + row_at
    first = virt_ref[:, pl.ds(pl.multiple_of(first_at, 128), width)]
    first = jnp.broadcast_to(first, (width, width)).T[:, :1]

    def amplitudes_of(n):
        tile = tiles[n % 2]
        columns = slice(n * part, (n + 1) * part)
        second_at = pl.multiple_of(here_col * span + n * part, 128)
        second = virt_ref[:, pl.ds(second_at, part)]
        for i in range(2):
            for j in range(i, 2):
                inverse = 1.0 / (((occ_ref[i] + occ_ref[j]) - first) - second)
                for one, two in ((i, j), (j, i))[: 1 + (i != j)]:
                    direct = tile[two, one * width : (one + 1) * width, :]
                    exchange = tile[one, two * width : (two + 1) * width, :]
                    block = ((2.0 * direct - exchange) * inverse).astype(jnp.bfloat16)
                    amps[one, two, :, columns] = block
                    t2[
                        one * width : (one + 1) * width,
                        two * span + n * part : two * span + (n + 1) * part,
                    ] = block

    for n in range(SLICES):
        for copy in copies[n]:
            copy.wait()
        if n:
            amplitudes_of(n - 1)
        for j in range(2):
            tiles[n % 2][j] = jnp.dot(
                bt[...],
                kv[:, j * span + n * part : j * span + (n + 1) * part],
                preferred_element_type=jnp.float32,
            )
    amplitudes_of(SLICES - 1)
    at = pl.multiple_of(me * half + row_at, 16)
    outs = [
        pltpu.make_async_copy(amps, whole_ref.at[:, :, pl.ds(at, width), :], out_sem.at[0]),
        pltpu.make_async_copy(amps, half_ref.at[:, :, pl.ds(start, width), :], out_sem.at[1]),
    ]
    if group == 1:
        given_in.wait()
        at = pl.multiple_of((1 - me) * half, 16)
        outs.append(
            pltpu.make_async_copy(
                given, whole_ref.at[:, :, pl.ds(at, block_width), :], out_sem.at[2]
            )
        )
    if group == 0:
        outs.append(pltpu.make_async_copy(kv, ket_all, out_sem.at[2]))
    for copy in outs:
        copy.start()

    def share_of(home):
        rows = pl.ds(pl.multiple_of(home * (2 * batch), 16), 2 * batch)
        return lax.dot_general(
            kv[rows, :],
            t2[...],
            (((1,), (1,)), ((), ())),
            preferred_element_type=jnp.float32,
        )

    for n in range(2):
        share = share_of(jnp.where(low, 2 + n, n))
        for p, rows in enumerate(parts_of(group, batch)):
            far_ref[p][n] = share[rows]
            send_ref[p][n] = share[rows].astype(jnp.bfloat16)
    for out, home in ((pair_ref, pair), (own_ref, here_col)):
        share = share_of(home)
        for p, rows in enumerate(parts_of(group, batch)):
            out[p][...] = share[rows]
    for copy in outs:
        copy.wait()


def run_group(group, ket, pieces, bras, energies, held):
    _, _, block_width, batch = bras[0].shape
    _, _, width = place_of(group, block_width)
    span = ket[0].shape[1] // 2
    half = block_width * BLOCKS
    total = 8 * batch
    flops = 2 * 2 * total * 2 * width * 2 * span
    any_space = pl.BlockSpec(memory_space=pl.ANY)
    in_vmem = pl.BlockSpec(memory_space=pltpu.VMEM)
    in_hbm = pl.BlockSpec(memory_space=pltpu.HBM)
    ahead = len(ket) + len(bras) + 2
    count = 1 + SPLIT[group]
    rows = 2 * batch // count
    block = jax.ShapeDtypeStruct((rows, 2 * width), jnp.float32)
    far = jax.ShapeDtypeStruct((2, rows, 2 * width), jnp.float32)
    send = jax.ShapeDtypeStruct((2, rows, 2 * width), jnp.bfloat16)
    half_shape = (2, 2, block_width, span)
    results = pl.pallas_call(
        functools.partial(group_kernel, pieces, group),
        out_shape=(
            jax.ShapeDtypeStruct((2, 2, 2 * half, span), jnp.bfloat16),
            jax.ShapeDtypeStruct(half_shape, jnp.bfloat16),
        )
        + (block,) * (2 * count)
        + (far,) * count
        + (send,) * count
        + (() if group else (jax.ShapeDtypeStruct((total, 2 * span), jnp.bfloat16),)),
        in_specs=[in_hbm if group else any_space] * len(ket)
        + [any_space] * len(bras)
        + [pl.BlockSpec(memory_space=pltpu.SMEM), in_vmem]
        + [any_space] * len(held),
        out_specs=(any_space, any_space) + (in_vmem,) * (4 * count) + (() if group else (in_hbm,)),
        scratch_shapes=[
            pltpu.VMEM((total, 2 * span), jnp.bfloat16),
            pltpu.VMEM((2 * width, total), jnp.bfloat16),
            pltpu.VMEM((2 * width, 2 * span), jnp.bfloat16),
            pltpu.VMEM((2, 2, width, span), jnp.bfloat16),
            pltpu.VMEM(half_shape if group == 1 else (2, 2, 16, 128), jnp.bfloat16),
            pltpu.VMEM((2, 2 * width, span // SLICES), jnp.float32),
            pltpu.VMEM((2, 2 * width, span // SLICES), jnp.float32),
            pltpu.SemaphoreType.DMA((SLICES, 2 * len(pieces), 2)),
            pltpu.SemaphoreType.DMA((4, 2, 2)),
            pltpu.SemaphoreType.DMA((3,)),
        ],
        input_output_aliases=({}, {ahead + 1: 0}, {ahead: 1, ahead + 1: 0})[group],
        compiler_params=pltpu.CompilerParams(vmem_limit_bytes=44 * 2**20),
        cost_estimate=pl.CostEstimate(
            flops=flops, bytes_accessed=total * 2 * span * 2, transcendentals=0
        ),
    )(*ket, *bras, *energies, *held)
    ends = [2 + n * count for n in range(5)]
    return results[:2], *(results[n : n + count] for n in ends[:4]), results[ends[4] :]


def pick_kernel(bra, kept_out, given_out):
    width = kept_out.shape[2]
    span = bra.shape[1] // 2
    me = lax.axis_index("occ")
    for side, out in ((1 - me, given_out), (me, kept_out)):
        for g in range(BLOCKS):
            for i in range(2):
                home = i * span + side * (span // 2) + g * width
                out[g, i] = bra[:, pl.ds(pl.multiple_of(home, 128), width)].T


def pick(bra):
    batch, columns = bra.shape
    part = jax.ShapeDtypeStruct((BLOCKS, 2, columns // 4 // BLOCKS, batch), bra.dtype)
    return pl.pallas_call(
        pick_kernel,
        out_shape=(part, part),
        compiler_params=pltpu.CompilerParams(vmem_limit_bytes=16 * 2**20),
        cost_estimate=pl.CostEstimate(
            flops=0, bytes_accessed=4 * bra.size, transcendentals=0
        ),
    )(bra)


def close_kernel(*refs):
    other, _, *totals = refs[: 2 + 2 * GROUPS]
    amps, gamma, amp_buffer, gamma_buffer, sems, gamma_sems = refs[2 + 2 * GROUPS :]
    block_width = other.shape[2]
    half = block_width * BLOCKS
    batch = gamma.shape[0]
    me = lax.axis_index("occ")
    at = pl.multiple_of((1 - me) * half + half - block_width, 16)
    blocks = [(i, j) for i in range(2) for j in range(2)]
    reads = [
        pltpu.make_async_copy(other.at[i, j], amp_buffer.at[i, j], sems.at[0, i, j])
        for i, j in blocks
    ]
    writes = [
        pltpu.make_async_copy(
            amp_buffer.at[i, j], amps.at[i, j, pl.ds(at, block_width), :], sems.at[1, i, j]
        )
        for i, j in blocks
    ]
    for copy in reads:
        copy.start()
    for n in range(2 * GROUPS):
        side, group = divmod(n, GROUPS)
        number, start, width = place_of(group, block_width)
        at = number * block_width + start
        home = jnp.where(me == side, 0, half) + at
        columns = pl.ds(side * half + at, width)
        for i in range(2):
            gamma_buffer[:, i, columns] = totals[n][:batch, i * width : (i + 1) * width]
        writes.append(
            pltpu.make_async_copy(
                gamma_buffer.at[:, :, columns],
                gamma.at[:, :, pl.ds(pl.multiple_of(home, 128), width)],
                gamma_sems.at[n],
            )
        )
        if n < len(blocks):
            reads[n].wait()
            writes[n].start()
        writes[-1].start()
    for copy in writes:
        copy.wait()


def close(other, whole, kept, received):
    batch = received[0].shape[0]
    columns = whole.shape[2]
    any_space = pl.BlockSpec(memory_space=pl.ANY)
    in_vmem = pl.BlockSpec(memory_space=pltpu.VMEM)
    return pl.pallas_call(
        close_kernel,
        out_shape=(
            jax.ShapeDtypeStruct(whole.shape, whole.dtype),
            jax.ShapeDtypeStruct((batch, 2, columns), jnp.float32),
        ),
        in_specs=[any_space, any_space] + [in_vmem] * (2 * GROUPS),
        out_specs=(any_space, any_space),
        scratch_shapes=[
            pltpu.VMEM(other.shape, other.dtype),
            pltpu.VMEM((batch, 2, columns), jnp.float32),
            pltpu.SemaphoreType.DMA((2, 2, 2)),
            pltpu.SemaphoreType.DMA((2 * GROUPS,)),
        ],
        input_output_aliases={1: 0},
        compiler_params=pltpu.CompilerParams(vmem_limit_bytes=48 * 2**20),
        cost_estimate=pl.CostEstimate(
            flops=0, bytes_accessed=4 * other.size + 16 * batch * columns, transcendentals=0
        ),
    )(other, whole, *kept, *received)


def swap(x):
    return lax.ppermute(x, "occ", [(0, 1), (1, 0)])


def planar(x, offset):
    return lax.ppermute(x, "row", [(r, r ^ offset) for r in range(4)])


def hop_up(x, first):
    return lax.ppermute(x, "col", [(c, c + 1) for c in range(first, 3)])


def hop_down(x, first):
    return lax.ppermute(x, "col", [(3 - c, 2 - c) for c in range(first, 3)])


def pairs(x):
    return lax.ppermute(x, "col", [(0, 1), (1, 0), (2, 3), (3, 2)])


def across(x):
    return lax.ppermute(x, "col", [(1, 2), (2, 1)])


def outward(x):
    return lax.ppermute(x, "col", [(1, 0), (2, 3)])


def inward(x):
    return lax.ppermute(x, "col", [(0, 1), (3, 2)])


def tie(*arrays):
    return lax.optimization_barrier(arrays)


def planned(bra_factor, ket_factor, occ_energy, virt_energy):
    batch, _, a_width = bra_factor.shape
    b_width = ket_factor.shape[2]

    bra_kept, bra_given = pick(bra_factor.reshape(batch, 2 * a_width))
    ket_own = ket_factor.reshape(batch, 2 * b_width)
    bra = jnp.stack([bra_kept, swap(bra_given)], axis=1)
    ket_x = planar(ket_own, 1)
    ket_y = planar(ket_own, 2)
    cut = batch // 2
    pieces = ((0, 0, batch), (1, 0, batch), (2, 0, batch), (3, 0, cut), (3, cut, batch - cut))

    ups, downs = [[hop_up(bra[0], 0)], []], [[hop_down(bra[0], 0)], []]
    ket_swapped = swap(ket_own)
    ups[0].append(hop_up(ups[0][0], 1))
    downs[0].append(hop_down(downs[0][0], 1))
    ket_x, ket_y, ups[0][1], downs[0][1], ket_swapped = tie(
        ket_x, ket_y, ups[0][1], downs[0][1], ket_swapped
    )
    part_x, part_y, late_x, late_y = tie(ket_x[:cut], ket_y[cut:], ket_x, ket_y)
    far_y, far_x = planar(part_x, 2), planar(part_y, 1)
    late_y, far_y = tie(late_y, far_y)
    ups[0].append(hop_up(ups[0][1], 2))
    downs[0].append(hop_down(downs[0][1], 2))
    straight = [swap(late_x), swap(late_y)]
    ups[0][2], downs[0][2], far_y, far_x = tie(ups[0][2], downs[0][2], far_y, far_x)
    ket = [ket_own, ket_x, ket_y, far_y, far_x, ket_swapped, *straight, swap(far_y), swap(far_x)]
    ups[0][2], downs[0][2], block = tie(ups[0][2], downs[0][2], bra[1])
    ups[1].append(hop_up(block, 0))
    downs[1].append(hop_down(block, 0))
    energies = (occ_energy, virt_energy[None, :])

    def up_cast(x):
        return x.astype(jnp.float32)

    near = lax.bitwise_and(lax.axis_index("col"), 1)

    def cross(far, one):
        return across((far + up_cast(one)).astype(jnp.bfloat16))

    def exchange(pair, two):
        theirs = lax.dynamic_index_in_dim(two, 1 - near, 0, keepdims=False)
        return pairs((pair + up_cast(theirs)).astype(jnp.bfloat16))

    def finish(own, two, three):
        ours = lax.dynamic_index_in_dim(two, near, 0, keepdims=False)
        return own + up_cast(ours) + up_cast(three)

    def finish_all(group, own, two, three):
        total = [finish(*part) for part in zip(own, two, three)]
        if not SPLIT[group]:
            total = [total[0][batch:], total[0][:batch]]
        return total[1], swap(total[0])

    arrived = [bra[0], *ups[0], *downs[0]]
    (whole, mine), own0, pair0, far0, send0, (ket_all,) = run_group(
        0, ket, pieces, arrived, energies, ()
    )
    one0 = [inward(send) for send in send0]
    own_last, up, down = tie(own0[1], ups[1][0], downs[1][0])
    own0 = (own0[0], own_last)
    ups[1] += [hop_up(up, 1)]
    downs[1] += [hop_down(down, 1)]
    ups[1] += [hop_up(ups[1][1], 2)]
    downs[1] += [hop_down(downs[1][1], 2)]
    other = swap(mine)
    two0 = [cross(far0[0], one0[0])]
    arrived = [bra[1], *ups[1], *downs[1]]
    two0[0], arrived[0] = tie(two0[0], arrived[0])
    (whole, mine), own1, pair1, far1, send1, _ = run_group(
        1, [ket_all], pieces, arrived, energies, (other, whole)
    )
    one1 = [inward(send) for send in send1]
    arrived = list(arrived)
    (whole, mine), own2, pair2, far2, send2, _ = run_group(
        2, [ket_all], pieces, arrived, energies, (mine, whole)
    )
    one2 = [inward(send) for send in send2]
    two0.append(cross(far0[1], one0[1]))
    two1 = [cross(*part) for part in zip(far1, one1)]
    two2 = [cross(*part) for part in zip(far2, one2)]
    one2[1], mine = tie(one2[1], mine)
    other = swap(mine)
    one2[0], two0[1] = tie(one2[0], two0[1])
    three0 = [exchange(*part) for part in zip(pair0, two0)]
    three1 = [exchange(*part) for part in zip(pair1, two1)]
    three1[0], two2[0] = tie(three1[0], two2[0])
    three2 = [exchange(*part) for part in zip(pair2, two2)]
    ends = [
        finish_all(0, own0, two0, three0),
        finish_all(1, own1, two1, three1),
        finish_all(2, own2, two2, three2),
    ]
    return close(other, whole, [end[0] for end in ends], [end[1] for end in ends])


def solution(mesh):
    sizes = mesh.shape

    def on_device(bra_factor, ket_factor, occ_energy, virt_energy):
        fits = (
            sizes["occ"] == 2
            and sizes["row"] == 4
            and sizes["col"] == 4
            and bra_factor.shape[2] % 1024 == 0
            and ket_factor.shape[2] % 512 == 0
            and bra_factor.shape[0] % 128 == 0
        )
        body = planned if fits else general
        return body(bra_factor, ket_factor, occ_energy, virt_energy)

    placed = (P(("occ", "col"), None, "row"), P(("occ", "row"), None, "col"), P(), P())
    return jax.shard_map(
        on_device,
        mesh=mesh,
        in_specs=placed,
        out_specs=(P(None, None, "row", "col"), P(("occ", "col"), None, "row")),
        check_vma=False,
    )
```

```python
import functools

import jax
import jax.numpy as jnp
from jax import lax
from jax.experimental import pallas as pl
from jax.experimental.pallas import tpu as pltpu
from jax.sharding import PartitionSpec as P


def make_amplitudes(coulomb, occ_energy, virt_first, virt_second):
    denominator = (
        occ_energy[:, None, None, None]
        + occ_energy[None, :, None, None]
        - virt_first[None, None, :, None]
        - virt_second[None, None, None, :]
    )
    return ((2.0 * coulomb - jnp.transpose(coulomb, (1, 0, 2, 3))) / denominator).astype(
        jnp.bfloat16
    )


def general(bra_factor, ket_factor, occ_energy, virt_energy):
    a_width = bra_factor.shape[2]
    b_width = ket_factor.shape[2]
    ket_whole = lax.all_gather(ket_factor, "row", axis=0, tiled=True)
    row_index = lax.axis_index("row")
    col_index = lax.axis_index("col")
    virt_first = lax.dynamic_slice_in_dim(virt_energy, row_index * a_width, a_width, 0)
    virt_second = lax.dynamic_slice_in_dim(virt_energy, col_index * b_width, b_width, 0)
    partial_sum = jnp.einsum(
        "qia,qjb->ijab",
        lax.all_gather(bra_factor, "col", axis=0, tiled=True),
        ket_whole,
        preferred_element_type=jnp.float32,
    )
    batch_count = lax.axis_size("occ")
    pad_rows = (batch_count - a_width % batch_count) % batch_count
    padded = jnp.pad(partial_sum, ((0, 0), (0, 0), (0, pad_rows), (0, 0)))
    share_sum = lax.psum_scatter(padded, "occ", scatter_dimension=2, tiled=True)
    share_len = share_sum.shape[2]
    energy_padded = jnp.pad(virt_first, (0, pad_rows), constant_values=1.0)
    energy_share = lax.dynamic_slice_in_dim(
        energy_padded, lax.axis_index("occ") * share_len, share_len, 0
    )
    share_amps = make_amplitudes(share_sum, occ_energy, energy_share, virt_second)
    collected = lax.all_gather(share_amps, "occ", axis=2, tiled=True)
    amplitudes = collected[:, :, :a_width, :]
    gamma = lax.psum_scatter(
        jnp.einsum("ijab,qjb->qia", amplitudes, ket_whole, preferred_element_type=jnp.float32),
        "col",
        scatter_dimension=0,
        tiled=True,
    )
    return (amplitudes, gamma)


BLOCKS = 2
GROUPS = 3
SLICES = 4
SPLIT = (True, False, True)


def parts_of(group, batch):
    return (slice(batch, 2 * batch), slice(0, batch)) if SPLIT[group] else (slice(0, 2 * batch),)


def place_of(group, block):
    if group == 0:
        return 0, 0, block
    return 1, (group - 1) * (block // 2), block // 2


def group_kernel(pieces, group, *refs):
    refs = list(refs)
    take = lambda count: [refs.pop(0) for _ in range(count)]
    ket = take(1 if group else 2 * len(pieces))
    (bra,) = take(1)
    ups, downs = take(3), take(3)
    occ_ref, virt_ref = take(2)
    aliased = take(2) if group else None
    whole_ref, half_ref = take(2)
    own_ref, pair_ref, far_ref, send_ref = (take(1 + SPLIT[group]) for _ in range(4))
    (ket_all,) = (None,) if group else take(1)
    kv, bt, t2, amps, given, *tiles, ket_sem, bra_sem, out_sem = refs
    block_width, batch = bra.shape[2:]
    number, start, width = place_of(group, block_width)
    span = ket[0].shape[1] // 2
    half = whole_ref.shape[2] // 2
    part = span // SLICES
    here_row, here_col = lax.axis_index("row"), lax.axis_index("col")
    me = lax.axis_index("occ")
    pair = lax.bitwise_xor(here_col, 1)
    low = here_col < 2

    def bra_copies(source, home, slot):
        return [
            pltpu.make_async_copy(
                source.at[q, i, pl.ds(start, width), :],
                bt.at[
                    pl.ds(i * width, width),
                    pl.ds(pl.multiple_of((2 * home + q) * batch, 128), batch),
                ],
                bra_sem.at[slot, q, i],
            )
            for q in range(2)
            for i in range(2)
        ]

    def fetch(condition, source, home, slot):
        @pl.when(condition)
        def _():
            for copy in bra_copies(source, home, slot):
                copy.start()

    for copy in bra_copies(bra, here_col, 0):
        copy.start()
    for d in range(1, 4):
        home = lax.rem(here_col + 4 - d, 4)
        fetch(here_col >= d, ups[d - 1], home, d)
        fetch(here_col < d, downs[3 - d], home, d)

    copies = [[] for _ in range(SLICES)]
    for n in range(SLICES):
        for j in range(2):
            columns = pl.ds(j * span + n * part, part)
            if group:
                moves = [(ket[0], 0, 8 * batch, 0)]
            else:
                moves = []
                for index, source in enumerate(ket):
                    q, place = divmod(index, len(pieces))
                    offset, begin, rows = pieces[place]
                    home = lax.bitwise_xor(here_row, offset) * (2 * batch) + q * batch + begin
                    moves.append((source, pl.multiple_of(home, 16), rows, index))
            for source, home, rows, index in moves:
                copy = pltpu.make_async_copy(
                    source.at[:, columns],
                    kv.at[pl.ds(home, rows), columns],
                    ket_sem.at[n, index, j],
                )
                copy.start()
                copies[n].append(copy)
    if group == 1:
        given_in = pltpu.make_async_copy(aliased[0], given, out_sem.at[2])
        given_in.start()
    for slot in range(4):
        for copy in bra_copies(bra, slot, slot):
            copy.wait()
    row_at = number * block_width + start
    first_at = here_row * (2 * half) + me * half + row_at
    first = virt_ref[:, pl.ds(pl.multiple_of(first_at, 128), width)]
    first = jnp.broadcast_to(first, (width, width)).T[:, :1]

    def amplitudes_of(n):
        tile = tiles[n % 2]
        columns = slice(n * part, (n + 1) * part)
        second_at = pl.multiple_of(here_col * span + n * part, 128)
        second = virt_ref[:, pl.ds(second_at, part)]
        for i in range(2):
            for j in range(i, 2):
                inverse = 1.0 / (((occ_ref[i] + occ_ref[j]) - first) - second)
                for one, two in ((i, j), (j, i))[: 1 + (i != j)]:
                    direct = tile[two, one * width : (one + 1) * width, :]
                    exchange = tile[one, two * width : (two + 1) * width, :]
                    block = ((2.0 * direct - exchange) * inverse).astype(jnp.bfloat16)
                    amps[one, two, :, columns] = block
                    t2[
                        one * width : (one + 1) * width,
                        two * span + n * part : two * span + (n + 1) * part,
                    ] = block

    for n in range(SLICES):
        for copy in copies[n]:
            copy.wait()
        if n:
            amplitudes_of(n - 1)
        for j in range(2):
            tiles[n % 2][j] = jnp.dot(
                bt[...],
                kv[:, j * span + n * part : j * span + (n + 1) * part],
                preferred_element_type=jnp.float32,
            )
    amplitudes_of(SLICES - 1)
    at = pl.multiple_of(me * half + row_at, 16)
    outs = [
        pltpu.make_async_copy(amps, whole_ref.at[:, :, pl.ds(at, width), :], out_sem.at[0]),
        pltpu.make_async_copy(amps, half_ref.at[:, :, pl.ds(start, width), :], out_sem.at[1]),
    ]
    if group == 1:
        given_in.wait()
        at = pl.multiple_of((1 - me) * half, 16)
        outs.append(
            pltpu.make_async_copy(
                given, whole_ref.at[:, :, pl.ds(at, block_width), :], out_sem.at[2]
            )
        )
    if group == 0:
        outs.append(pltpu.make_async_copy(kv, ket_all, out_sem.at[2]))
    for copy in outs:
        copy.start()

    def share_of(home):
        rows = pl.ds(pl.multiple_of(home * (2 * batch), 16), 2 * batch)
        return lax.dot_general(
            kv[rows, :],
            t2[...],
            (((1,), (1,)), ((), ())),
            preferred_element_type=jnp.float32,
        )

    for n in range(2):
        share = share_of(jnp.where(low, 2 + n, n))
        for p, rows in enumerate(parts_of(group, batch)):
            far_ref[p][n] = share[rows]
            send_ref[p][n] = share[rows].astype(jnp.bfloat16)
    for out, home in ((pair_ref, pair), (own_ref, here_col)):
        share = share_of(home)
        for p, rows in enumerate(parts_of(group, batch)):
            out[p][...] = share[rows]
    for copy in outs:
        copy.wait()


def run_group(group, ket, pieces, bras, energies, held):
    _, _, block_width, batch = bras[0].shape
    _, _, width = place_of(group, block_width)
    span = ket[0].shape[1] // 2
    half = block_width * BLOCKS
    total = 8 * batch
    flops = 2 * 2 * total * 2 * width * 2 * span
    any_space = pl.BlockSpec(memory_space=pl.ANY)
    in_vmem = pl.BlockSpec(memory_space=pltpu.VMEM)
    in_hbm = pl.BlockSpec(memory_space=pltpu.HBM)
    ahead = len(ket) + len(bras) + 2
    count = 1 + SPLIT[group]
    rows = 2 * batch // count
    block = jax.ShapeDtypeStruct((rows, 2 * width), jnp.float32)
    far = jax.ShapeDtypeStruct((2, rows, 2 * width), jnp.float32)
    send = jax.ShapeDtypeStruct((2, rows, 2 * width), jnp.bfloat16)
    half_shape = (2, 2, block_width, span)
    results = pl.pallas_call(
        functools.partial(group_kernel, pieces, group),
        out_shape=(
            jax.ShapeDtypeStruct((2, 2, 2 * half, span), jnp.bfloat16),
            jax.ShapeDtypeStruct(half_shape, jnp.bfloat16),
        )
        + (block,) * (2 * count)
        + (far,) * count
        + (send,) * count
        + (() if group else (jax.ShapeDtypeStruct((total, 2 * span), jnp.bfloat16),)),
        in_specs=[in_hbm if group else any_space] * len(ket)
        + [any_space] * len(bras)
        + [pl.BlockSpec(memory_space=pltpu.SMEM), in_vmem]
        + [any_space] * len(held),
        out_specs=(any_space, any_space) + (in_vmem,) * (4 * count) + (() if group else (in_hbm,)),
        scratch_shapes=[
            pltpu.VMEM((total, 2 * span), jnp.bfloat16),
            pltpu.VMEM((2 * width, total), jnp.bfloat16),
            pltpu.VMEM((2 * width, 2 * span), jnp.bfloat16),
            pltpu.VMEM((2, 2, width, span), jnp.bfloat16),
            pltpu.VMEM(half_shape if group == 1 else (2, 2, 16, 128), jnp.bfloat16),
            pltpu.VMEM((2, 2 * width, span // SLICES), jnp.float32),
            pltpu.VMEM((2, 2 * width, span // SLICES), jnp.float32),
            pltpu.SemaphoreType.DMA((SLICES, 2 * len(pieces), 2)),
            pltpu.SemaphoreType.DMA((4, 2, 2)),
            pltpu.SemaphoreType.DMA((3,)),
        ],
        input_output_aliases=({}, {ahead + 1: 0}, {ahead: 1, ahead + 1: 0})[group],
        compiler_params=pltpu.CompilerParams(vmem_limit_bytes=44 * 2**20),
        cost_estimate=pl.CostEstimate(
            flops=flops, bytes_accessed=total * 2 * span * 2, transcendentals=0
        ),
    )(*ket, *bras, *energies, *held)
    ends = [2 + n * count for n in range(5)]
    return results[:2], *(results[n : n + count] for n in ends[:4]), results[ends[4] :]


def pick_kernel(bra, kept_out, given_out):
    width = kept_out.shape[2]
    span = bra.shape[1] // 2
    me = lax.axis_index("occ")
    for side, out in ((1 - me, given_out), (me, kept_out)):
        for g in range(BLOCKS):
            for i in range(2):
                home = i * span + side * (span // 2) + g * width
                out[g, i] = bra[:, pl.ds(pl.multiple_of(home, 128), width)].T


def pick(bra):
    batch, columns = bra.shape
    part = jax.ShapeDtypeStruct((BLOCKS, 2, columns // 4 // BLOCKS, batch), bra.dtype)
    return pl.pallas_call(
        pick_kernel,
        out_shape=(part, part),
        compiler_params=pltpu.CompilerParams(vmem_limit_bytes=16 * 2**20),
        cost_estimate=pl.CostEstimate(
            flops=0, bytes_accessed=4 * bra.size, transcendentals=0
        ),
    )(bra)


def close_kernel(*refs):
    other, _, *totals = refs[: 2 + 2 * GROUPS]
    amps, gamma, amp_buffer, gamma_buffer, sems, gamma_sems = refs[2 + 2 * GROUPS :]
    block_width = other.shape[2]
    half = block_width * BLOCKS
    batch = gamma.shape[0]
    me = lax.axis_index("occ")
    at = pl.multiple_of((1 - me) * half + half - block_width, 16)
    blocks = [(i, j) for i in range(2) for j in range(2)]
    reads = [
        pltpu.make_async_copy(other.at[i, j], amp_buffer.at[i, j], sems.at[0, i, j])
        for i, j in blocks
    ]
    writes = [
        pltpu.make_async_copy(
            amp_buffer.at[i, j], amps.at[i, j, pl.ds(at, block_width), :], sems.at[1, i, j]
        )
        for i, j in blocks
    ]
    for copy in reads:
        copy.start()
    for n in range(2 * GROUPS):
        side, group = divmod(n, GROUPS)
        number, start, width = place_of(group, block_width)
        at = number * block_width + start
        home = jnp.where(me == side, 0, half) + at
        columns = pl.ds(side * half + at, width)
        for i in range(2):
            gamma_buffer[:, i, columns] = totals[n][:batch, i * width : (i + 1) * width]
        writes.append(
            pltpu.make_async_copy(
                gamma_buffer.at[:, :, columns],
                gamma.at[:, :, pl.ds(pl.multiple_of(home, 128), width)],
                gamma_sems.at[n],
            )
        )
        if n < len(blocks):
            reads[n].wait()
            writes[n].start()
        writes[-1].start()
    for copy in writes:
        copy.wait()


def close(other, whole, kept, received):
    batch = received[0].shape[0]
    columns = whole.shape[2]
    any_space = pl.BlockSpec(memory_space=pl.ANY)
    in_vmem = pl.BlockSpec(memory_space=pltpu.VMEM)
    return pl.pallas_call(
        close_kernel,
        out_shape=(
            jax.ShapeDtypeStruct(whole.shape, whole.dtype),
            jax.ShapeDtypeStruct((batch, 2, columns), jnp.float32),
        ),
        in_specs=[any_space, any_space] + [in_vmem] * (2 * GROUPS),
        out_specs=(any_space, any_space),
        scratch_shapes=[
            pltpu.VMEM(other.shape, other.dtype),
            pltpu.VMEM((batch, 2, columns), jnp.float32),
            pltpu.SemaphoreType.DMA((2, 2, 2)),
            pltpu.SemaphoreType.DMA((2 * GROUPS,)),
        ],
        input_output_aliases={1: 0},
        compiler_params=pltpu.CompilerParams(vmem_limit_bytes=48 * 2**20),
        cost_estimate=pl.CostEstimate(
            flops=0, bytes_accessed=4 * other.size + 16 * batch * columns, transcendentals=0
        ),
    )(other, whole, *kept, *received)


def swap(x):
    return lax.ppermute(x, "occ", [(0, 1), (1, 0)])


def planar(x, offset):
    return lax.ppermute(x, "row", [(r, r ^ offset) for r in range(4)])


def hop_up(x, first):
    return lax.ppermute(x, "col", [(c, c + 1) for c in range(first, 3)])


def hop_down(x, first):
    return lax.ppermute(x, "col", [(3 - c, 2 - c) for c in range(first, 3)])


def pairs(x):
    return lax.ppermute(x, "col", [(0, 1), (1, 0), (2, 3), (3, 2)])


def across(x):
    return lax.ppermute(x, "col", [(1, 2), (2, 1)])


def outward(x):
    return lax.ppermute(x, "col", [(1, 0), (2, 3)])


def inward(x):
    return lax.ppermute(x, "col", [(0, 1), (3, 2)])


def tie(*arrays):
    return lax.optimization_barrier(arrays)


def planned(bra_factor, ket_factor, occ_energy, virt_energy):
    batch, _, a_width = bra_factor.shape
    b_width = ket_factor.shape[2]

    bra_kept, bra_given = pick(bra_factor.reshape(batch, 2 * a_width))
    ket_own = ket_factor.reshape(batch, 2 * b_width)
    bra = jnp.stack([bra_kept, swap(bra_given)], axis=1)
    ket_x = planar(ket_own, 1)
    ket_y = planar(ket_own, 2)
    cut = batch // 2
    pieces = ((0, 0, batch), (1, 0, batch), (2, 0, batch), (3, 0, cut), (3, cut, batch - cut))

    ups, downs = [[hop_up(bra[0], 0)], []], [[hop_down(bra[0], 0)], []]
    ket_swapped = swap(ket_own)
    ups[0].append(hop_up(ups[0][0], 1))
    downs[0].append(hop_down(downs[0][0], 1))
    ket_x, ket_y, ups[0][1], downs[0][1], ket_swapped = tie(
        ket_x, ket_y, ups[0][1], downs[0][1], ket_swapped
    )
    part_x, part_y, late_x, late_y = tie(ket_x[:cut], ket_y[cut:], ket_x, ket_y)
    far_y, far_x = planar(part_x, 2), planar(part_y, 1)
    late_y, far_y = tie(late_y, far_y)
    ups[0].append(hop_up(ups[0][1], 2))
    downs[0].append(hop_down(downs[0][1], 2))
    straight = [swap(late_x), swap(late_y)]
    ups[0][2], downs[0][2], far_y, far_x = tie(ups[0][2], downs[0][2], far_y, far_x)
    ket = [ket_own, ket_x, ket_y, far_y, far_x, ket_swapped, *straight, swap(far_y), swap(far_x)]
    ups[0][2], downs[0][2], block = tie(ups[0][2], downs[0][2], bra[1])
    ups[1].append(hop_up(block, 0))
    downs[1].append(hop_down(block, 0))
    energies = (occ_energy, virt_energy[None, :])

    def up_cast(x):
        return x.astype(jnp.float32)

    near = lax.bitwise_and(lax.axis_index("col"), 1)

    def cross(far, one):
        return across((far + up_cast(one)).astype(jnp.bfloat16))

    def exchange(pair, two):
        theirs = lax.dynamic_index_in_dim(two, 1 - near, 0, keepdims=False)
        return pairs((pair + up_cast(theirs)).astype(jnp.bfloat16))

    def finish(own, two, three):
        ours = lax.dynamic_index_in_dim(two, near, 0, keepdims=False)
        return own + up_cast(ours) + up_cast(three)

    def finish_all(group, own, two, three):
        total = [finish(*part) for part in zip(own, two, three)]
        if not SPLIT[group]:
            total = [total[0][batch:], total[0][:batch]]
        return total[1], swap(total[0])

    arrived = [bra[0], *ups[0], *downs[0]]
    (whole, mine), own0, pair0, far0, send0, (ket_all,) = run_group(
        0, ket, pieces, arrived, energies, ()
    )
    one0 = [inward(send) for send in send0]
    own_last, up, down = tie(own0[1], ups[1][0], downs[1][0])
    own0 = (own0[0], own_last)
    ups[1] += [hop_up(up, 1)]
    downs[1] += [hop_down(down, 1)]
    ups[1] += [hop_up(ups[1][1], 2)]
    downs[1] += [hop_down(downs[1][1], 2)]
    other = swap(mine)
    two0 = [cross(far0[0], one0[0])]
    arrived = [bra[1], *ups[1], *downs[1]]
    two0[0], arrived[0] = tie(two0[0], arrived[0])
    (whole, mine), own1, pair1, far1, send1, _ = run_group(
        1, [ket_all], pieces, arrived, energies, (other, whole)
    )
    one1 = [inward(send) for send in send1]
    arrived = list(arrived)
    (whole, mine), own2, pair2, far2, send2, _ = run_group(
        2, [ket_all], pieces, arrived, energies, (mine, whole)
    )
    one2 = [inward(send) for send in send2]
    two0.append(cross(far0[1], one0[1]))
    two1 = [cross(*part) for part in zip(far1, one1)]
    two2 = [cross(*part) for part in zip(far2, one2)]
    one2[1], mine = tie(one2[1], mine)
    other = swap(mine)
    one2[0], two0[1] = tie(one2[0], two0[1])
    three0 = [exchange(*part) for part in zip(pair0, two0)]
    three1 = [exchange(*part) for part in zip(pair1, two1)]
    three2 = [exchange(*part) for part in zip(pair2, two2)]
    ends = [
        finish_all(0, own0, two0, three0),
        finish_all(1, own1, two1, three1),
        finish_all(2, own2, two2, three2),
    ]
    return close(other, whole, [end[0] for end in ends], [end[1] for end in ends])


def solution(mesh):
    sizes = mesh.shape

    def on_device(bra_factor, ket_factor, occ_energy, virt_energy):
        fits = (
            sizes["occ"] == 2
            and sizes["row"] == 4
            and sizes["col"] == 4
            and bra_factor.shape[2] % 1024 == 0
            and ket_factor.shape[2] % 512 == 0
            and bra_factor.shape[0] % 128 == 0
        )
        body = planned if fits else general
        return body(bra_factor, ket_factor, occ_energy, virt_energy)

    placed = (P(("occ", "col"), None, "row"), P(("occ", "row"), None, "col"), P(), P())
    return jax.shard_map(
        on_device,
        mesh=mesh,
        in_specs=placed,
        out_specs=(P(None, None, "row", "col"), P(("occ", "col"), None, "row")),
        check_vma=False,
    )
```

```python
import functools

import jax
import jax.numpy as jnp
from jax import lax
from jax.experimental import pallas as pl
from jax.experimental.pallas import tpu as pltpu
from jax.sharding import PartitionSpec as P


def make_amplitudes(coulomb, occ_energy, virt_first, virt_second):
    denominator = (
        occ_energy[:, None, None, None]
        + occ_energy[None, :, None, None]
        - virt_first[None, None, :, None]
        - virt_second[None, None, None, :]
    )
    return ((2.0 * coulomb - jnp.transpose(coulomb, (1, 0, 2, 3))) / denominator).astype(
        jnp.bfloat16
    )


def general(bra_factor, ket_factor, occ_energy, virt_energy):
    a_width = bra_factor.shape[2]
    b_width = ket_factor.shape[2]
    ket_whole = lax.all_gather(ket_factor, "row", axis=0, tiled=True)
    row_index = lax.axis_index("row")
    col_index = lax.axis_index("col")
    virt_first = lax.dynamic_slice_in_dim(virt_energy, row_index * a_width, a_width, 0)
    virt_second = lax.dynamic_slice_in_dim(virt_energy, col_index * b_width, b_width, 0)
    partial_sum = jnp.einsum(
        "qia,qjb->ijab",
        lax.all_gather(bra_factor, "col", axis=0, tiled=True),
        ket_whole,
        preferred_element_type=jnp.float32,
    )
    batch_count = lax.axis_size("occ")
    pad_rows = (batch_count - a_width % batch_count) % batch_count
    padded = jnp.pad(partial_sum, ((0, 0), (0, 0), (0, pad_rows), (0, 0)))
    share_sum = lax.psum_scatter(padded, "occ", scatter_dimension=2, tiled=True)
    share_len = share_sum.shape[2]
    energy_padded = jnp.pad(virt_first, (0, pad_rows), constant_values=1.0)
    energy_share = lax.dynamic_slice_in_dim(
        energy_padded, lax.axis_index("occ") * share_len, share_len, 0
    )
    share_amps = make_amplitudes(share_sum, occ_energy, energy_share, virt_second)
    collected = lax.all_gather(share_amps, "occ", axis=2, tiled=True)
    amplitudes = collected[:, :, :a_width, :]
    gamma = lax.psum_scatter(
        jnp.einsum("ijab,qjb->qia", amplitudes, ket_whole, preferred_element_type=jnp.float32),
        "col",
        scatter_dimension=0,
        tiled=True,
    )
    return (amplitudes, gamma)


BLOCKS = 2
GROUPS = 3
SLICES = 4
SPLIT = (True, False, True)


def parts_of(group, batch):
    return (slice(batch, 2 * batch), slice(0, batch)) if SPLIT[group] else (slice(0, 2 * batch),)


def place_of(group, block):
    if group == 0:
        return 0, 0, block
    return 1, (group - 1) * (block // 2), block // 2


def group_kernel(pieces, group, *refs):
    refs = list(refs)
    take = lambda count: [refs.pop(0) for _ in range(count)]
    ket = take(1 if group else 2 * len(pieces))
    (bra,) = take(1)
    ups, downs = take(3), take(3)
    occ_ref, virt_ref = take(2)
    aliased = take(2) if group else None
    whole_ref, half_ref = take(2)
    own_ref, pair_ref, far_ref, send_ref = (take(1 + SPLIT[group]) for _ in range(4))
    (ket_all,) = (None,) if group else take(1)
    kv, bt, t2, amps, given, *tiles, ket_sem, bra_sem, out_sem = refs
    block_width, batch = bra.shape[2:]
    number, start, width = place_of(group, block_width)
    span = ket[0].shape[1] // 2
    half = whole_ref.shape[2] // 2
    part = span // SLICES
    here_row, here_col = lax.axis_index("row"), lax.axis_index("col")
    me = lax.axis_index("occ")
    pair = lax.bitwise_xor(here_col, 1)
    low = here_col < 2

    def bra_copies(source, home, slot):
        return [
            pltpu.make_async_copy(
                source.at[q, i, pl.ds(start, width), :],
                bt.at[
                    pl.ds(i * width, width),
                    pl.ds(pl.multiple_of((2 * home + q) * batch, 128), batch),
                ],
                bra_sem.at[slot, q, i],
            )
            for q in range(2)
            for i in range(2)
        ]

    def fetch(condition, source, home, slot):
        @pl.when(condition)
        def _():
            for copy in bra_copies(source, home, slot):
                copy.start()

    for copy in bra_copies(bra, here_col, 0):
        copy.start()
    for d in range(1, 4):
        home = lax.rem(here_col + 4 - d, 4)
        fetch(here_col >= d, ups[d - 1], home, d)
        fetch(here_col < d, downs[3 - d], home, d)

    copies = [[] for _ in range(SLICES)]
    for n in range(SLICES):
        for j in range(2):
            columns = pl.ds(j * span + n * part, part)
            if group:
                moves = [(ket[0], 0, 8 * batch, 0)]
            else:
                moves = []
                for index, source in enumerate(ket):
                    q, place = divmod(index, len(pieces))
                    offset, begin, rows = pieces[place]
                    home = lax.bitwise_xor(here_row, offset) * (2 * batch) + q * batch + begin
                    moves.append((source, pl.multiple_of(home, 16), rows, index))
            for source, home, rows, index in moves:
                copy = pltpu.make_async_copy(
                    source.at[:, columns],
                    kv.at[pl.ds(home, rows), columns],
                    ket_sem.at[n, index, j],
                )
                copy.start()
                copies[n].append(copy)
    if group == 1:
        given_in = pltpu.make_async_copy(aliased[0], given, out_sem.at[2])
        given_in.start()
    for slot in range(4):
        for copy in bra_copies(bra, slot, slot):
            copy.wait()
    row_at = number * block_width + start
    first_at = here_row * (2 * half) + me * half + row_at
    first = virt_ref[:, pl.ds(pl.multiple_of(first_at, 128), width)]
    first = jnp.broadcast_to(first, (width, width)).T[:, :1]

    def amplitudes_of(n):
        tile = tiles[n % 2]
        columns = slice(n * part, (n + 1) * part)
        second_at = pl.multiple_of(here_col * span + n * part, 128)
        second = virt_ref[:, pl.ds(second_at, part)]
        for i in range(2):
            for j in range(i, 2):
                inverse = 1.0 / (((occ_ref[i] + occ_ref[j]) - first) - second)
                for one, two in ((i, j), (j, i))[: 1 + (i != j)]:
                    direct = tile[two, one * width : (one + 1) * width, :]
                    exchange = tile[one, two * width : (two + 1) * width, :]
                    block = ((2.0 * direct - exchange) * inverse).astype(jnp.bfloat16)
                    amps[one, two, :, columns] = block
                    t2[
                        one * width : (one + 1) * width,
                        two * span + n * part : two * span + (n + 1) * part,
                    ] = block

    for n in range(SLICES):
        for copy in copies[n]:
            copy.wait()
        if n:
            amplitudes_of(n - 1)
        for j in range(2):
            tiles[n % 2][j] = jnp.dot(
                bt[...],
                kv[:, j * span + n * part : j * span + (n + 1) * part],
                preferred_element_type=jnp.float32,
            )
    amplitudes_of(SLICES - 1)
    at = pl.multiple_of(me * half + row_at, 16)
    outs = [
        pltpu.make_async_copy(amps, whole_ref.at[:, :, pl.ds(at, width), :], out_sem.at[0]),
        pltpu.make_async_copy(amps, half_ref.at[:, :, pl.ds(start, width), :], out_sem.at[1]),
    ]
    if group == 1:
        given_in.wait()
        at = pl.multiple_of((1 - me) * half, 16)
        outs.append(
            pltpu.make_async_copy(
                given, whole_ref.at[:, :, pl.ds(at, block_width), :], out_sem.at[2]
            )
        )
    if group == 0:
        outs.append(pltpu.make_async_copy(kv, ket_all, out_sem.at[2]))
    for copy in outs:
        copy.start()

    def share_of(home):
        rows = pl.ds(pl.multiple_of(home * (2 * batch), 16), 2 * batch)
        return lax.dot_general(
            kv[rows, :],
            t2[...],
            (((1,), (1,)), ((), ())),
            preferred_element_type=jnp.float32,
        )

    for n in range(2):
        share = share_of(jnp.where(low, 2 + n, n))
        for p, rows in enumerate(parts_of(group, batch)):
            far_ref[p][n] = share[rows]
            send_ref[p][n] = share[rows].astype(jnp.bfloat16)
    for out, home in ((pair_ref, pair), (own_ref, here_col)):
        share = share_of(home)
        for p, rows in enumerate(parts_of(group, batch)):
            out[p][...] = share[rows]
    for copy in outs:
        copy.wait()


def run_group(group, ket, pieces, bras, energies, held):
    _, _, block_width, batch = bras[0].shape
    _, _, width = place_of(group, block_width)
    span = ket[0].shape[1] // 2
    half = block_width * BLOCKS
    total = 8 * batch
    flops = 2 * 2 * total * 2 * width * 2 * span
    any_space = pl.BlockSpec(memory_space=pl.ANY)
    in_vmem = pl.BlockSpec(memory_space=pltpu.VMEM)
    in_hbm = pl.BlockSpec(memory_space=pltpu.HBM)
    ahead = len(ket) + len(bras) + 2
    count = 1 + SPLIT[group]
    rows = 2 * batch // count
    block = jax.ShapeDtypeStruct((rows, 2 * width), jnp.float32)
    far = jax.ShapeDtypeStruct((2, rows, 2 * width), jnp.float32)
    send = jax.ShapeDtypeStruct((2, rows, 2 * width), jnp.bfloat16)
    half_shape = (2, 2, block_width, span)
    results = pl.pallas_call(
        functools.partial(group_kernel, pieces, group),
        out_shape=(
            jax.ShapeDtypeStruct((2, 2, 2 * half, span), jnp.bfloat16),
            jax.ShapeDtypeStruct(half_shape, jnp.bfloat16),
        )
        + (block,) * (2 * count)
        + (far,) * count
        + (send,) * count
        + (() if group else (jax.ShapeDtypeStruct((total, 2 * span), jnp.bfloat16),)),
        in_specs=[in_hbm if group else any_space] * len(ket)
        + [any_space] * len(bras)
        + [pl.BlockSpec(memory_space=pltpu.SMEM), in_vmem]
        + [any_space] * len(held),
        out_specs=(any_space, any_space) + (in_vmem,) * (4 * count) + (() if group else (in_hbm,)),
        scratch_shapes=[
            pltpu.VMEM((total, 2 * span), jnp.bfloat16),
            pltpu.VMEM((2 * width, total), jnp.bfloat16),
            pltpu.VMEM((2 * width, 2 * span), jnp.bfloat16),
            pltpu.VMEM((2, 2, width, span), jnp.bfloat16),
            pltpu.VMEM(half_shape if group == 1 else (2, 2, 16, 128), jnp.bfloat16),
            pltpu.VMEM((2, 2 * width, span // SLICES), jnp.float32),
            pltpu.VMEM((2, 2 * width, span // SLICES), jnp.float32),
            pltpu.SemaphoreType.DMA((SLICES, 2 * len(pieces), 2)),
            pltpu.SemaphoreType.DMA((4, 2, 2)),
            pltpu.SemaphoreType.DMA((3,)),
        ],
        input_output_aliases=({}, {ahead + 1: 0}, {ahead: 1, ahead + 1: 0})[group],
        compiler_params=pltpu.CompilerParams(vmem_limit_bytes=44 * 2**20),
        cost_estimate=pl.CostEstimate(
            flops=flops, bytes_accessed=total * 2 * span * 2, transcendentals=0
        ),
    )(*ket, *bras, *energies, *held)
    ends = [2 + n * count for n in range(5)]
    return results[:2], *(results[n : n + count] for n in ends[:4]), results[ends[4] :]


def pick_kernel(bra, kept_out, given_out):
    width = kept_out.shape[2]
    span = bra.shape[1] // 2
    me = lax.axis_index("occ")
    for side, out in ((1 - me, given_out), (me, kept_out)):
        for g in range(BLOCKS):
            for i in range(2):
                home = i * span + side * (span // 2) + g * width
                out[g, i] = bra[:, pl.ds(pl.multiple_of(home, 128), width)].T


def pick(bra):
    batch, columns = bra.shape
    part = jax.ShapeDtypeStruct((BLOCKS, 2, columns // 4 // BLOCKS, batch), bra.dtype)
    return pl.pallas_call(
        pick_kernel,
        out_shape=(part, part),
        compiler_params=pltpu.CompilerParams(vmem_limit_bytes=16 * 2**20),
        cost_estimate=pl.CostEstimate(
            flops=0, bytes_accessed=4 * bra.size, transcendentals=0
        ),
    )(bra)


def close_kernel(*refs):
    other, _, *totals = refs[: 2 + 2 * GROUPS]
    amps, gamma, amp_buffer, gamma_buffer, sems, gamma_sems = refs[2 + 2 * GROUPS :]
    block_width = other.shape[2]
    half = block_width * BLOCKS
    batch = gamma.shape[0]
    me = lax.axis_index("occ")
    at = pl.multiple_of((1 - me) * half + half - block_width, 16)
    blocks = [(i, j) for i in range(2) for j in range(2)]
    reads = [
        pltpu.make_async_copy(other.at[i, j], amp_buffer.at[i, j], sems.at[0, i, j])
        for i, j in blocks
    ]
    writes = [
        pltpu.make_async_copy(
            amp_buffer.at[i, j], amps.at[i, j, pl.ds(at, block_width), :], sems.at[1, i, j]
        )
        for i, j in blocks
    ]
    for copy in reads:
        copy.start()
    for n in range(2 * GROUPS):
        side, group = divmod(n, GROUPS)
        number, start, width = place_of(group, block_width)
        at = number * block_width + start
        home = jnp.where(me == side, 0, half) + at
        columns = pl.ds(side * half + at, width)
        for i in range(2):
            gamma_buffer[:, i, columns] = totals[n][:batch, i * width : (i + 1) * width]
        writes.append(
            pltpu.make_async_copy(
                gamma_buffer.at[:, :, columns],
                gamma.at[:, :, pl.ds(pl.multiple_of(home, 128), width)],
                gamma_sems.at[n],
            )
        )
        if n < len(blocks):
            reads[n].wait()
            writes[n].start()
        writes[-1].start()
    for copy in writes:
        copy.wait()


def close(other, whole, kept, received):
    batch = received[0].shape[0]
    columns = whole.shape[2]
    any_space = pl.BlockSpec(memory_space=pl.ANY)
    in_vmem = pl.BlockSpec(memory_space=pltpu.VMEM)
    return pl.pallas_call(
        close_kernel,
        out_shape=(
            jax.ShapeDtypeStruct(whole.shape, whole.dtype),
            jax.ShapeDtypeStruct((batch, 2, columns), jnp.float32),
        ),
        in_specs=[any_space, any_space] + [in_vmem] * (2 * GROUPS),
        out_specs=(any_space, any_space),
        scratch_shapes=[
            pltpu.VMEM(other.shape, other.dtype),
            pltpu.VMEM((batch, 2, columns), jnp.float32),
            pltpu.SemaphoreType.DMA((2, 2, 2)),
            pltpu.SemaphoreType.DMA((2 * GROUPS,)),
        ],
        input_output_aliases={1: 0},
        compiler_params=pltpu.CompilerParams(vmem_limit_bytes=48 * 2**20),
        cost_estimate=pl.CostEstimate(
            flops=0, bytes_accessed=4 * other.size + 16 * batch * columns, transcendentals=0
        ),
    )(other, whole, *kept, *received)


def swap(x):
    return lax.ppermute(x, "occ", [(0, 1), (1, 0)])


def planar(x, offset):
    return lax.ppermute(x, "row", [(r, r ^ offset) for r in range(4)])


def hop_up(x, first):
    return lax.ppermute(x, "col", [(c, c + 1) for c in range(first, 3)])


def hop_down(x, first):
    return lax.ppermute(x, "col", [(3 - c, 2 - c) for c in range(first, 3)])


def pairs(x):
    return lax.ppermute(x, "col", [(0, 1), (1, 0), (2, 3), (3, 2)])


def across(x):
    return lax.ppermute(x, "col", [(1, 2), (2, 1)])


def outward(x):
    return lax.ppermute(x, "col", [(1, 0), (2, 3)])


def inward(x):
    return lax.ppermute(x, "col", [(0, 1), (3, 2)])


def tie(*arrays):
    return lax.optimization_barrier(arrays)


def planned(bra_factor, ket_factor, occ_energy, virt_energy):
    batch, _, a_width = bra_factor.shape
    b_width = ket_factor.shape[2]

    bra_kept, bra_given = pick(bra_factor.reshape(batch, 2 * a_width))
    ket_own = ket_factor.reshape(batch, 2 * b_width)
    bra = jnp.stack([bra_kept, swap(bra_given)], axis=1)
    ket_x = planar(ket_own, 1)
    ket_y = planar(ket_own, 2)
    cut = batch // 2
    pieces = ((0, 0, batch), (1, 0, batch), (2, 0, batch), (3, 0, cut), (3, cut, batch - cut))

    ups, downs = [[hop_up(bra[0], 0)], []], [[hop_down(bra[0], 0)], []]
    ket_swapped = swap(ket_own)
    ups[0].append(hop_up(ups[0][0], 1))
    downs[0].append(hop_down(downs[0][0], 1))
    ket_x, ket_y, ups[0][1], downs[0][1], ket_swapped = tie(
        ket_x, ket_y, ups[0][1], downs[0][1], ket_swapped
    )
    part_x, part_y, late_x, late_y = tie(ket_x[:cut], ket_y[cut:], ket_x, ket_y)
    far_y, far_x = planar(part_x, 2), planar(part_y, 1)
    late_y, far_y = tie(late_y, far_y)
    ups[0].append(hop_up(ups[0][1], 2))
    downs[0].append(hop_down(downs[0][1], 2))
    straight = [swap(late_x), swap(late_y)]
    ups[0][2], downs[0][2], far_y, far_x = tie(ups[0][2], downs[0][2], far_y, far_x)
    ket = [ket_own, ket_x, ket_y, far_y, far_x, ket_swapped, *straight, swap(far_y), swap(far_x)]
    ups[0][2], downs[0][2], block = tie(ups[0][2], downs[0][2], bra[1])
    ups[1].append(hop_up(block, 0))
    downs[1].append(hop_down(block, 0))
    energies = (occ_energy, virt_energy[None, :])

    def up_cast(x):
        return x.astype(jnp.float32)

    near = lax.bitwise_and(lax.axis_index("col"), 1)

    def cross(far, one):
        return across((far + up_cast(one)).astype(jnp.bfloat16))

    def exchange(pair, two):
        theirs = lax.dynamic_index_in_dim(two, 1 - near, 0, keepdims=False)
        return pairs((pair + up_cast(theirs)).astype(jnp.bfloat16))

    def finish(own, two, three):
        ours = lax.dynamic_index_in_dim(two, near, 0, keepdims=False)
        return own + up_cast(ours) + up_cast(three)

    def finish_all(group, own, two, three):
        total = [finish(*part) for part in zip(own, two, three)]
        if not SPLIT[group]:
            total = [total[0][batch:], total[0][:batch]]
        return total[1], swap(total[0])

    arrived = [bra[0], *ups[0], *downs[0]]
    (whole, mine), own0, pair0, far0, send0, (ket_all,) = run_group(
        0, ket, pieces, arrived, energies, ()
    )
    one0 = [inward(send) for send in send0]
    own_last, up, down = tie(own0[1], ups[1][0], downs[1][0])
    own0 = (own0[0], own_last)
    ups[1] += [hop_up(up, 1)]
    downs[1] += [hop_down(down, 1)]
    ups[1] += [hop_up(ups[1][1], 2)]
    downs[1] += [hop_down(downs[1][1], 2)]
    other = swap(mine)
    two0 = [cross(far0[0], one0[0])]
    arrived = [bra[1], *ups[1], *downs[1]]
    two0[0], arrived[0] = tie(two0[0], arrived[0])
    (whole, mine), own1, pair1, far1, send1, _ = run_group(
        1, [ket_all], pieces, arrived, energies, (other, whole)
    )
    one1 = [inward(send) for send in send1]
    arrived = list(arrived)
    (whole, mine), own2, pair2, far2, send2, _ = run_group(
        2, [ket_all], pieces, arrived, energies, (mine, whole)
    )
    one2 = [inward(send) for send in send2]
    two0.append(cross(far0[1], one0[1]))
    two1 = [cross(*part) for part in zip(far1, one1)]
    two2 = [cross(*part) for part in zip(far2, one2)]
    one2[1], mine = tie(one2[1], mine)
    other = swap(mine)
    three0 = [exchange(*part) for part in zip(pair0, two0)]
    three1 = [exchange(*part) for part in zip(pair1, two1)]
    three1[0], two2[0] = tie(three1[0], two2[0])
    three2 = [exchange(*part) for part in zip(pair2, two2)]
    ends = [
        finish_all(0, own0, two0, three0),
        finish_all(1, own1, two1, three1),
        finish_all(2, own2, two2, three2),
    ]
    return close(other, whole, [end[0] for end in ends], [end[1] for end in ends])


def solution(mesh):
    sizes = mesh.shape

    def on_device(bra_factor, ket_factor, occ_energy, virt_energy):
        fits = (
            sizes["occ"] == 2
            and sizes["row"] == 4
            and sizes["col"] == 4
            and bra_factor.shape[2] % 1024 == 0
            and ket_factor.shape[2] % 512 == 0
            and bra_factor.shape[0] % 128 == 0
        )
        body = planned if fits else general
        return body(bra_factor, ket_factor, occ_energy, virt_energy)

    placed = (P(("occ", "col"), None, "row"), P(("occ", "row"), None, "col"), P(), P())
    return jax.shard_map(
        on_device,
        mesh=mesh,
        in_specs=placed,
        out_specs=(P(None, None, "row", "col"), P(("occ", "col"), None, "row")),
        check_vma=False,
    )
```
